32 devices in a mesh: seq: 8 (over y, x, core), dp: 4 (over z).
Axes of the slice: x: 2, y: 2, z: 4, core: 2. Of those that a mesh axis runs over, the one named last changes fastest.
Arguments:
- tokens: bfloat16 [8, 1024, 767], P('dp', 'seq'), may hold values from -6 to 6
- doc_lengths: int32 [8, 4], P('dp'), may hold values from 16 to 976, as said below
- first_gain: bfloat16 [767], replicated, may hold values from 0.25 to 1.75
- inward_weight: bfloat16 [767, 2304], replicated, may hold values from -0.21875 to 0.21875
- inward_bias: bfloat16 [2, 768], replicated, may hold values from -3 to 3
- outward_weight: bfloat16 [768, 767], replicated, may hold values from -0.875 to 0.875
- outward_bias: bfloat16 [767], replicated, may hold values from -2 to 2
- second_gain: bfloat16 [767], replicated, may hold values from 0.25 to 1.75
- up_weight: bfloat16 [767, 3072], replicated, may hold values from -0.21875 to 0.21875
- up_bias: bfloat16 [3072], replicated, may hold values from -3 to 3
- down_weight: bfloat16 [3072, 767], replicated, may hold values from -0.109375 to 0.109375
- down_bias: bfloat16 [767], replicated, may hold values from -2 to 2
- cotangent: bfloat16 [8, 1024, 767], P('dp', 'seq'), may hold values from -6 to 6
Outputs:
- output_tokens: bfloat16 [8, 1024, 767], P('dp', 'seq')
- grad_tokens: bfloat16 [8, 1024, 767], P('dp', 'seq')
- gain_first: float32 [767], replicated
- grad_inward: float32 [767, 2304], P(None, ('seq', 'dp'))
- bias_inward: float32 [2, 768], replicated
- grad_outward: float32 [768, 767], P(('seq', 'dp'))
- bias_outward: float32 [767], replicated
- gain_second: float32 [767], replicated
- grad_up: float32 [767, 3072], P(None, ('seq', 'dp'))
- bias_up: float32 [3072], replicated
- grad_down: float32 [3072, 767], P(('seq', 'dp'))
- bias_down: float32 [767], replicated
The draws below stay inside these ranges and needn't reach their ends.
Inputs may be any that keep to these rules, and one draw needn't show every extreme that they name: `doc_lengths`: in each row the 4 lengths sum to 1024; one of them exceeds 1024 - 128, and which one is drawn.
All inputs are finite; a program needn't handle non-finite values.
Results may differ from the reference program's by a relative error of at most 0.013.
Values may be sent and summed in bfloat16 or wider, within the bound.
No kernel may reach another device: no remote copies, remote signals or barrier semaphores. Data moves between devices by JAX's collectives and lax.ppermute only.
A program may use at most 192 MiB of HBM per device.

```python
import jax
import jax.numpy as jnp
from jax import lax

HEADS = 12
HEAD_DIM = 64
FF = 3072
TOK_DEV = 128
D = 767
ROW = 1024
ROWS = 8


def draw_doc_lengths(key, part):
    key = jax.random.fold_in(key, 11)
    first_key, second_key, order_key = jax.random.split(key, 3)
    leading = jax.random.randint(first_key, (ROWS, 1), TOK_DEV // 8, TOK_DEV // 2)
    middle = jax.random.randint(second_key, (ROWS, 2), TOK_DEV // 8, TOK_DEV // 4)
    longest = ROW - leading - jnp.sum(middle, axis=1, keepdims=True)
    pieces = jnp.concatenate([longest, leading, middle], axis=1)
    orders = jax.vmap(lambda row_key: jax.random.permutation(row_key, 4))(jax.random.split(order_key, ROWS))
    return jnp.take_along_axis(pieces, orders, axis=1).astype(jnp.int32)


def block_levels(rng, extent, shards, smallest, high):
    def one(axis_at, blocks):
        draws = jax.random.uniform(jax.random.fold_in(jax.random.fold_in(rng, 6), axis_at), (blocks,), jnp.float32, smallest / len(shards), high / len(shards))
        return jnp.repeat(jnp.exp(draws), extent[axis_at] // blocks).reshape((-1,) + (1,) * (len(extent) - axis_at - 1))

    gain = one(*shards[0])
    for cut in shards[1:]:
        gain = gain * one(*cut)
    return gain


def gaussian(stream_key, shape, deviation, bound, cuts=(), kind=jnp.bfloat16):
    result = deviation * jax.random.normal(stream_key, shape, jnp.float32)
    if cuts:
        result = result * block_levels(stream_key, shape, cuts, -0.22, 0.18)
    return jnp.clip(result, -bound, bound).astype(kind)


def setup_inputs(seed: int = 0) -> dict:
    key_list = jax.random.split(jax.random.key(seed), 14)
    return {
        "tokens": gaussian(key_list[0], (ROWS, ROW, D), 1.0, 6.0, ((0, 4), (1, 8))),
        "doc_lengths": draw_doc_lengths(jax.random.fold_in(key_list[13], 71), 0),
        "first_gain": jnp.clip(1.0 + 0.15 * jax.random.normal(key_list[2], (D,), jnp.float32), 0.25, 1.75).astype(jnp.bfloat16),
        "inward_weight": gaussian(key_list[3], (D, 3 * HEADS * HEAD_DIM), D ** -0.5, 0.21875),
        "inward_bias": gaussian(key_list[4], (2, HEADS * HEAD_DIM), 0.5, 3.0),
        "outward_weight": gaussian(key_list[5], (HEADS * HEAD_DIM, D), (HEADS * HEAD_DIM // 16) ** -0.5, 0.875),
        "outward_bias": gaussian(key_list[6], (D,), 0.3, 2.0),
        "second_gain": jnp.clip(1.0 + 0.15 * jax.random.normal(key_list[7], (D,), jnp.float32), 0.25, 1.75).astype(jnp.bfloat16),
        "up_weight": gaussian(key_list[8], (D, FF), D ** -0.5, 0.21875),
        "up_bias": gaussian(key_list[9], (FF,), 0.5, 3.0),
        "down_weight": gaussian(key_list[10], (FF, D), FF ** -0.5, 0.109375),
        "down_bias": gaussian(key_list[11], (D,), 0.3, 2.0),
        "cotangent": gaussian(key_list[12], (ROWS, ROW, D), 1.0, 6.0, ((0, 4), (1, 8))),
    }


EPSILON = 1e-05
FLOOR = -1e+30
HIGHEST = lax.Precision.HIGHEST

@jax.custom_vjp
def low(v):
    return lax.optimization_barrier(v.astype(jnp.bfloat16)).astype(jnp.float32)

@jax.custom_vjp
def low_back(v):
    return v

def low_keep(v):
    return (low(v), None)

def low_pass(kept, grad):
    return (grad,)

def back_keep(v):
    return (v, None)

def back_low(kept, grad):
    return (low(grad),)
low.defvjp(low_keep, low_pass)
low_back.defvjp(back_keep, back_low)

def compressed_norm(values, gain_row):
    squares = lax.optimization_barrier(jnp.sum(values * values, axis=-1, keepdims=True))
    totals = lax.optimization_barrier(jnp.sum(values, axis=-1, keepdims=True))
    full_width = values.shape[-1] + 1
    return values * gain_row * lax.rsqrt((squares + totals * totals) / full_width + EPSILON)

def document_ids(doc_lengths, positions):
    doc_ends = jnp.cumsum(doc_lengths, axis=-1)
    return lax.optimization_barrier(jnp.sum((positions[..., :, None] >= doc_ends[..., None, :]).astype(jnp.int32), axis=-1))

def row_attention(queries, keys_row, values_row, doc_lengths):
    positions = jnp.arange(queries.shape[0], dtype=jnp.int32)
    ids_row = document_ids(doc_lengths, positions)
    allowed = (ids_row[:, None] == ids_row[None, :]) & (positions[None, :] <= positions[:, None])
    scores = jnp.einsum('qhe,khe->qhk', queries, keys_row, precision=HIGHEST) * queries.shape[-1] ** (-0.5)
    scores = low_back(scores)
    masked = jnp.where(allowed[:, None, :], scores, FLOOR)
    weights = low(jax.nn.softmax(masked, axis=-1))
    return jnp.einsum('qhk,khe->qhe', weights, values_row, precision=HIGHEST)

def layer(tokens, first_gain, inward_weight, inward_bias, outward_weight, outward_bias, second_gain, up_weight, up_bias, down_weight, down_bias, doc_lengths):
    head_width = HEADS * HEAD_DIM
    normed = low(compressed_norm(tokens, first_gain))
    projected = jnp.matmul(normed, inward_weight, precision=HIGHEST)
    queries = low(low_back(projected[..., :head_width] + inward_bias[0]))
    keys_all = low(low_back(projected[..., head_width:2 * head_width]))
    values_all = low(low_back(projected[..., 2 * head_width:] + inward_bias[1]))
    shaped = (ROWS, ROW, HEADS, HEAD_DIM)
    rowwise = jax.checkpoint(row_attention)
    attended = lax.map(lambda packed: rowwise(packed[0], packed[1], packed[2], packed[3]), (queries.reshape(shaped), keys_all.reshape(shaped), values_all.reshape(shaped), doc_lengths))
    attended = low(low_back(attended.reshape(ROWS, ROW, head_width)))
    branch = low_back(jnp.matmul(attended, outward_weight, precision=HIGHEST) + outward_bias)
    residual = tokens + branch
    normed_two = low(compressed_norm(residual, second_gain))
    upward = low_back(jnp.matmul(normed_two, up_weight, precision=HIGHEST) + up_bias)
    active = low(jax.nn.gelu(upward))
    return residual + low_back(jnp.matmul(active, down_weight, precision=HIGHEST) + down_bias)

def reference(tokens, doc_lengths, first_gain, inward_weight, inward_bias, outward_weight, outward_bias, second_gain, up_weight, up_bias, down_weight, down_bias, cotangent):
    floats = tuple((member.astype(jnp.float32) for member in (tokens, first_gain, inward_weight, inward_bias, outward_weight, outward_bias, second_gain, up_weight, up_bias, down_weight, down_bias)))

    def forward(*params):
        return layer(*params, doc_lengths)
    output, pullback = jax.vjp(forward, *floats)
    gradients = pullback(cotangent.astype(jnp.float32))
    return (output.astype(jnp.bfloat16), gradients[0].astype(jnp.bfloat16), gradients[1], gradients[2], gradients[3], gradients[4], gradients[5], gradients[6], gradients[7], gradients[8], gradients[9], gradients[10])
```

```python
import functools

import jax
import jax.numpy as jnp
from jax import lax
from jax.experimental import pallas as pl
from jax.experimental.pallas import tpu as pltpu
from jax.sharding import PartitionSpec as P

HEADS = 12
HEAD_DIM = 64
EPSILON = 1e-05
FLOOR = -1e30
QB = 256
F32 = jnp.float32
BF16 = jnp.bfloat16


def inverse_rms(values):
    squares = jnp.sum(values * values, axis=-1, keepdims=True)
    totals = jnp.sum(values, axis=-1, keepdims=True)
    return lax.rsqrt((squares + totals * totals) / (values.shape[-1] + 1) + EPSILON), totals


def norm_back(values, gain, inverse, totals, incoming):
    weighted = incoming * gain
    dots = jnp.sum(weighted * values, axis=-1, keepdims=True)
    factor = inverse * inverse * inverse * dots / (values.shape[-1] + 1)
    grad = inverse * weighted - factor * (values + totals)
    return grad, jnp.sum(incoming * values * inverse, axis=0)


def dot(left, right, left_dim, right_dim):
    return lax.dot_general(
        left, right, (((left_dim,), (right_dim,)), ((), ())), preferred_element_type=F32
    )


def allowed_block(ends, query_start, keys):
    query_pos = query_start + lax.broadcasted_iota(jnp.int32, (QB, 1), 0)
    start = jnp.zeros_like(query_pos)
    for end in ends:
        start = jnp.where(query_pos >= end, end, start)
    key_pos = lax.broadcasted_iota(jnp.int32, (1, keys), 1)
    return (key_pos <= query_pos) & (key_pos >= start)


def attention_forward(heads, length, ends_ref, qkv_ref, attended_ref, log_ref):
    width = heads * HEAD_DIM
    ends = [ends_ref[at] for at in range(3)]
    for block in range(length // QB):
        rows = pl.ds(block * QB, QB)
        keys = (block + 1) * QB
        allowed = allowed_block(ends, block * QB, keys)
        for head in range(heads):
            at = head * HEAD_DIM
            query = qkv_ref[rows, at : at + HEAD_DIM] * BF16(HEAD_DIM**-0.5)
            key = qkv_ref[:keys, width + at : width + at + HEAD_DIM]
            value = qkv_ref[:keys, 2 * width + at : 2 * width + at + HEAD_DIM]
            scores = jnp.where(allowed, dot(query, key, 1, 1), FLOOR)
            top = jnp.max(scores, axis=-1, keepdims=True)
            weights = jnp.exp(scores - top)
            total = jnp.sum(weights, axis=-1, keepdims=True)
            attended = dot(weights.astype(BF16), value, 1, 0) / total
            attended_ref[rows, at : at + HEAD_DIM] = attended
            log_ref[rows, head : head + 1] = top + jnp.log(total)


def attention_backward(
    heads, length, ends_ref, qkv_ref, attended_ref, log_ref, grad_ref, out_ref, key_grad, value_grad
):
    width = heads * HEAD_DIM
    ends = [ends_ref[at] for at in range(3)]
    blocks = length // QB
    for head in range(heads):
        at = head * HEAD_DIM
        for block in reversed(range(blocks)):
            rows = pl.ds(block * QB, QB)
            keys = (block + 1) * QB
            allowed = allowed_block(ends, block * QB, keys)
            query = qkv_ref[rows, at : at + HEAD_DIM] * BF16(HEAD_DIM**-0.5)
            key = qkv_ref[:keys, width + at : width + at + HEAD_DIM]
            value = qkv_ref[:keys, 2 * width + at : 2 * width + at + HEAD_DIM]
            grad = grad_ref[rows, at : at + HEAD_DIM]
            delta = jnp.sum(
                grad.astype(F32) * attended_ref[rows, at : at + HEAD_DIM], axis=-1, keepdims=True
            )
            scores = dot(query, key, 1, 1)
            weights = jnp.where(allowed, jnp.exp(scores - log_ref[rows, head : head + 1]), 0.0)
            grad_weights = dot(grad, value, 1, 1)
            grad_scores = (weights * (grad_weights - delta)).astype(BF16)
            out_ref[rows, at : at + HEAD_DIM] = (
                dot(grad_scores, key, 1, 0) * HEAD_DIM**-0.5
            ).astype(BF16)
            key_part = dot(grad_scores, query, 0, 0)
            value_part = dot(weights.astype(BF16), grad, 0, 0)
            if block == blocks - 1:
                key_grad[...] = key_part
                value_grad[...] = value_part
            else:
                key_grad[:keys, :] += key_part
                value_grad[:keys, :] += value_part
        out_ref[:, width + at : width + at + HEAD_DIM] = key_grad[...].astype(BF16)
        out_ref[:, 2 * width + at : 2 * width + at + HEAD_DIM] = value_grad[...].astype(BF16)


def flip(value, mask, axis="seq"):
    return lax.ppermute(value, axis, [(at, at ^ mask) for at in range(lax.axis_size(axis))])


def pick(value, index, axis):
    return lax.dynamic_index_in_dim(value, index, axis, keepdims=False)


def halving(value, stages):
    kept = value
    for axis, mask, at, bit in stages:
        sent = pick(kept, 1 - bit, at).astype(BF16)
        kept = pick(kept, bit, at).astype(F32) + flip(sent, mask, axis).astype(F32)
    return kept


def bits_of(size):
    return [1 << at for at in range(size.bit_length() - 1)]


def local(
    tokens, doc_lengths, first_gain, inward_weight, inward_bias, outward_weight, outward_bias,
    second_gain, up_weight, up_bias, down_weight, down_bias, cotangent,
):
    rows, local_len, width = tokens.shape
    seq, dp = lax.axis_size("seq"), lax.axis_size("dp")
    me, replica = lax.axis_index("seq"), lax.axis_index("dp")
    core, chip, chips = me % 2, me // 2, seq // 2
    block = rows * local_len
    length = seq * local_len
    head_width = HEADS * HEAD_DIM
    heads = -(-HEADS // chips)
    mine = heads * HEAD_DIM
    slots = chips * mine
    order = jnp.arange(chips, dtype=jnp.int32) ^ chip

    def to_rows(value):
        kept, got = pick(value, core, 0), flip(pick(value, 1 - core, 0), 1)
        first, second = jnp.where(core == 0, kept, got), jnp.where(core == 0, got, kept)
        return jnp.concatenate([first, second], axis=0)

    def from_rows(value):
        halves = value.reshape(2, local_len, width)
        kept, got = pick(halves, core, 0), flip(pick(halves, 1 - core, 0), 1)
        return jnp.where(core == 0, jnp.stack([kept, got]), jnp.stack([got, kept]))

    def gather_chips(value):
        if chips == 4:
            half = value.shape[0] // 2
            one, two = flip(value, 2), flip(value, 4)
            three = jnp.concatenate([flip(two[:half], 2), flip(one[half:], 4)], axis=0)
            return jnp.stack([value, one, two, three])
        held = value[None]
        for bit in bits_of(chips):
            held = jnp.concatenate([held, flip(held, 2 * bit)], axis=0)
        return held

    def exchange(pieces):
        return [pieces[0]] + [flip(pieces[at], 2 * at) for at in range(1, chips)]

    mine_rows = to_rows(tokens)
    row_tokens = jnp.take(gather_chips(mine_rows), order, axis=0).reshape(length, width)
    cot_rows = to_rows(cotangent)
    token_values = mine_rows.astype(F32)
    cot_values = cot_rows.astype(F32)
    gain_one, gain_two = first_gain.astype(F32), second_gain.astype(F32)

    inward_t = inward_weight.T.reshape(3, head_width, width)
    outward_p = outward_weight
    bias_q, bias_v = inward_bias[0], inward_bias[1]
    if slots != head_width:
        inward_t = jnp.pad(inward_t, ((0, 0), (0, slots - head_width), (0, 0)))
        outward_p = jnp.pad(outward_p, ((0, slots - head_width), (0, 0)))
        bias_q = jnp.pad(bias_q, (0, slots - head_width))
        bias_v = jnp.pad(bias_v, (0, slots - head_width))
    inward_x = jnp.take(inward_t.reshape(3, chips, mine, width), order, axis=1)
    inward_x = inward_x.transpose(1, 0, 2, 3).reshape(chips, 3 * mine, width)
    outward_x = jnp.take(outward_p.reshape(chips, mine, width), order, axis=0).reshape(slots, width)
    bias_mine = jnp.concatenate(
        [pick(bias_q.reshape(chips, mine), chip, 0), jnp.zeros((mine,), BF16), pick(bias_v.reshape(chips, mine), chip, 0)]
    )

    row_values = row_tokens.astype(F32)
    row_inverse, unused = inverse_rms(row_values)
    row_normed = (row_values * gain_one * row_inverse).astype(BF16)
    qkv = (dot(row_normed, inward_x[0], 1, 1) + bias_mine.astype(F32)).astype(BF16)
    ends = jnp.cumsum(pick(doc_lengths, core, 0))[:3]
    whole = pl.BlockSpec(memory_space=pltpu.VMEM)
    scalars = pl.BlockSpec(memory_space=pltpu.SMEM)
    params = pltpu.CompilerParams(vmem_limit_bytes=48 * 1024 * 1024)
    attended, log_total = pl.pallas_call(
        functools.partial(attention_forward, heads, length),
        out_shape=(
            jax.ShapeDtypeStruct((length, mine), F32),
            jax.ShapeDtypeStruct((length, 8), F32),
        ),
        in_specs=[scalars, whole],
        out_specs=(whole, whole),
        compiler_params=params,
        cost_estimate=pl.CostEstimate(flops=8 * length * length * mine, bytes_accessed=8 * length * mine, transcendentals=0),
        name="attention_forward",
    )(ends, qkv)
    attended_blocks = jnp.take(attended.astype(BF16).reshape(chips, block, mine), order, axis=0)
    attended_low = jnp.concatenate(exchange(attended_blocks), axis=-1)

    residual = token_values + (dot(attended_low, outward_x, 1, 0) + outward_bias.astype(F32))
    inverse_two, totals_two = inverse_rms(residual)
    normed_two = (residual * gain_two * inverse_two).astype(BF16)
    upward = dot(normed_two, up_weight, 1, 0) + up_bias.astype(F32)
    grad_active = dot(cot_rows, down_weight, 1, 1)
    active, gelu_back = jax.vjp(jax.nn.gelu, upward)
    active_low = active.astype(BF16)
    grad_upward = gelu_back(grad_active)[0].astype(BF16)
    grad_normed_two = dot(grad_upward, up_weight, 1, 1)
    grad_inner, gain_second = norm_back(residual, gain_two, inverse_two, totals_two, grad_normed_two)
    grad_residual = cot_values + grad_inner
    grad_low = grad_residual.astype(BF16)
    grad_attended = dot(grad_low, outward_x, 1, 1).astype(BF16).reshape(block, chips, mine)
    output_rows = residual + (dot(active_low, down_weight, 1, 0) + down_bias.astype(F32))
    output_tokens = from_rows(output_rows.astype(BF16))

    grad_row = exchange([grad_attended[:, at] for at in range(chips)])
    grad_row = jnp.take(jnp.stack(grad_row), order, axis=0).reshape(length, mine)
    grad_qkv = pl.pallas_call(
        functools.partial(attention_backward, heads, length),
        out_shape=jax.ShapeDtypeStruct((length, 3 * mine), BF16),
        in_specs=[scalars, whole, whole, whole, whole],
        out_specs=whole,
        scratch_shapes=[pltpu.VMEM((length, HEAD_DIM), F32)] * 2,
        compiler_params=params,
        cost_estimate=pl.CostEstimate(flops=20 * length * length * mine, bytes_accessed=16 * length * mine, transcendentals=0),
        name="attention_backward",
    )(ends, qkv, attended, log_total, grad_row)
    grad_blocks = jnp.take(grad_qkv.reshape(chips, block, 3 * mine), order, axis=0)
    grad_projected = jnp.concatenate(exchange(grad_blocks), axis=-1)
    grad_normed_one = dot(grad_projected, inward_x.reshape(chips * 3 * mine, width), 1, 0)
    inverse_one, totals_one = inverse_rms(token_values)
    normed_one = (token_values * gain_one * inverse_one).astype(BF16)
    grad_first, gain_first = norm_back(token_values, gain_one, inverse_one, totals_one, grad_normed_one)
    grad_tokens = from_rows((grad_residual + grad_first).astype(BF16))

    def chip_pair(value):
        return jnp.concatenate([value, flip(value, 1)], axis=0)

    def halves(value):
        parts = value.reshape(block, chips, 2, -1)
        return jnp.concatenate(
            [pick(parts, core, 2).reshape(block, -1), flip(pick(parts, 1 - core, 2).reshape(block, -1), 1)], axis=0
        )

    chip_bits, dp_bits = bits_of(chips), bits_of(dp)
    plane_shape = (2,) * len(chip_bits)
    dp_shape = (2,) * len(dp_bits)

    def stages(bits_in_order, with_core):
        axes = [("seq", 2 * bit) for bit in reversed(chip_bits)]
        if with_core:
            axes.append(("seq", 1))
        axes += [("dp", bit) for bit in reversed(dp_bits)]
        out = []
        for axis, mask in bits_in_order:
            at = axes.index((axis, mask))
            axes.pop(at)
            index = me if axis == "seq" else replica
            out.append((axis, mask, at, (index & mask) // mask))
        return out

    xs = [("seq", 2 * bit) for bit in chip_bits]
    zs = [("dp", bit) for bit in dp_bits]
    ff = up_weight.shape[1]
    ff_share = ff // (seq * dp)
    plane = plane_shape + dp_shape
    grad_down = dot(halves(active_low), chip_pair(cot_rows), 0, 0).reshape(plane + (ff_share, width))
    grad_up = dot(halves(grad_upward), chip_pair(normed_two), 0, 0).reshape(plane + (ff_share, width))
    down_share = halving(grad_down, stages(xs + zs, False))
    up_share = halving(grad_up, stages(xs[::-1] + zs, False))

    grad_in = dot(grad_projected, normed_one, 0, 0).reshape(chips, 3, mine, width)
    grad_in = jnp.take(grad_in, order, axis=0).transpose(1, 0, 2, 3).reshape(3, slots, width)
    grad_in = grad_in[:, :head_width].reshape(plane_shape + (2,) + dp_shape + (-1, width))
    grad_out = dot(attended_low, grad_low, 0, 0).reshape(chips, mine, width)
    grad_out = jnp.take(grad_out, order, axis=0).reshape(slots, width)[:head_width]
    grad_out = grad_out.reshape(plane_shape + (2,) + dp_shape + (-1, width))
    both = jnp.concatenate([grad_in, grad_out], axis=-2)
    in_share = grad_in.shape[-2]
    cut = both.shape[-2] // 2
    first = halving(both[..., :cut, :], stages([("seq", 1)] + xs + zs, True))
    second = halving(both[..., cut:, :], stages([("seq", 1)] + xs[::-1] + zs, True))
    shares = jnp.concatenate([first, second], axis=0)

    grad_p = grad_projected.reshape(block, chips, 3, mine).astype(F32).sum(axis=0)
    grad_p = jnp.take(grad_p, order, axis=0).transpose(1, 0, 2).reshape(3, slots)[:, :head_width]
    small = [
        gain_first, grad_p[0], grad_p[2], jnp.sum(grad_low.astype(F32), axis=0), gain_second,
        jnp.sum(grad_upward.astype(F32), axis=0), jnp.sum(cot_values, axis=0),
    ]
    sizes = [member.shape[0] for member in small]
    vector = jnp.concatenate(small)
    vector = jnp.pad(vector, (0, -vector.shape[0] % 1024)).reshape(-1, 128)
    for axis, mask in [("seq", 1)] + xs + zs:
        vector = vector + flip(vector, mask, axis)
    vector = vector.reshape(-1)
    sums, at = [], 0
    for size in sizes:
        sums.append(vector[at : at + size])
        at += size

    return (
        output_tokens,
        grad_tokens,
        sums[0],
        shares[:in_share].T,
        jnp.stack([sums[1], sums[2]]),
        shares[in_share:],
        sums[3],
        sums[4],
        up_share.T,
        sums[5],
        down_share,
        sums[6],
    )


def solution(mesh):
    return jax.shard_map(
        local,
        mesh=mesh,
        in_specs=(P("dp", "seq", None), P("dp", None)) + (P(),) * 10 + (P("dp", "seq", None),),
        out_specs=(
            P("dp", "seq", None),
            P("dp", "seq", None),
            P(),
            P(None, ("seq", "dp")),
            P(),
            P(("seq", "dp"), None),
            P(),
            P(),
            P(None, ("seq", "dp")),
            P(),
            P(("seq", "dp"), None),
            P(),
        ),
        check_vma=False,
    )
```

```python
import functools

import jax
import jax.numpy as jnp
from jax import lax
from jax.experimental import pallas as pl
from jax.experimental.pallas import tpu as pltpu
from jax.sharding import PartitionSpec as P

HEADS = 12
HEAD_DIM = 64
EPSILON = 1e-05
FLOOR = -1e30
SCALE = HEAD_DIM**-0.5
QB = 256
F32 = jnp.float32
BF16 = jnp.bfloat16
VMEM = pl.BlockSpec(memory_space=pltpu.VMEM)
SMEM = pl.BlockSpec(memory_space=pltpu.SMEM)
hold = lax.optimization_barrier

def inverse_rms(values):
    squares = jnp.sum(values * values, axis=-1, keepdims=True)
    totals = jnp.sum(values, axis=-1, keepdims=True)
    return lax.rsqrt((squares + totals * totals) / (values.shape[-1] + 1) + EPSILON), totals


def norm_back(values, gain, inverse, totals, incoming):
    weighted = incoming * gain
    dots = jnp.sum(weighted * values, axis=-1, keepdims=True)
    factor = inverse * inverse * inverse * dots / (values.shape[-1] + 1)
    grad = inverse * weighted - factor * (values + totals)
    return grad, jnp.sum(incoming * values * inverse, axis=0, keepdims=True)


def dot(left, right, left_dim, right_dim):
    return lax.dot_general(
        left, right, (((left_dim,), (right_dim,)), ((), ())), preferred_element_type=F32
    )


def gelu_both(value):
    root = 0.7978845608028654
    square = value * value
    curve = jnp.tanh(root * value * (1.0 + 0.044715 * square))
    half = 0.5 * (1.0 + curve)
    slope = half + 0.5 * value * (1.0 - curve * curve) * (root * (1.0 + 3 * 0.044715 * square))
    return value * half, slope


def at_block(index, block):
    return pl.ds(pl.multiple_of(index * block, block), block)


def position():
    me = lax.axis_index("seq")
    return me >> 1, me & 1


def either(flag, first, second, left, right):
    @pl.when(flag == 0)
    def straight():
        first[...] = left
        second[...] = right

    @pl.when(flag != 0)
    def crossed():
        first[...] = right
        second[...] = left


def for_each_chip(chip, chips, body):
    for candidate in range(chips):
        pl.when(chip == candidate)(functools.partial(body, candidate))


def allowed_block(ends, query_start, keys):
    query_pos = query_start + lax.broadcasted_iota(jnp.int32, (QB, 1), 0)
    start = jnp.zeros_like(query_pos)
    for end in ends:
        start = jnp.where(query_pos >= end, end, start)
    key_pos = lax.broadcasted_iota(jnp.int32, (1, keys), 1)
    return (key_pos <= query_pos) & (key_pos >= start)


def split_rows(value, kept, sent):
    unused, core = position()
    length = value.shape[2]
    turned = value[...].reshape(value.shape[0], 2 * length).T
    either(core, kept, sent, turned[:length], turned[length:])


def join_rows(kept, got, out):
    unused, core = position()

    def store(first, second):
        both = jnp.concatenate([first[...], second[...]], axis=0).T
        out[...] = both.reshape(out.shape)

    pl.when(core == 0)(lambda: store(kept, got))
    pl.when(core != 0)(lambda: store(got, kept))


def attention_forward(heads, chips, block, places, real, docs, *refs):
    count = len(places)
    pieces, (gain, weight, bias), outs = refs[:count], refs[count : count + 3], refs[count + 3 :]
    qkv, attended, logs, normed_own, own = outs[:5]
    sends, (weight_mine, bias_mine) = outs[5 : 5 + chips], outs[5 + chips :]
    width = heads * HEAD_DIM
    chip, core = position()
    first_end = docs[core, 0]
    second_end = first_end + docs[core, 1]
    ends = [first_end, second_end, second_end + docs[core, 2]]

    def choose(candidate):
        for part in range(3):
            size = max(min(width, real - candidate * width), 0)
            at, start = part * width, part * real + candidate * width
            if size > 0:
                weight_mine[:, at : at + size] = weight[:, start : start + size]
                if part != 1:
                    bias_mine[:, at : at + size] = bias[
                        part // 2 : part // 2 + 1, candidate * width : candidate * width + size
                    ].astype(F32)
            if size < width:
                weight_mine[:, at + size : at + width] = jnp.zeros((weight.shape[0], width - size), BF16)

    bias_mine[...] = jnp.zeros(bias_mine.shape, F32)
    for_each_chip(chip, chips, choose)
    scale = gain[...].astype(F32).reshape(1, -1)
    for (source, mine), piece in zip(places, pieces):
        rows = piece.shape[0]
        values = piece[...].astype(F32)
        inverse, unused = inverse_rms(values)
        normed = (values * scale * inverse).astype(BF16)
        half = core if mine else 1 - core
        if source == 0:
            normed_own[at_block(half, rows), :] = normed
            own[at_block(half, rows), :] = piece[...]
        start = pl.multiple_of((chip ^ source) * block + half * rows, rows)
        qkv[pl.ds(start, rows), :] = (dot(normed, weight_mine[...], 1, 0) + bias_mine[...]).astype(BF16)
    for at_query in range(chips * block // QB):
        rows = pl.ds(at_query * QB, QB)
        keys = (at_query + 1) * QB
        allowed = allowed_block(ends, at_query * QB, keys)
        for head in range(heads):
            at = head * HEAD_DIM
            query = qkv[rows, at : at + HEAD_DIM] * BF16(SCALE)
            key = qkv[:keys, width + at : width + at + HEAD_DIM]
            value = qkv[:keys, 2 * width + at : 2 * width + at + HEAD_DIM]
            scores = jnp.where(allowed, dot(query, key, 1, 1), FLOOR)
            top = jnp.max(scores, axis=-1, keepdims=True)
            weights = jnp.exp(scores - top)
            total = jnp.sum(weights, axis=-1, keepdims=True)
            attended[rows, at : at + HEAD_DIM] = dot(weights.astype(BF16), value, 1, 0) / total
            logs[rows, head : head + 1] = top + jnp.log(total)
    for source in range(chips):
        sends[source][...] = attended[at_block(chip ^ source, block), :].astype(BF16)


def attention_backward(heads, chips, block, docs, qkv, attended, logs, *refs):
    grads, sends = refs[:chips], refs[chips : 2 * chips]
    grad_row, out, key_grad, value_grad = refs[2 * chips :]
    width = heads * HEAD_DIM
    chip, core = position()
    first_end = docs[core, 0]
    second_end = first_end + docs[core, 1]
    ends = [first_end, second_end, second_end + docs[core, 2]]
    for source in range(chips):
        grad_row[at_block(chip ^ source, block), :] = grads[source][...]
    blocks = chips * block // QB
    for head in range(heads):
        at = head * HEAD_DIM
        for at_query in reversed(range(blocks)):
            rows = pl.ds(at_query * QB, QB)
            keys = (at_query + 1) * QB
            allowed = allowed_block(ends, at_query * QB, keys)
            query = qkv[rows, at : at + HEAD_DIM] * BF16(SCALE)
            key = qkv[:keys, width + at : width + at + HEAD_DIM]
            value = qkv[:keys, 2 * width + at : 2 * width + at + HEAD_DIM]
            grad = grad_row[rows, at : at + HEAD_DIM]
            delta = jnp.sum(
                grad.astype(F32) * attended[rows, at : at + HEAD_DIM], axis=-1, keepdims=True
            )
            scores = dot(query, key, 1, 1)
            weights = jnp.where(allowed, jnp.exp(scores - logs[rows, head : head + 1]), 0.0)
            grad_weights = dot(grad, value, 1, 1)
            grad_scores = (weights * (grad_weights - delta)).astype(BF16)
            out[rows, at : at + HEAD_DIM] = (dot(grad_scores, key, 1, 0) * SCALE).astype(BF16)
            key_part = dot(grad_scores, query, 0, 0)
            value_part = dot(weights.astype(BF16), grad, 0, 0)
            if at_query == blocks - 1:
                key_grad[...] = key_part
                value_grad[...] = value_part
            else:
                key_grad[:keys, :] += key_part
                value_grad[:keys, :] += value_part
        out[:, width + at : width + at + HEAD_DIM] = key_grad[...].astype(BF16)
        out[:, 2 * width + at : 2 * width + at + HEAD_DIM] = value_grad[...].astype(BF16)
    for source in range(chips):
        sends[source][...] = out[at_block(chip ^ source, block), :]


def active_cotangent(kept, got, weight, row, out):
    unused, core = position()
    length = kept.shape[0]
    row[at_block(core, length), :] = kept[...]
    row[at_block(1 - core, length), :] = got[...]
    out[...] = dot(row[...], weight[...], 1, 1)


def up_branch(heads, chips, real, *refs):
    pieces = refs[:chips]
    tokens, grad_active, out_weight, out_bias, gain, up_weight, up_bias = refs[chips : chips + 7]
    (residual, normed, att_low, att_kept, att_sent, active, active_kept, active_sent) = refs[
        chips + 7 : chips + 15
    ]
    grad_up, up_kept, up_sent, up_sums = refs[chips + 15 :]
    chip, core = position()
    mine = heads * HEAD_DIM

    def place(candidate):
        for source in range(chips):
            start = (candidate ^ source) * mine
            size = min(mine, real - start)
            if size > 0:
                att_low[:, start : start + size] = pieces[source][:, :size]

    for_each_chip(chip, chips, place)
    values = (
        tokens[...].astype(F32)
        + dot(att_low[...], out_weight[...], 1, 0)
        + out_bias[...].astype(F32).reshape(1, -1)
    )
    residual[...] = values
    inverse, unused = inverse_rms(values)
    normed[...] = (values * gain[...].astype(F32).reshape(1, -1) * inverse).astype(BF16)
    piece = real // (2 * chips)
    for at in range(chips):
        left = att_low[:, 2 * at * piece : (2 * at + 1) * piece]
        right = att_low[:, (2 * at + 1) * piece : (2 * at + 2) * piece]
        place = (slice(None), slice(at * piece, (at + 1) * piece))
        either(core, att_kept.at[place], att_sent.at[place], left, right)
    tile = up_weight.shape[1] // chips
    piece = tile // 2
    for at in range(chips):
        cols = slice(at * tile, (at + 1) * tile)
        place = (slice(None), slice(at * piece, (at + 1) * piece))
        upward = dot(normed[...], up_weight[:, cols], 1, 0) + up_bias[cols].astype(F32).reshape(1, -1)
        act, slope = gelu_both(upward)
        low = act.astype(BF16)
        active[:, cols] = low
        either(core, active_kept.at[place], active_sent.at[place], low[:, :piece], low[:, piece:])
        back = (grad_active[:, cols] * slope).astype(BF16)
        grad_up[:, cols] = back
        either(core, up_kept.at[place], up_sent.at[place], back[:, :piece], back[:, piece:])
        up_sums[:, cols] = jnp.sum(back.astype(F32), axis=0, keepdims=True)


def back_branch(heads, chips, real, residual, cotangent, grad_up, up_weight, out_weight, gain, *refs):
    sends = refs[:chips]
    grad_res, grad_low, sums, wide = refs[chips:]
    chip, unused = position()
    mine = heads * HEAD_DIM
    values = residual[...]
    inverse, totals = inverse_rms(values)
    incoming = dot(grad_up[...], up_weight[...], 1, 1)
    grad, gain_sum = norm_back(values, gain[...].astype(F32).reshape(1, -1), inverse, totals, incoming)
    cot = cotangent[...].astype(F32)
    grad = grad + cot
    grad_res[...] = grad
    low = grad.astype(BF16)
    grad_low[...] = low
    sums[0:1, :] = jnp.sum(low.astype(F32), axis=0, keepdims=True)
    sums[1:2, :] = gain_sum
    sums[2:3, :] = jnp.sum(cot, axis=0, keepdims=True)
    wide[:, :real] = dot(low, out_weight[...], 1, 1).astype(BF16)
    if wide.shape[1] > real:
        wide[:, real:] = jnp.zeros((wide.shape[0], wide.shape[1] - real), BF16)

    def give(candidate):
        for source in range(chips):
            start = (candidate ^ source) * mine
            sends[source][...] = wide[:, start : start + mine]

    for_each_chip(chip, chips, give)


def finish_output(residual, active, weight, bias, kept, sent):
    unused, core = position()
    values = residual[...] + dot(active[...], weight[...], 1, 0) + bias[...].astype(F32).reshape(1, -1)
    low = values.astype(BF16)
    length = kept.shape[0]
    either(core, kept, sent, low[:length], low[length:])


def assemble_projected(heads, chips, real, *refs):
    pieces = refs[:chips]
    projected, kept, sent = refs[chips:]
    chip, core = position()
    mine = heads * HEAD_DIM

    def place(candidate):
        for source in range(chips):
            start = (candidate ^ source) * mine
            size = min(mine, real - start)
            for part in range(3):
                if size > 0:
                    projected[:, part * real + start : part * real + start + size] = pieces[source][
                        :, part * mine : part * mine + size
                    ]

    for_each_chip(chip, chips, place)
    piece = 3 * real // (2 * chips)
    for at in range(chips):
        left = projected[:, 2 * at * piece : (2 * at + 1) * piece]
        right = projected[:, (2 * at + 1) * piece : (2 * at + 2) * piece]
        place = (slice(None), slice(at * piece, (at + 1) * piece))
        either(core, kept.at[place], sent.at[place], left, right)


def finish_tokens(real, projected, tokens, gain, grad_res, weight, sums, up_sums, kept, sent, packed):
    unused, core = position()
    values = tokens[...].astype(F32)
    width = values.shape[1]
    inverse, totals = inverse_rms(values)
    incoming = dot(projected[...], weight[...], 1, 1)
    grad, gain_sum = norm_back(values, gain[...].astype(F32).reshape(1, -1), inverse, totals, incoming)
    low = (grad + grad_res[...]).astype(BF16)
    length = kept.shape[0]
    either(core, kept, sent, low[:length], low[length:])
    packed[...] = jnp.zeros(packed.shape, F32)
    packed[0:1, :width] = gain_sum
    packed[1:2, :real] = jnp.sum(projected[:, :real].astype(F32), axis=0, keepdims=True)
    packed[2:3, :real] = jnp.sum(projected[:, 2 * real :].astype(F32), axis=0, keepdims=True)
    packed[3:6, :width] = sums[0:3, :]
    for at in range(up_sums.shape[1] // real):
        packed[6 + at : 7 + at, :real] = up_sums[:, at * real : (at + 1) * real]


def shared(chips, bit, at):
    chip, unused = position()
    return ((chip >> bit) & 1) == ((at >> bit) & 1), (at >> (bit + 1) << bit) | (at & ((1 << bit) - 1))


def weight_sums(chips, dp, bit, left, left_other, right, right_other, sent, kept):
    rows = left.shape[1] // chips
    share = rows // dp
    for at in range(chips):
        cols = slice(at * rows, (at + 1) * rows)
        total = dot(left[:, cols], right[...], 0, 0) + dot(left_other[:, cols], right_other[...], 0, 0)
        stays, rest = shared(chips, bit, at)

        @pl.when(stays)
        def keep():
            for part in range(dp):
                kept[rest, part] = total[part * share : (part + 1) * share]

        @pl.when(jnp.logical_not(stays))
        def send():
            for part in range(dp):
                sent[rest, part] = total[part * share : (part + 1) * share].astype(BF16)


def attention_sums(chips, dp, bits, *refs):
    in_left, in_other, in_right, in_right_other, out_left, out_other, out_right, out_right_other = refs[:8]
    sents, kepts = refs[8:10], refs[10:12]
    in_rows, out_rows = in_left.shape[1] // chips, out_left.shape[1] // chips
    in_share, out_share = in_rows // dp, out_rows // dp
    cut = (in_share + out_share) // 2
    for at in range(chips):
        cols = slice(at * in_rows, (at + 1) * in_rows)
        ins = dot(in_left[:, cols], in_right[...], 0, 0) + dot(in_other[:, cols], in_right_other[...], 0, 0)
        cols = slice(at * out_rows, (at + 1) * out_rows)
        outs = dot(out_left[:, cols], out_right[...], 0, 0) + dot(
            out_other[:, cols], out_right_other[...], 0, 0
        )

        def store(ref, stream, rest, kind):
            for part in range(dp):
                start = part * in_share
                if stream == 0:
                    ref[rest, part] = ins[start : start + cut].astype(kind)
                else:
                    ref[rest, part, : in_share - cut] = ins[start + cut : start + in_share].astype(kind)
                    ref[rest, part, in_share - cut :] = outs[
                        part * out_share : (part + 1) * out_share
                    ].astype(kind)

        for stream, bit in enumerate(bits):
            stays, rest = shared(chips, bit, at)
            pl.when(stays)(functools.partial(store, kepts[stream], stream, rest, F32))
            pl.when(jnp.logical_not(stays))(functools.partial(store, sents[stream], stream, rest, BF16))


def fold(axis, masks, *refs):
    count = len(masks)
    kepts, gots, sents, outs = (refs[at * count : (at + 1) * count] for at in range(4))
    for mask, kept, got, sent, out in zip(masks, kepts, gots, sents, outs):
        bit = (lax.axis_index(axis) & mask) // mask if mask > 1 else lax.axis_index(axis) & 1
        for at in range(out.shape[0]):
            out[at] = kept[2 * at + bit] + got[2 * at + bit].astype(F32)
            sent[at] = (kept[2 * at + 1 - bit] + got[2 * at + 1 - bit].astype(F32)).astype(BF16)


def last_sums(count, *refs):
    for kept, got, out in zip(refs[:count], refs[count : 2 * count], refs[2 * count :]):
        out[...] = kept[0] + got[0].astype(F32)


def last_attention_sums(in_share, real, *refs):
    kepts, gots, (packed, packed_got), outs = refs[:2], refs[2:4], refs[4:6], refs[6:]
    in_out, out_out, gain_first, bias_in, bias_out, gain_second, bias_up, bias_down = outs
    cut = kepts[0].shape[1]
    in_out[:cut] = kepts[0][0] + gots[0][0].astype(F32)
    second = kepts[1][0] + gots[1][0].astype(F32)
    in_out[cut:] = second[: in_share - cut]
    out_out[...] = second[in_share - cut :]
    sums = packed[...] + packed_got[...]
    width = gain_first.shape[0]
    gain_first[...] = sums[0:1, :width].reshape(width)
    bias_in[...] = sums[1:3, :real]
    bias_out[...] = sums[3:4, :width].reshape(width)
    gain_second[...] = sums[4:5, :width].reshape(width)
    bias_down[...] = sums[5:6, :width].reshape(width)
    for at in range(bias_up.shape[0] // real):
        bias_up[at * real : (at + 1) * real] = sums[6 + at : 7 + at, :real].reshape(real)


def flip(value, mask, axis="seq"):
    return lax.ppermute(value, axis, [(at, at ^ mask) for at in range(lax.axis_size(axis))])


def bits_of(size):
    return [1 << at for at in range(size.bit_length() - 1)]


def local(
    tokens, doc_lengths, first_gain, inward_weight, inward_bias, outward_weight, outward_bias,
    second_gain, up_weight, up_bias, down_weight, down_bias, cotangent,
):
    rows, local_len, width = tokens.shape
    seq, dp = lax.axis_size("seq"), lax.axis_size("dp")
    chips = seq // 2
    block = rows * local_len
    length = seq * local_len
    real = HEADS * HEAD_DIM
    heads = -(-HEADS // chips)
    mine = heads * HEAD_DIM
    slots = chips * mine
    ff = up_weight.shape[1]
    chip_bits, dp_bits = bits_of(chips), bits_of(dp)

    def shape(*dims, kind=BF16):
        return jax.ShapeDtypeStruct(dims, kind)

    def call(kernel, name, outs, args, scratch=(), flops=0, mib=16, scalars=0):
        nbytes = sum(arg.size * arg.dtype.itemsize for arg in args)
        return pl.pallas_call(
            kernel,
            out_shape=outs,
            in_specs=[SMEM] * scalars + [VMEM] * (len(args) - scalars),
            out_specs=jax.tree.map(lambda unused: VMEM, outs),
            scratch_shapes=scratch,
            compiler_params=pltpu.CompilerParams(vmem_limit_bytes=mib * 1024 * 1024),
            cost_estimate=pl.CostEstimate(flops=flops, bytes_accessed=nbytes, transcendentals=0),
            name=name,
        )(*args)

    half_rows = (shape(local_len, width),) * 2

    def to_rows(value, name):
        kept, sent = call(split_rows, name, half_rows, (jnp.transpose(value, (2, 0, 1)),), mib=8)
        return kept, flip(sent, 1)

    def from_rows(kept, sent, name):
        out = call(join_rows, name, shape(width, rows, local_len), (kept, flip(sent, 1)), mib=8)
        return jnp.transpose(out, (1, 2, 0))

    def gather_chips(kept, got):
        if chips == 4:
            kept_one, kept_two = flip(kept, 2), flip(kept, 4)
            got_one, got_two = flip(got, 2), flip(got, 4)
            places = [(0, 1), (0, 0), (1, 1), (2, 1), (1, 0), (2, 0), (3, 1), (3, 0)]
            return places, [kept, got, kept_one, kept_two, got_one, got_two, flip(kept_two, 2), flip(got_one, 4)]
        places, pieces = [], []
        for which, value in ((1, kept), (0, got)):
            held = value[None]
            for bit in chip_bits:
                held = jnp.concatenate([held, flip(held, 2 * bit)], axis=0)
            places += [(at, which) for at in range(chips)]
            pieces += [held[at] for at in range(chips)]
        return places, pieces

    def exchange(pieces):
        return [pieces[0]] + [flip(pieces[at], 2 * at) for at in range(1, chips)]

    kept, got = to_rows(tokens, "split_tokens")
    places, pieces = gather_chips(kept, got)
    cotangent, pieces[0] = hold((cotangent, kept))
    cot_kept, cot_got = to_rows(cotangent, "split_cotangent")
    row_cot, grad_active = call(
        active_cotangent, "active_cotangent", (shape(block, width), shape(block, ff, kind=F32)),
        (cot_kept, cot_got, down_weight), flops=2 * block * width * ff, mib=20,
    )

    forward = call(
        functools.partial(attention_forward, heads, chips, block, places, real), "attention_forward",
        (
            shape(length, 3 * mine), shape(length, mine, kind=F32), shape(length, 8, kind=F32),
            shape(block, width), shape(block, width),
        ) + (shape(block, mine),) * chips,
        (doc_lengths, *pieces, first_gain, inward_weight, inward_bias),
        scratch=[pltpu.VMEM((width, 3 * mine), BF16), pltpu.VMEM((1, 3 * mine), F32)],
        flops=8 * length * length * mine, mib=24, scalars=1,
    )
    qkv, attended, logs, normed_one, row_tokens = forward[:5]
    attended_in = exchange(forward[5:])

    half_ff, half_real = shape(block, ff // 2), shape(block, real // 2)
    (
        residual, normed_two, att_low, att_kept, att_sent, active, active_kept, active_sent,
        grad_up, up_kept, up_sent, up_sums,
    ) = call(
        functools.partial(up_branch, heads, chips, real), "up_branch",
        (
            shape(block, width, kind=F32), shape(block, width), shape(block, real), half_real, half_real,
            shape(block, ff), half_ff, half_ff, shape(block, ff), half_ff, half_ff, shape(1, ff, kind=F32),
        ),
        (*attended_in, row_tokens, grad_active, outward_weight, outward_bias, second_gain, up_weight, up_bias),
        flops=2 * block * width * ff, mib=28,
    )
    one_other, cot_other, two_other = flip(normed_one, 1), flip(row_cot, 1), flip(normed_two, 1)
    active_other, up_other, att_other = flip(active_sent, 1), flip(up_sent, 1), flip(att_sent, 1)
    back = call(
        functools.partial(back_branch, heads, chips, real), "back_branch",
        (shape(block, mine),) * chips
        + (shape(block, width, kind=F32), shape(block, width), shape(8, width, kind=F32)),
        (residual, row_cot, grad_up, up_weight, outward_weight, second_gain),
        scratch=[pltpu.VMEM((block, slots), BF16)], flops=2 * block * width * ff, mib=20,
    )
    grad_res, grad_low, sums = back[chips:]
    low_other = flip(grad_low, 1)
    grad_in = exchange(back[:chips])

    def sums_over(name, left, left_other, right, right_other, bit):
        dims = (chips // 2, dp, left.shape[1] // (chips * dp), width)
        return call(
            functools.partial(weight_sums, chips, dp, bit), name, (shape(*dims), shape(*dims, kind=F32)),
            (left, left_other, right, right_other), flops=4 * block * left.shape[1] * width,
        )

    def scatter(sents, kepts, bits, name):
        gots = [flip(sent, 2 << bit) for sent, bit in zip(sents, bits)]
        left = [[mask for mask in chip_bits if mask != 1 << bit] for bit in bits]

        def step(axis, masks):
            dims = [(kept.shape[0] // 2,) + kept.shape[1:] for kept in kepts]
            outs = call(
                functools.partial(fold, axis, masks), name,
                tuple(shape(*dim) for dim in dims) + tuple(shape(*dim, kind=F32) for dim in dims),
                (*kepts, *gots),
            )
            return outs[: len(kepts)], list(outs[len(kepts) :])

        for at in range(len(chip_bits) - 1):
            masks = [2 * mask[at] for mask in left]
            sents, kepts = step("seq", masks)
            gots = [flip(sent, mask) for sent, mask in zip(sents, masks)]
        kepts, gots = [kept[0] for kept in kepts], [got[0] for got in gots]
        for mask in dp_bits:
            sents, kepts = step("dp", [mask] * len(kepts))
            gots = [flip(sent, mask, "dp") for sent in sents]
        return kepts, gots

    bits = (0, len(chip_bits) - 1)
    down_sent, down_kept = sums_over("grad_down", active_kept, active_other, row_cot, cot_other, bits[0])
    up_sent_sum, up_kept_sum = sums_over("grad_up", up_kept, up_other, normed_two, two_other, bits[1])
    *grad_in, down_sent, up_sent_sum = hold((*grad_in, down_sent, up_sent_sum))
    ff_kepts, ff_gots = scatter((down_sent, up_sent_sum), (down_kept, up_kept_sum), bits, "fold_wide")
    ff_share = ff // (seq * dp)
    down_share, up_share = call(
        functools.partial(last_sums, 2), "last_wide", (shape(ff_share, width, kind=F32),) * 2, (*ff_kepts, *ff_gots)
    )

    grad_qkv = call(
        functools.partial(attention_backward, heads, chips, block), "attention_backward",
        (shape(block, 3 * mine),) * chips, (doc_lengths, qkv, attended, logs, *grad_in),
        scratch=[
            pltpu.VMEM((length, mine), BF16), pltpu.VMEM((length, 3 * mine), BF16),
            pltpu.VMEM((length, HEAD_DIM), F32), pltpu.VMEM((length, HEAD_DIM), F32),
        ],
        flops=20 * length * length * mine, mib=24, scalars=1,
    )
    projected_in = exchange(grad_qkv)
    active, unused = hold((active, grad_qkv[0]))
    out_kept, out_sent = call(
        finish_output, "finish_output", half_rows, (residual, active, down_weight, down_bias),
        flops=2 * block * width * ff, mib=20,
    )
    projected, proj_kept, proj_sent = call(
        functools.partial(assemble_projected, heads, chips, real), "assemble_projected",
        (shape(block, 3 * real), shape(block, 3 * real // 2), shape(block, 3 * real // 2)), tuple(projected_in),
    )
    proj_other = flip(proj_sent, 1)
    packed_shape = shape(-(-(6 + ff // real) // 8) * 8, real, kind=F32)
    rows_kept, rows_sent, packed = call(
        functools.partial(finish_tokens, real), "finish_tokens", half_rows + (packed_shape,),
        (projected, row_tokens, first_gain, grad_res, inward_weight, sums, up_sums),
        flops=6 * block * width * real, mib=20,
    )
    output_tokens = from_rows(out_kept, out_sent, "join_output")
    grad_tokens = from_rows(rows_kept, rows_sent, "join_tokens")

    in_share, out_share = 3 * real // (seq * dp), real // (seq * dp)
    dims = (chips // 2, dp, (in_share + out_share) // 2, width)
    a_sums = call(
        functools.partial(attention_sums, chips, dp, bits), "attention_sums",
        (shape(*dims),) * 2 + (shape(*dims, kind=F32),) * 2,
        (proj_kept, proj_other, normed_one, one_other, att_kept, att_other, grad_low, low_other),
        flops=8 * block * real * width, mib=20,
    )
    a_kepts, a_gots = scatter(a_sums[:2], a_sums[2:], bits, "fold_attention")
    hops = [("seq", 1)] + [("seq", 2 * bit) for bit in chip_bits] + [("dp", bit) for bit in dp_bits]
    for axis, mask in hops[:-1]:
        packed = packed + flip(packed, mask, axis)
    packed_got = flip(packed, hops[-1][1], hops[-1][0])
    flat = [shape(width, kind=F32), shape(2, real, kind=F32), shape(width, kind=F32), shape(width, kind=F32)]
    flat += [shape(ff, kind=F32), shape(width, kind=F32)]
    in_out, out_out, gain_first, bias_in, bias_out, gain_second, bias_up, bias_down = call(
        functools.partial(last_attention_sums, in_share, real), "last_attention",
        (shape(in_share, width, kind=F32), shape(out_share, width, kind=F32), *flat),
        (*a_kepts, *a_gots, packed, packed_got),
    )
    return (
        output_tokens, grad_tokens, gain_first, in_out.T, bias_in, out_out, bias_out, gain_second,
        up_share.T, bias_up, down_share, bias_down,
    )


def solution(mesh):
    return jax.shard_map(
        local,
        mesh=mesh,
        in_specs=(P("dp", "seq", None), P("dp", None)) + (P(),) * 10 + (P("dp", "seq", None),),
        out_specs=(
            P("dp", "seq", None),
            P("dp", "seq", None),
            P(),
            P(None, ("seq", "dp")),
            P(),
            P(("seq", "dp"), None),
            P(),
            P(),
            P(None, ("seq", "dp")),
            P(),
            P(("seq", "dp"), None),
            P(),
        ),
        check_vma=False,
    )
```

```python
import functools
import math

import jax
import jax.numpy as jnp
import numpy as np
from jax import lax
from jax.experimental import pallas as pl
from jax.experimental.pallas import tpu as pltpu
from jax.sharding import PartitionSpec as P

HEADS = 12
HEAD_DIM = 64
EPSILON = 1e-05
FLOOR = -1e30
SCALE = HEAD_DIM**-0.5
QB = 256
F32 = jnp.float32
BF16 = jnp.bfloat16
VMEM = pl.BlockSpec(memory_space=pltpu.VMEM)
SMEM = pl.BlockSpec(memory_space=pltpu.SMEM)
HBM = pl.BlockSpec(memory_space=pltpu.HBM)
hold = lax.optimization_barrier

def inverse_rms(values):
    squares = jnp.sum(values * values, axis=-1, keepdims=True)
    totals = jnp.sum(values, axis=-1, keepdims=True)
    return lax.rsqrt((squares + totals * totals) / (values.shape[-1] + 1) + EPSILON), totals


def norm_back(values, gain, inverse, totals, incoming):
    weighted = incoming * gain
    dots = jnp.sum(weighted * values, axis=-1, keepdims=True)
    factor = inverse * inverse * inverse * dots / (values.shape[-1] + 1)
    grad = inverse * weighted - factor * (values + totals)
    return grad, jnp.sum(incoming * values * inverse, axis=0, keepdims=True)


def dot(left, right, left_dim, right_dim):
    return lax.dot_general(
        left, right, (((left_dim,), (right_dim,)), ((), ())), preferred_element_type=F32
    )


def gelu_both(value):
    root = 0.7978845608028654
    square = value * value
    curve = jnp.tanh(root * value * (1.0 + 0.044715 * square))
    half = 0.5 * (1.0 + curve)
    slope = half + 0.5 * value * (1.0 - curve * curve) * (root * (1.0 + 3 * 0.044715 * square))
    return value * half, slope


def at_block(index, block):
    return pl.ds(pl.multiple_of(index * block, block), block)


def position():
    me = lax.axis_index("seq")
    return me >> 1, me & 1


def either(flag, first, second, left, right):
    @pl.when(flag == 0)
    def straight():
        first[...] = left
        second[...] = right

    @pl.when(flag != 0)
    def crossed():
        first[...] = right
        second[...] = left


def for_each_chip(chip, chips, body):
    for candidate in range(chips):
        pl.when(chip == candidate)(functools.partial(body, candidate))


def allowed_block(starts, query_start, keys):
    query_pos = query_start + lax.broadcasted_iota(jnp.int32, (QB, 1), 0)
    key_pos = lax.broadcasted_iota(jnp.int32, (1, keys), 1)
    return (key_pos <= query_pos) & (key_pos >= starts)


def split_rows(value, kept, sent):
    unused, core = position()
    length = value.shape[2]
    turned = value[...].reshape(value.shape[0], 2 * length).T
    either(core, kept, sent, turned[:length], turned[length:])


def join_rows(kept, got, out):
    unused, core = position()

    def store(first, second):
        both = jnp.concatenate([first[...], second[...]], axis=0).T
        out[...] = both.reshape(out.shape)

    pl.when(core == 0)(lambda: store(kept, got))
    pl.when(core != 0)(lambda: store(got, kept))


def project(piece, scale, weight, bias, normed, inverse, qkv):
    values = piece[...].astype(F32)
    factor, unused = inverse_rms(values)
    low = (values * scale[...] * factor).astype(BF16)
    normed[...] = low
    inverse[...] = factor
    qkv[...] = (dot(low, weight[...], 1, 0) + bias[...]).astype(BF16)


def pick_weights(heads, chips, real, docs, gain, weight, bias, weight_mine, bias_mine, scale, starts, *scratch):
    window, gain_v, bias_v, docs_v, sems = scratch
    width = heads * HEAD_DIM
    chip, core = position()
    wide = window.shape[2]
    gain_copy = pltpu.make_async_copy(gain, gain_v, sems.at[3])
    bias_copy = pltpu.make_async_copy(bias, bias_v, sems.at[4])
    docs_copy = pltpu.make_async_copy(docs, docs_v, sems.at[5])

    def copies(candidate):
        start = min(candidate * width, real - 1)
        low = min(start // 128 * 128, real - wide)
        return low, [
            pltpu.make_async_copy(weight.at[:, pl.ds(part * real + low, wide)], window.at[part], sems.at[part])
            for part in range(3)
        ]

    def begin(candidate):
        for copy in copies(candidate)[1]:
            copy.start()

    for_each_chip(chip, chips, begin)
    gain_copy.start()
    bias_copy.start()
    docs_copy.start()
    gain_copy.wait()
    scale[...] = gain_v[...].astype(F32).reshape(1, -1)
    bias_copy.wait()
    docs_copy.wait()
    places = lax.broadcasted_iota(jnp.int32, starts.shape, 0)
    start, end = jnp.zeros_like(places), jnp.int32(0)
    for at in range(3):
        end = end + docs_v[core, at]
        start = jnp.where(places >= end, end, start)
    starts[...] = start

    def choose(candidate):
        low, waits = copies(candidate)
        size = max(min(width, real - candidate * width), 0)
        for part in range(3):
            waits[part].wait()
            at = part * width
            if size > 0:
                shift = candidate * width - low
                weight_mine[:, at : at + size] = window[part, :, shift : shift + size]
                if part != 1:
                    bias_mine[:, at : at + size] = bias_v[
                        part // 2 : part // 2 + 1, candidate * width : candidate * width + size
                    ].astype(F32)
            if size < width:
                weight_mine[:, at + size : at + width] = jnp.zeros((weight.shape[0], width - size), BF16)

    bias_mine[...] = jnp.zeros(bias_mine.shape, F32)
    for_each_chip(chip, chips, choose)


def project_first(kept, got, weight, bias, scale, normed_own, own, *refs):
    unused, core = position()
    rows = kept.shape[0]
    for at, (piece, half) in enumerate(((kept, core), (got, 1 - core))):
        normed, inverse, qkv = refs[3 * at : 3 + 3 * at]
        project(piece, scale, weight, bias, normed, inverse, qkv)
        normed_own[at_block(half, rows), :] = normed[...]
        own[at_block(half, rows), :] = piece[...]


def project_more(count, *refs):
    pieces, (weight, bias, scale), outs = refs[:count], refs[count : count + 3], refs[count + 3 :]
    for at, piece in enumerate(pieces):
        project(piece, scale, weight, bias, *outs[3 * at : 3 * at + 3])


def attention_forward(heads, chips, block, places, fresh, *refs):
    count = len(places)
    done, pieces = refs[: count - fresh], refs[count - fresh : count]
    (weight, bias, scale, starts), outs = refs[count : count + 4], refs[count + 4 :]
    qkv, attended, logs = outs[:3]
    sends, parts = outs[3 : 3 + chips], outs[3 + chips :]
    width = heads * HEAD_DIM
    chip, core = position()
    for at, (source, mine) in enumerate(places):
        part = done[at] if at < count - fresh else parts[3 * (at - count + fresh) + 2]
        if at >= count - fresh:
            at_parts = 3 * (at - count + fresh)
            project(pieces[at - count + fresh], scale, weight, bias, *parts[at_parts : at_parts + 3])
        rows = part.shape[0]
        half = core if mine else 1 - core
        start = pl.multiple_of((chip ^ source) * block + half * rows, rows)
        qkv[pl.ds(start, rows), :] = part[...]
    for at_query in range(chips * block // QB):
        rows = pl.ds(at_query * QB, QB)
        keys = (at_query + 1) * QB
        allowed = allowed_block(starts[rows, :], at_query * QB, keys)
        for head in range(heads):
            at = head * HEAD_DIM
            query = qkv[rows, at : at + HEAD_DIM] * BF16(SCALE)
            key = qkv[:keys, width + at : width + at + HEAD_DIM]
            value = qkv[:keys, 2 * width + at : 2 * width + at + HEAD_DIM]
            scores = jnp.where(allowed, dot(query, key, 1, 1), FLOOR)
            top = jnp.max(scores, axis=-1, keepdims=True)
            weights = jnp.exp(scores - top)
            total = jnp.sum(weights, axis=-1, keepdims=True)
            attended[rows, at : at + HEAD_DIM] = dot(weights.astype(BF16), value, 1, 0) / total
            logs[rows, head : head + 1] = top + jnp.log(total)
    for source in range(chips):
        sends[source][...] = attended[at_block(chip ^ source, block), :].astype(BF16)


def attention_backward(heads, chips, block, starts, qkv, attended, logs, *refs):
    grads, sends = refs[:chips], refs[chips : 2 * chips]
    out, grad_row, key_grad, value_grad = refs[2 * chips :]
    width = heads * HEAD_DIM
    chip, core = position()
    for source in range(chips):
        grad_row[at_block(chip ^ source, block), :] = grads[source][...]
    blocks = chips * block // QB
    for head in range(heads):
        at = head * HEAD_DIM
        for at_query in reversed(range(blocks)):
            rows = pl.ds(at_query * QB, QB)
            keys = (at_query + 1) * QB
            allowed = allowed_block(starts[rows, :], at_query * QB, keys)
            query = qkv[rows, at : at + HEAD_DIM] * BF16(SCALE)
            key = qkv[:keys, width + at : width + at + HEAD_DIM]
            value = qkv[:keys, 2 * width + at : 2 * width + at + HEAD_DIM]
            grad = grad_row[rows, at : at + HEAD_DIM]
            delta = jnp.sum(
                grad.astype(F32) * attended[rows, at : at + HEAD_DIM], axis=-1, keepdims=True
            )
            scores = dot(query, key, 1, 1)
            weights = jnp.where(allowed, jnp.exp(scores - logs[rows, head : head + 1]), 0.0)
            grad_weights = dot(grad, value, 1, 1)
            grad_scores = (weights * (grad_weights - delta)).astype(BF16)
            out[rows, at : at + HEAD_DIM] = (dot(grad_scores, key, 1, 0) * SCALE).astype(BF16)
            key_part = dot(grad_scores, query, 0, 0)
            value_part = dot(weights.astype(BF16), grad, 0, 0)
            if at_query == blocks - 1:
                key_grad[...] = key_part
                value_grad[...] = value_part
            else:
                key_grad[:keys, :] += key_part
                value_grad[:keys, :] += value_part
        out[:, width + at : width + at + HEAD_DIM] = key_grad[...].astype(BF16)
        out[:, 2 * width + at : 2 * width + at + HEAD_DIM] = value_grad[...].astype(BF16)
    for source in range(chips):
        sends[source][...] = out[at_block(chip ^ source, block), :]


def active_cotangent(kept, got, weight, row, out):
    unused, core = position()
    length = kept.shape[0]
    row[at_block(core, length), :] = kept[...]
    row[at_block(1 - core, length), :] = got[...]
    out[...] = dot(row[...], weight[...], 1, 1)


def up_branch(heads, chips, real, *refs):
    pieces = refs[:chips]
    tokens, grad_active, out_weight, out_bias, gain, up_weight, up_bias = refs[chips : chips + 7]
    (residual, normed, att_low, att_kept, att_sent, active, active_kept, active_sent) = refs[
        chips + 7 : chips + 15
    ]
    grad_up, up_kept, up_sent, up_sums = refs[chips + 15 :]
    chip, core = position()
    mine = heads * HEAD_DIM

    def place(candidate):
        for source in range(chips):
            start = (candidate ^ source) * mine
            size = min(mine, real - start)
            if size > 0:
                att_low[:, start : start + size] = pieces[source][:, :size]

    for_each_chip(chip, chips, place)
    values = (
        tokens[...].astype(F32)
        + dot(att_low[...], out_weight[...], 1, 0)
        + out_bias[...].astype(F32).reshape(1, -1)
    )
    residual[...] = values
    inverse, unused = inverse_rms(values)
    normed[...] = (values * gain[...].astype(F32).reshape(1, -1) * inverse).astype(BF16)
    piece = real // (2 * chips)
    for at in range(chips):
        left = att_low[:, 2 * at * piece : (2 * at + 1) * piece]
        right = att_low[:, (2 * at + 1) * piece : (2 * at + 2) * piece]
        place = (slice(None), slice(at * piece, (at + 1) * piece))
        either(core, att_kept.at[place], att_sent.at[place], left, right)
    tile = up_weight.shape[1] // chips
    piece = tile // 2
    for at in range(chips):
        cols = slice(at * tile, (at + 1) * tile)
        place = (slice(None), slice(at * piece, (at + 1) * piece))
        upward = dot(normed[...], up_weight[:, cols], 1, 0) + up_bias[cols].astype(F32).reshape(1, -1)
        act, slope = gelu_both(upward)
        low = act.astype(BF16)
        active[:, cols] = low
        either(core, active_kept.at[place], active_sent.at[place], low[:, :piece], low[:, piece:])
        back = (grad_active[:, cols] * slope).astype(BF16)
        grad_up[:, cols] = back
        either(core, up_kept.at[place], up_sent.at[place], back[:, :piece], back[:, piece:])
        up_sums[:, cols] = jnp.sum(back.astype(F32), axis=0, keepdims=True)


def back_branch(heads, chips, real, residual, cotangent, grad_up, up_weight, out_weight, gain, *refs):
    sends = refs[:chips]
    grad_res, grad_low, sums, wide = refs[chips:]
    chip, unused = position()
    mine = heads * HEAD_DIM
    values = residual[...]
    inverse, totals = inverse_rms(values)
    incoming = dot(grad_up[...], up_weight[...], 1, 1)
    grad, gain_sum = norm_back(values, gain[...].astype(F32).reshape(1, -1), inverse, totals, incoming)
    cot = cotangent[...].astype(F32)
    grad = grad + cot
    grad_res[...] = grad
    low = grad.astype(BF16)
    grad_low[...] = low
    sums[0:1, :] = jnp.sum(low.astype(F32), axis=0, keepdims=True)
    sums[1:2, :] = gain_sum
    sums[2:3, :] = jnp.sum(cot, axis=0, keepdims=True)
    wide[:, :real] = dot(low, out_weight[...], 1, 1).astype(BF16)
    if wide.shape[1] > real:
        wide[:, real:] = jnp.zeros((wide.shape[0], wide.shape[1] - real), BF16)

    def give(candidate):
        for source in range(chips):
            start = (candidate ^ source) * mine
            sends[source][...] = wide[:, start : start + mine]

    for_each_chip(chip, chips, give)


def finish_output(residual, active, weight, bias, kept, sent):
    unused, core = position()
    values = residual[...] + dot(active[...], weight[...], 1, 0) + bias[...].astype(F32).reshape(1, -1)
    low = values.astype(BF16)
    length = kept.shape[0]
    either(core, kept, sent, low[:length], low[length:])


def row_pieces(chips, block, places, pieces, out):
    chip, core = position()
    for (source, mine), piece in zip(places, pieces):
        rows = piece.shape[0]
        half = core if mine else 1 - core
        out[pl.ds(pl.multiple_of((chip ^ source) * block + half * rows, rows), rows), :] = piece[...]


def row_sums(heads, chips, block, places, real, units, grad_qkv, weight_mine, sums, up_sums, *refs):
    count = len(places)
    tokens, normed, inverse = refs[:count], refs[count : 2 * count], refs[2 * count : 3 * count]
    outs, scratch = refs[3 * count : -4], refs[-4:]
    row_tokens, row_normed, row_inverse, partial = scratch
    packed = outs[0]
    chip, core = position()
    mine = heads * HEAD_DIM
    row_pieces(chips, block, places, tokens, row_tokens)
    row_pieces(chips, block, places, inverse, row_inverse)
    if units is not None:
        row_pieces(chips, block, places, normed, row_normed)
        partial[...] = dot(grad_qkv[...], row_normed[...], 0, 0)
        sent, kept = outs[1:]

        def split(candidate):
            for for_core, for_replica, at, start, size in units[candidate]:

                @pl.when(core == for_core)
                def keep():
                    kept[for_replica, at : at + size] = partial[start : start + size]

                @pl.when(core != for_core)
                def send():
                    sent[for_replica, at : at + size] = partial[start : start + size].astype(BF16)

        for_each_chip(chip, chips, split)
    width = row_tokens.shape[1]
    packed[...] = jnp.zeros(packed.shape, F32)
    gain_sum = jnp.zeros((1, width), F32)
    for at in range(chips):
        rows = pl.ds(at * block, block)
        incoming = dot(grad_qkv[rows, :], weight_mine[...], 1, 1)
        gain_sum += jnp.sum(
            incoming * (row_tokens[rows, :].astype(F32) * row_inverse[rows, :]), axis=0, keepdims=True
        )
    packed[0:1, :width] = gain_sum
    query_sum = jnp.sum(grad_qkv[:, :mine].astype(F32), axis=0, keepdims=True)
    value_sum = jnp.sum(grad_qkv[:, 2 * mine :].astype(F32), axis=0, keepdims=True)

    def place(candidate):
        size = min(mine, real - candidate * mine)
        if size > 0:
            packed[1:2, candidate * mine : candidate * mine + size] = query_sum[:, :size]
            packed[2:3, candidate * mine : candidate * mine + size] = value_sum[:, :size]

    for_each_chip(chip, chips, place)
    packed[3:6, :width] = sums[0:3, :]
    for at in range(up_sums.shape[1] // real):
        packed[6 + at : 7 + at, :real] = up_sums[:, at * real : (at + 1) * real]


def finish_tokens(heads, chips, real, *refs):
    pieces = refs[:chips]
    tokens, gain, grad_res, weight, kept, sent, projected = refs[chips : chips + 7]
    halves = refs[chips + 7 :]
    chip, core = position()
    mine = heads * HEAD_DIM

    def place(candidate):
        for source in range(chips):
            start = (candidate ^ source) * mine
            size = min(mine, real - start)
            for part in range(3):
                if size > 0:
                    projected[:, part * real + start : part * real + start + size] = pieces[source][
                        :, part * mine : part * mine + size
                    ]

    for_each_chip(chip, chips, place)
    values = tokens[...].astype(F32)
    inverse, totals = inverse_rms(values)
    incoming = dot(projected[...], weight[...], 1, 1)
    grad, unused = norm_back(values, gain[...].astype(F32).reshape(1, -1), inverse, totals, incoming)
    low = (grad + grad_res[...]).astype(BF16)
    length = kept.shape[0]
    either(core, kept, sent, low[:length], low[length:])


def shared(chips, bit, at):
    chip, unused = position()
    return ((chip >> bit) & 1) == ((at >> bit) & 1), (at >> (bit + 1) << bit) | (at & ((1 << bit) - 1))


def pair_dot(left, left_other, right, right_other, cols):
    return dot(left[:, cols], right[...], 0, 0) + dot(left_other[:, cols], right_other[...], 0, 0)


def store_chunks(total, chips, dp, bit, at, cuts, sents, kepts):
    share = total.shape[0] // dp
    stays, rest = shared(chips, bit, at)

    @pl.when(stays)
    def keep():
        for part in range(dp):
            for kept, (low, high) in zip(kepts, cuts):
                kept[rest, part] = total[part * share + low : part * share + high]

    @pl.when(jnp.logical_not(stays))
    def send():
        for part in range(dp):
            for sent, (low, high) in zip(sents, cuts):
                sent[rest, part] = total[part * share + low : part * share + high].astype(BF16)


def stream_sums(chips, dp, bit, cuts, left, left_other, right, right_other, *outs):
    rows = left.shape[1] // chips
    count = len(cuts)
    for at in range(chips):
        total = pair_dot(left, left_other, right, right_other, slice(at * rows, (at + 1) * rows))
        store_chunks(total, chips, dp, bit, at, cuts, outs[:count], outs[count:])


def third_sums(chips, dp, left, left_other, right, right_other, sent, kept):
    rows = left.shape[1] // chips
    share = rows // dp
    mine = lax.axis_index("dp") & 1
    for at in range(chips):
        total = pair_dot(left, left_other, right, right_other, slice(at * rows, (at + 1) * rows))
        for part in range(dp):

            @pl.when(mine == part & 1)
            def keep():
                kept[part >> 1, at] = total[part * share : (part + 1) * share]

            @pl.when(mine != part & 1)
            def send():
                sent[part >> 1, at] = total[part * share : (part + 1) * share].astype(BF16)


def fold(steps, *refs):
    count = len(steps)
    kepts, gots, sents, outs = (refs[at * count : (at + 1) * count] for at in range(4))
    for (axis, shift), kept, got, sent, out in zip(steps, kepts, gots, sents, outs):
        bit = (lax.axis_index(axis) >> shift) & 1
        for at in range(out.shape[0]):
            out[at] = kept[2 * at + bit] + got[2 * at + bit].astype(F32)
            sent[at] = (kept[2 * at + 1 - bit] + got[2 * at + 1 - bit].astype(F32)).astype(BF16)


def fold_small(step, kept, got, packed, packed_got, sent, out, packed_out):
    fold((step,), kept, got, sent, out)
    packed_out[...] = packed[...] + packed_got[...]


def last_wide(cuts, *refs):
    pairs, (down, up, outward) = refs[:-3], refs[-3:]
    count = len(cuts)
    for out, first in ((down, 0), (up, count)):
        for (low, high), at in zip(cuts, range(first, first + count)):
            out[low:high] = pairs[2 * at][0] + pairs[2 * at + 1][0].astype(F32)
    outward[...] = pairs[-2][0] + pairs[-1][0].astype(F32)


def last_inward(kept, got, packed, packed_got, share, low, packed_out):
    total = kept[0] + got[0].astype(F32)
    share[...] = total
    low[...] = total.astype(BF16)
    packed_out[...] = packed[...] + packed_got[...]


def place_inward(chips, dp, size, table, share, *refs):
    gots, out, held = refs[:-2], refs[-2], refs[-1]
    count = share.shape[0] // size
    for at, piece in enumerate((share, *gots)):
        for unit in range(count):
            held[at, unit] = piece[unit * size : (unit + 1) * size].astype(F32)
    device = lax.axis_index("seq") * dp + lax.axis_index("dp")
    for unit in range(count):
        place = 2 * (device * count + unit)
        out[unit * size : (unit + 1) * size] = held[table[place], table[place + 1]]


def last_small(real, count, *refs):
    gain_first, bias_in, bias_out, gain_second, bias_up, bias_down = refs[count:]
    sums = refs[0][...]
    for packed in refs[1:count]:
        sums = sums + packed[...]
    width = gain_first.shape[0]
    gain_first[...] = sums[0:1, :width].reshape(width)
    bias_in[...] = sums[1:3, :real]
    bias_out[...] = sums[3:4, :width].reshape(width)
    gain_second[...] = sums[4:5, :width].reshape(width)
    bias_down[...] = sums[5:6, :width].reshape(width)
    for at in range(bias_up.shape[0] // real):
        bias_up[at * real : (at + 1) * real] = sums[6 + at : 7 + at, :real].reshape(real)


def inward_units(chips, dp, real, mine):
    share = 3 * real // (2 * chips * dp)
    size = math.gcd(share, mine)
    count = share // size
    if chips * mine != real or size % 8:
        return None
    units, table = [], np.zeros((2 * chips * dp, count, 2), np.int32)
    for chip in range(chips):
        filled, own = {}, []
        for part in range(3):
            for at in range(mine // size):
                unit = (part * real + chip * mine) // size + at
                holder, place = unit // count, unit % count
                slot = ((holder // dp) & 1, holder % dp)
                here = filled.get(slot, 0)
                filled[slot] = here + 1
                own.append((*slot, here * size, part * mine + at * size, size))
                table[holder, place] = (holder // dp // 2) ^ chip, here
        if len(filled) != 2 * dp or set(filled.values()) != {count}:
            return None
        units.append(own)
    return size, units, table.reshape(-1)


def flip(value, mask, axis="seq"):
    return lax.ppermute(value, axis, [(at, at ^ mask) for at in range(lax.axis_size(axis))])


def bits_of(size):
    return [1 << at for at in range(size.bit_length() - 1)]


def local(
    tokens, doc_lengths, first_gain, inward_weight, inward_bias, outward_weight, outward_bias,
    second_gain, up_weight, up_bias, down_weight, down_bias, cotangent,
):
    rows, local_len, width = tokens.shape
    seq, dp = lax.axis_size("seq"), lax.axis_size("dp")
    chips = seq // 2
    block = rows * local_len
    length = seq * local_len
    real = HEADS * HEAD_DIM
    heads = -(-HEADS // chips)
    mine = heads * HEAD_DIM
    slots = chips * mine
    ff = up_weight.shape[1]
    chip_bits, dp_bits = bits_of(chips), bits_of(dp)

    def shape(*dims, kind=BF16):
        return jax.ShapeDtypeStruct(dims, kind)

    def call(kernel, name, outs, args, scratch=(), flops=0, mib=16, specs=None):
        nbytes = sum(arg.size * arg.dtype.itemsize for arg in args)
        return pl.pallas_call(
            kernel,
            out_shape=outs,
            in_specs=specs or [VMEM] * len(args),
            out_specs=jax.tree.map(lambda unused: VMEM, outs),
            scratch_shapes=scratch,
            compiler_params=pltpu.CompilerParams(vmem_limit_bytes=mib * 1024 * 1024),
            cost_estimate=pl.CostEstimate(flops=flops, bytes_accessed=nbytes, transcendentals=0),
            name=name,
        )(*args)

    def after(value, earlier):
        return hold((value, earlier))[0]

    half_rows = (shape(local_len, width),) * 2

    def to_rows(value, name):
        kept, sent = call(split_rows, name, half_rows, (jnp.transpose(value, (2, 0, 1)),), mib=8)
        return kept, flip(sent, 1)

    def from_rows(kept, sent, name):
        out = call(join_rows, name, shape(width, rows, local_len), (kept, flip(sent, 1)), mib=8)
        return jnp.transpose(out, (1, 2, 0))

    def exchange(pieces):
        return [pieces[0]] + [flip(pieces[at], 2 * at) for at in range(1, chips)]

    kept, got = to_rows(tokens, "split_tokens")
    wide = min(-(-mine // 128) * 128 + (128 if mine % 128 else 0), real)
    weight_mine, bias_mine, scale, starts = call(
        functools.partial(pick_weights, heads, chips, real), "pick_weights",
        [
            shape(width, 3 * mine), shape(1, 3 * mine, kind=F32), shape(1, width, kind=F32),
            shape(length, 1, kind=jnp.int32),
        ],
        (doc_lengths, after(first_gain, kept), inward_weight, inward_bias),
        scratch=[
            pltpu.VMEM((3, width, wide), BF16), pltpu.VMEM((width,), BF16), pltpu.VMEM((2, real), BF16),
            pltpu.SMEM(doc_lengths.shape, jnp.int32), pltpu.SemaphoreType.DMA((6,)),
        ],
        specs=[HBM] * 4,
    )
    projected = [shape(local_len, width), shape(local_len, 1, kind=F32), shape(local_len, 3 * mine)]

    def project_own():
        normed_one, row_tokens, *parts = call(
            project_first, "project_first", [shape(block, width)] * 2 + projected * 2,
            (kept, got, weight_mine, bias_mine, scale), flops=2 * block * width * 3 * mine,
        )
        return normed_one, row_tokens, parts

    places, pieces = [(0, 1), (0, 0)], [kept, got]
    if chips == 4:
        kept_one, kept_two = flip(kept, 2), flip(kept, 4)
        got_one, got_two = flip(got, 2), flip(got, 4)
        kept_three = flip(after(kept_two, weight_mine), 2)
        normed_one, row_tokens, parts = project_own()
        got_three = flip(after(got_one, row_tokens), 4)
        places += [(1, 1), (2, 1), (1, 0), (2, 0), (3, 1), (3, 0)]
        pieces += [kept_one, kept_two, got_one, got_two, kept_three, got_three]
    else:
        normed_one, row_tokens, parts = project_own()
        for which, value in ((1, kept), (0, got)):
            held = value[None]
            for bit in chip_bits:
                held = jnp.concatenate([held, flip(held, 2 * bit)], axis=0)
            places += [(at, which) for at in range(1, chips)]
            pieces += [held[at] for at in range(1, chips)]
    cot_kept, cot_got = to_rows(after(cotangent, row_tokens), "split_cotangent")
    fresh = 2
    middle = pieces[2:-fresh]
    parts += call(
        functools.partial(project_more, len(middle)), "project_more", projected * len(middle),
        (*middle, weight_mine, bias_mine, scale), flops=2 * block * len(middle) // 2 * width * 3 * mine,
    )
    row_cot, grad_active = call(
        active_cotangent, "active_cotangent", (shape(block, width), shape(block, ff, kind=F32)),
        (cot_kept, cot_got, down_weight), flops=2 * block * width * ff, mib=20,
    )

    forward = call(
        functools.partial(attention_forward, heads, chips, block, places, fresh), "attention_forward",
        [shape(length, 3 * mine), shape(length, mine, kind=F32), shape(length, 8, kind=F32)]
        + [shape(block, mine)] * chips + projected * fresh,
        (*parts[2::3], *pieces[-fresh:], weight_mine, bias_mine, scale, starts),
        flops=8 * length * length * mine, mib=20,
    )
    qkv, attended, logs = forward[:3]
    parts += forward[3 + chips :]
    attended_in = exchange(forward[3 : 3 + chips])

    half_ff, half_real = shape(block, ff // 2), shape(block, real // 2)
    (
        residual, normed_two, att_low, att_kept, att_sent, active, active_kept, active_sent,
        grad_up, up_kept, up_sent, up_sums,
    ) = call(
        functools.partial(up_branch, heads, chips, real), "up_branch",
        (
            shape(block, width, kind=F32), shape(block, width), shape(block, real), half_real, half_real,
            shape(block, ff), half_ff, half_ff, shape(block, ff), half_ff, half_ff, shape(1, ff, kind=F32),
        ),
        (*attended_in, row_tokens, grad_active, outward_weight, outward_bias, second_gain, up_weight, up_bias),
        flops=2 * block * width * ff, mib=28,
    )
    active_other, cot_other = flip(active_sent, 1), flip(row_cot, 1)
    up_other, two_other, att_other = flip(up_sent, 1), flip(normed_two, 1), flip(att_sent, 1)
    back = call(
        functools.partial(back_branch, heads, chips, real), "back_branch",
        (shape(block, mine),) * chips
        + (shape(block, width, kind=F32), shape(block, width), shape(8, width, kind=F32)),
        (residual, row_cot, grad_up, up_weight, outward_weight, second_gain),
        scratch=[pltpu.VMEM((block, slots), BF16)], flops=2 * block * width * ff, mib=20,
    )
    grad_res, grad_low, sums = back[chips:]
    low_other = flip(grad_low, 1)
    grad_in = exchange(back[:chips])

    share, out_share, in_share = ff // (seq * dp), real // (seq * dp), 3 * real // (seq * dp)
    cuts = ((0, share // 2), (share // 2, share))
    x_bit, y_bit = 0, len(chip_bits) - 1

    def stream(name, args, bit):
        dims = [(chips // 2, dp, high - low, width) for low, high in cuts]
        outs = call(
            functools.partial(stream_sums, chips, dp, bit, cuts), name,
            [shape(*dim) for dim in dims] + [shape(*dim, kind=F32) for dim in dims], args,
            flops=2 * block * ff * width, mib=20,
        )
        return list(outs[: len(cuts)]), list(outs[len(cuts) :])

    a_sent, a_kept = stream("down_sums", (active_kept, active_other, row_cot, cot_other), x_bit)
    a_got = [flip(sent, 2 << x_bit) for sent in a_sent]
    b_sent, b_kept = stream(
        "up_sums", (after(up_kept, a_sent[0]), up_other, normed_two, two_other), y_bit
    )
    b_got = [flip(sent, 2 << y_bit) for sent in b_sent]
    c_sent, c_kept = call(
        functools.partial(third_sums, chips, dp), "out_sums",
        [shape(dp // 2, chips, out_share, width), shape(dp // 2, chips, out_share, width, kind=F32)],
        (after(att_kept, b_sent[0]), att_other, grad_low, low_other), flops=2 * block * real * width,
    )
    c_got = flip(c_sent, dp_bits[0], "dp")

    grad_in[0] = after(grad_in[0], c_sent)
    *grad_qkv, grad_all = call(
        functools.partial(attention_backward, heads, chips, block), "attention_backward",
        [shape(block, 3 * mine)] * chips + [shape(length, 3 * mine)],
        (starts, qkv, attended, logs, *grad_in),
        scratch=[
            pltpu.VMEM((length, mine), BF16), pltpu.VMEM((length, HEAD_DIM), F32),
            pltpu.VMEM((length, HEAD_DIM), F32),
        ],
        flops=20 * length * length * mine, mib=20,
    )
    plan = inward_units(chips, dp, real, mine)
    row_outs = [shape(-(-(6 + ff // real) // 8) * 8, real, kind=F32)]
    if plan is not None:
        row_outs += [shape(dp, in_share, width), shape(dp, in_share, width, kind=F32)]
    packed, *inward = call(
        functools.partial(row_sums, heads, chips, block, places, real, plan and plan[1]), "row_sums", row_outs,
        (grad_all, weight_mine, sums, up_sums, *pieces, *parts[0::3], *parts[1::3]),
        scratch=[
            pltpu.VMEM((length, width), BF16), pltpu.VMEM((length, width), BF16),
            pltpu.VMEM((length, 1), F32), pltpu.VMEM((3 * mine, width), F32),
        ],
        flops=12 * length * mine * width, mib=24,
    )

    def folded(steps, kepts, gots, name, earlier):
        dims = [(kept.shape[0] // 2,) + kept.shape[1:] for kept in kepts]
        kepts = [after(kepts[0], earlier)] + kepts[1:]
        outs = call(
            functools.partial(fold, steps), name,
            [shape(*dim) for dim in dims] + [shape(*dim, kind=F32) for dim in dims], (*kepts, *gots),
        )
        return list(outs[: len(kepts)]), list(outs[len(kepts) :])

    def hop(value, step):
        return flip(value, 1 << step[1], step[0])

    def unwrap(members):
        return [member[0] if member.ndim == 4 and member.shape[0] == 1 else member for member in members]

    chip_steps = [("seq", 1 + at) for at in range(len(chip_bits))]
    dp_steps = [("dp", at) for at in range(len(dp_bits))]
    done = {}

    def wide_chain(chunk):
        kepts, gots = [a_kept[chunk], b_kept[chunk]], [a_got[chunk], b_got[chunk]]
        a_steps = [step for step in chip_steps if step[1] != 1 + x_bit] + dp_steps
        b_steps = [step for step in chip_steps if step[1] != 1 + y_bit] + dp_steps
        for steps in zip(a_steps, b_steps):
            earlier = yield
            sents, kepts = folded(steps, unwrap(kepts), unwrap(gots), f"fold_wide_{chunk}", earlier)
            gots = [hop(sent, step) for sent, step in zip(sents, steps)]
            done["last"] = sents[0]
        done[chunk] = [member for pair in zip(kepts, gots) for member in pair]

    def third_chain():
        kepts, gots = [c_kept], [c_got]
        for step in dp_steps[1:] + chip_steps:
            earlier = yield
            if step[0] == "seq":
                kepts, gots = unwrap(kepts), unwrap(gots)
            sents, kepts = folded((step,), kepts, gots, "fold_third", earlier)
            gots = [hop(sents[0], step)]
            done["last"] = sents[0]
        done["third"] = [kepts[0], gots[0]]

    def inward_chain():
        sent, kept = inward
        got, small, small_got = flip(sent, 1), packed, flip(packed, 1)
        for step in dp_steps:
            earlier = yield
            half = (kept.shape[0] // 2,) + kept.shape[1:]
            sent, kept, small = call(
                functools.partial(fold_small, step), "fold_inward",
                [shape(*half), shape(*half, kind=F32), shape(*packed.shape, kind=F32)],
                (after(kept, earlier), got, small, small_got),
            )
            got, small_got = hop(sent, step), hop(small, step)
            done["last"] = sent
        earlier = yield
        share_sum, share_low, small = call(
            last_inward, "last_inward",
            [shape(in_share, width, kind=F32), shape(in_share, width), shape(*packed.shape, kind=F32)],
            (after(kept, earlier), got, small, small_got),
        )
        done["last"] = share_low
        done["inward"] = [share_sum] + [flip(share_low, 2 * at) for at in range(1, chips)]
        done["small"] = [small] + [flip(small, 2 * at) for at in range(1, chips)]

    def output_chain():
        earlier = yield
        out_kept, out_sent = call(
            finish_output, "finish_output", half_rows, (residual, after(active, earlier), down_weight, down_bias),
            flops=2 * block * width * ff, mib=20,
        )
        done["last"] = out_sent
        done["output"] = from_rows(out_kept, out_sent, "join_output")

    def query_chain():
        earlier = yield
        done["pieces"] = exchange([after(piece, earlier) for piece in grad_qkv])

    chains = {"0": wide_chain(0), "1": wide_chain(1), "c": third_chain(), "o": output_chain(), "q": query_chain()}
    if plan is not None:
        chains["i"] = inward_chain()
    done["last"] = packed
    for chain in chains.values():
        next(chain)
    order = "0icoi1qc0i10c1c"
    names = list(order) + [name for unused in range(16) for name in chains]
    for name in names:
        if name in chains:
            try:
                chains[name].send(done["last"])
            except StopIteration:
                del chains[name]

    pairs = [done[chunk][2 * which + at] for which in range(2) for chunk in (0, 1) for at in range(2)]
    down_share, up_share, out_out = call(
        functools.partial(last_wide, cuts), "last_wide",
        [shape(share, width, kind=F32), shape(share, width, kind=F32), shape(out_share, width, kind=F32)],
        (*pairs, *done["third"]),
    )

    extra = [] if plan is not None else [shape(block, 3 * real)]
    rows_kept, rows_sent, *flat = call(
        functools.partial(finish_tokens, heads, chips, real), "finish_tokens", list(half_rows) + extra,
        (*done["pieces"], row_tokens, first_gain, grad_res, inward_weight),
        scratch=[] if extra else [pltpu.VMEM((block, 3 * real), BF16)],
        flops=6 * block * width * real, mib=20,
    )
    grad_tokens = from_rows(rows_kept, rows_sent, "join_tokens")
    if plan is not None:
        size, unused, table = plan
        in_out = call(
            functools.partial(place_inward, chips, dp, size), "place_inward", shape(in_share, width, kind=F32),
            (jnp.asarray(table), *done["inward"]),
            scratch=[pltpu.VMEM((chips, in_share // size, size, width), F32)],
            specs=[SMEM] + [VMEM] * chips,
        )
        smalls = done["small"]
    else:
        in_out = lax.psum_scatter(dot(flat[0], normed_one, 0, 0), ("seq", "dp"), scatter_dimension=0, tiled=True)
        for step in [("seq", 0)] + chip_steps + dp_steps:
            packed = packed + hop(packed, step)
        smalls = [packed]
    sums_shapes = [shape(width, kind=F32), shape(2, real, kind=F32), shape(width, kind=F32)]
    sums_shapes += [shape(width, kind=F32), shape(ff, kind=F32), shape(width, kind=F32)]
    gain_first, bias_in, bias_out, gain_second, bias_up, bias_down = call(
        functools.partial(last_small, real, len(smalls)), "last_small", sums_shapes, smalls
    )
    return (
        done["output"], grad_tokens, gain_first, in_out.T, bias_in, out_out, bias_out, gain_second,
        up_share.T, bias_up, down_share, bias_down,
    )


def solution(mesh):
    return jax.shard_map(
        local,
        mesh=mesh,
        in_specs=(P("dp", "seq", None), P("dp", None)) + (P(),) * 10 + (P("dp", "seq", None),),
        out_specs=(
            P("dp", "seq", None),
            P("dp", "seq", None),
            P(),
            P(None, ("seq", "dp")),
            P(),
            P(("seq", "dp"), None),
            P(),
            P(),
            P(None, ("seq", "dp")),
            P(),
            P(("seq", "dp"), None),
            P(),
        ),
        check_vma=False,
    )
```

```python
import functools
import math

import jax
import jax.numpy as jnp
import numpy as np
from jax import lax
from jax.experimental import pallas as pl
from jax.experimental.pallas import tpu as pltpu
from jax.sharding import PartitionSpec as P

HEADS = 12
HEAD_DIM = 64
EPSILON = 1e-05
FLOOR = -1e30
SCALE = HEAD_DIM**-0.5
QB = 256
F32 = jnp.float32
BF16 = jnp.bfloat16
VMEM = pl.BlockSpec(memory_space=pltpu.VMEM)
SMEM = pl.BlockSpec(memory_space=pltpu.SMEM)
hold = lax.optimization_barrier

def inverse_rms(values):
    squares = jnp.sum(values * values, axis=-1, keepdims=True)
    totals = jnp.sum(values, axis=-1, keepdims=True)
    return lax.rsqrt((squares + totals * totals) / (values.shape[-1] + 1) + EPSILON), totals


def norm_back(values, gain, inverse, totals, incoming):
    weighted = incoming * gain
    dots = jnp.sum(weighted * values, axis=-1, keepdims=True)
    factor = inverse * inverse * inverse * dots / (values.shape[-1] + 1)
    grad = inverse * weighted - factor * (values + totals)
    return grad, jnp.sum(incoming * values * inverse, axis=0, keepdims=True)


def dot(left, right, left_dim, right_dim):
    return lax.dot_general(
        left, right, (((left_dim,), (right_dim,)), ((), ())), preferred_element_type=F32
    )


def gelu_both(value):
    linear = 0.7978845608028654 * value
    cubic = linear * (0.044715 * (value * value))
    curve = jnp.tanh(linear + cubic)
    half = 0.5 + 0.5 * curve
    slope = half * (1.0 + (linear + 3.0 * cubic) * (1.0 - curve))
    return value * half, slope


def at_block(index, block):
    return pl.ds(pl.multiple_of(index * block, block), block)


def position():
    me = lax.axis_index("seq")
    return me >> 1, me & 1


def either(flag, first, second, left, right):
    @pl.when(flag == 0)
    def straight():
        first[...] = left
        second[...] = right

    @pl.when(flag != 0)
    def crossed():
        first[...] = right
        second[...] = left


def for_each_chip(chip, chips, body):
    for candidate in range(chips):
        pl.when(chip == candidate)(functools.partial(body, candidate))


def allowed_block(starts, query_start, keys):
    query_pos = query_start + lax.broadcasted_iota(jnp.int32, (QB, 1), 0)
    key_pos = lax.broadcasted_iota(jnp.int32, (1, keys), 1)
    return (key_pos <= query_pos) & (key_pos >= starts)


def split_rows(value, kept, sent):
    unused, core = position()
    length = value.shape[2]
    turned = value[...].reshape(value.shape[0], 2 * length).T
    either(core, kept, sent, turned[:length], turned[length:])


def join_rows(kept, *refs):
    gots, out = refs[:-1], refs[-1]
    unused, core = position()
    mine, other = [kept[...]], [got[...] for got in gots]

    def store(parts):
        out[...] = jnp.concatenate(parts, axis=0).T.reshape(out.shape)

    pl.when(core == 0)(lambda: store(mine + other))
    pl.when(core != 0)(lambda: store(other + mine))


def project(piece, scale, weight, bias, normed, inverse, qkv):
    values = piece[...].astype(F32)
    factor, unused = inverse_rms(values)
    low = (values * scale[...] * factor).astype(BF16)
    normed[...] = low
    inverse[...] = factor
    qkv[...] = (dot(low, weight[...], 1, 0) + bias[...]).astype(BF16)


def pick_weights(heads, chips, real, weight, weight_mine):
    width = heads * HEAD_DIM
    chip, unused = position()

    def choose(candidate):
        size = max(min(width, real - candidate * width), 0)
        for part in range(3):
            at, start = part * width, part * real + candidate * width
            if size > 0:
                weight_mine[:, at : at + size] = weight[:, start : start + size]
            if size < width:
                weight_mine[:, at + size : at + width] = jnp.zeros((weight.shape[0], width - size), BF16)

    for_each_chip(chip, chips, choose)


def project_first(heads, chips, real, docs, kept, got, gain, bias, weight, *refs):
    bias_mine, scale, starts, normed_own, own = refs[:5]
    width = heads * HEAD_DIM
    chip, core = position()

    def choose(candidate):
        size = max(min(width, real - candidate * width), 0)
        for part in (0, 2):
            if size > 0:
                bias_mine[:, part * width : part * width + size] = bias[
                    part // 2 : part // 2 + 1, candidate * width : candidate * width + size
                ].astype(F32)

    bias_mine[...] = jnp.zeros(bias_mine.shape, F32)
    for_each_chip(chip, chips, choose)
    scale[...] = gain[...].astype(F32).reshape(1, -1)
    places = lax.broadcasted_iota(jnp.int32, starts.shape, 0)
    start, end = jnp.zeros_like(places), jnp.int32(0)
    for at in range(3):
        end = end + docs[core, at]
        start = jnp.where(places >= end, end, start)
    starts[...] = start
    rows = kept.shape[0]
    for at, (piece, half) in enumerate(((kept, core), (got, 1 - core))):
        normed, inverse, qkv = refs[5 + 3 * at : 8 + 3 * at]
        project(piece, scale, weight, bias_mine, normed, inverse, qkv)
        normed_own[at_block(half, rows), :] = normed[...]
        own[at_block(half, rows), :] = piece[...]


def project_more(count, *refs):
    pieces, (weight, bias, scale), outs = refs[:count], refs[count : count + 3], refs[count + 3 :]
    for at, piece in enumerate(pieces):
        project(piece, scale, weight, bias, *outs[3 * at : 3 * at + 3])


def attention_forward(heads, chips, block, places, fresh, *refs):
    count = len(places)
    done, pieces = refs[: count - fresh], refs[count - fresh : count]
    (weight, bias, scale, starts), outs = refs[count : count + 4], refs[count + 4 :]
    qkv, attended, logs = outs[:3]
    sends, parts = outs[3 : 3 + chips], outs[3 + chips :]
    width = heads * HEAD_DIM
    chip, core = position()
    for at, (source, mine) in enumerate(places):
        part = done[at] if at < count - fresh else parts[3 * (at - count + fresh) + 2]
        if at >= count - fresh:
            at_parts = 3 * (at - count + fresh)
            project(pieces[at - count + fresh], scale, weight, bias, *parts[at_parts : at_parts + 3])
        rows = part.shape[0]
        half = core if mine else 1 - core
        start = pl.multiple_of((chip ^ source) * block + half * rows, rows)
        qkv[pl.ds(start, rows), :] = part[...]
    for at_query in range(chips * block // QB):
        rows = pl.ds(at_query * QB, QB)
        keys = (at_query + 1) * QB
        allowed = allowed_block(starts[rows, :], at_query * QB, keys)
        for head in range(heads):
            at = head * HEAD_DIM
            query = qkv[rows, at : at + HEAD_DIM] * BF16(SCALE)
            key = qkv[:keys, width + at : width + at + HEAD_DIM]
            value = qkv[:keys, 2 * width + at : 2 * width + at + HEAD_DIM]
            scores = jnp.where(allowed, dot(query, key, 1, 1), FLOOR)
            top = jnp.max(scores, axis=-1, keepdims=True)
            weights = jnp.exp(scores - top)
            total = jnp.sum(weights, axis=-1, keepdims=True)
            attended[rows, at : at + HEAD_DIM] = dot(weights.astype(BF16), value, 1, 0) / total
            logs[rows, head : head + 1] = top + jnp.log(total)
    for source in range(chips):
        sends[source][...] = attended[at_block(chip ^ source, block), :].astype(BF16)


def attention_backward(heads, chips, block, starts, qkv, attended, logs, *refs):
    grads, sends = refs[:chips], refs[chips : 2 * chips]
    out, grad_row, key_grad, value_grad = refs[2 * chips :]
    width = heads * HEAD_DIM
    chip, core = position()
    for source in range(chips):
        grad_row[at_block(chip ^ source, block), :] = grads[source][...]
    blocks = chips * block // QB
    for head in range(heads):
        at = head * HEAD_DIM
        for at_query in reversed(range(blocks)):
            rows = pl.ds(at_query * QB, QB)
            keys = (at_query + 1) * QB
            allowed = allowed_block(starts[rows, :], at_query * QB, keys)
            query = qkv[rows, at : at + HEAD_DIM] * BF16(SCALE)
            key = qkv[:keys, width + at : width + at + HEAD_DIM]
            value = qkv[:keys, 2 * width + at : 2 * width + at + HEAD_DIM]
            grad = grad_row[rows, at : at + HEAD_DIM]
            delta = jnp.sum(
                grad.astype(F32) * attended[rows, at : at + HEAD_DIM], axis=-1, keepdims=True
            )
            scores = dot(query, key, 1, 1)
            weights = jnp.where(allowed, jnp.exp(scores - logs[rows, head : head + 1]), 0.0)
            grad_weights = dot(grad, value, 1, 1)
            grad_scores = (weights * (grad_weights - delta)).astype(BF16)
            out[rows, at : at + HEAD_DIM] = (dot(grad_scores, key, 1, 0) * SCALE).astype(BF16)
            key_part = dot(grad_scores, query, 0, 0)
            value_part = dot(weights.astype(BF16), grad, 0, 0)
            if at_query == blocks - 1:
                key_grad[...] = key_part
                value_grad[...] = value_part
            else:
                key_grad[:keys, :] += key_part
                value_grad[:keys, :] += value_part
        out[:, width + at : width + at + HEAD_DIM] = key_grad[...].astype(BF16)
        out[:, 2 * width + at : 2 * width + at + HEAD_DIM] = value_grad[...].astype(BF16)
    for source in range(chips):
        sends[source][...] = out[at_block(chip ^ source, block), :]


def active_cotangent(kept, got, weight, row, out):
    unused, core = position()
    length = kept.shape[0]
    row[at_block(core, length), :] = kept[...]
    row[at_block(1 - core, length), :] = got[...]
    out[...] = dot(row[...], weight[...], 1, 1)


def up_branch(heads, chips, real, *refs):
    pieces = refs[:chips]
    tokens, grad_active, out_weight, out_bias, gain, up_weight, up_bias = refs[chips : chips + 7]
    residual, normed, att_low, active, grad_up, up_sums, kept, sent = refs[chips + 7 :]
    chip, core = position()
    mine = heads * HEAD_DIM
    ff = up_weight.shape[1]

    def place(candidate):
        for source in range(chips):
            start = (candidate ^ source) * mine
            size = min(mine, real - start)
            if size > 0:
                att_low[:, start : start + size] = pieces[source][:, :size]

    for_each_chip(chip, chips, place)
    values = (
        tokens[...].astype(F32)
        + dot(att_low[...], out_weight[...], 1, 0)
        + out_bias[...].astype(F32).reshape(1, -1)
    )
    residual[...] = values
    inverse, unused = inverse_rms(values)
    low = (values * gain[...].astype(F32).reshape(1, -1) * inverse).astype(BF16)
    normed[...] = low
    sent[:, ff + real // 2 :] = low

    def share(start, size, at, left, right):
        place = (slice(None), slice(start + at * size, start + (at + 1) * size))
        either(core, kept.at[place], sent.at[place], left, right)

    piece = real // (2 * chips)
    for at in range(chips):
        start = 2 * at * piece
        share(ff, piece, at, att_low[:, start : start + piece], att_low[:, start + piece : start + 2 * piece])
    tile = ff // chips
    piece = tile // 2
    for at in range(chips):
        cols = slice(at * tile, (at + 1) * tile)
        upward = dot(normed[...], up_weight[:, cols], 1, 0) + up_bias[cols].astype(F32).reshape(1, -1)
        act, slope = gelu_both(upward)
        low = act.astype(BF16)
        active[:, cols] = low
        share(0, piece, at, low[:, :piece], low[:, piece:])
        back = (grad_active[:, cols] * slope).astype(BF16)
        grad_up[:, cols] = back
        share(ff // 2, piece, at, back[:, :piece], back[:, piece:])
        up_sums[:, cols] = jnp.sum(back.astype(F32), axis=0, keepdims=True)


def back_branch(heads, chips, real, residual, cotangent, grad_up, up_weight, out_weight, gain, *refs):
    sends = refs[:chips]
    grad_res, grad_low, sums, wide = refs[chips:]
    chip, unused = position()
    mine = heads * HEAD_DIM
    values = residual[...]
    inverse, totals = inverse_rms(values)
    incoming = dot(grad_up[...], up_weight[...], 1, 1)
    grad, gain_sum = norm_back(values, gain[...].astype(F32).reshape(1, -1), inverse, totals, incoming)
    cot = cotangent[...].astype(F32)
    grad = grad + cot
    grad_res[...] = grad
    low = grad.astype(BF16)
    grad_low[...] = low
    sums[0:1, :] = jnp.sum(low.astype(F32), axis=0, keepdims=True)
    sums[1:2, :] = gain_sum
    sums[2:3, :] = jnp.sum(cot, axis=0, keepdims=True)
    wide[:, :real] = dot(low, out_weight[...], 1, 1).astype(BF16)
    if wide.shape[1] > real:
        wide[:, real:] = jnp.zeros((wide.shape[0], wide.shape[1] - real), BF16)

    def give(candidate):
        for source in range(chips):
            start = (candidate ^ source) * mine
            sends[source][...] = wide[:, start : start + mine]

    for_each_chip(chip, chips, give)


def finish_output(residual, active, weight, bias, kept, sent):
    unused, core = position()
    values = residual[...] + dot(active[...], weight[...], 1, 0) + bias[...].astype(F32).reshape(1, -1)
    low = values.astype(BF16)
    length = kept.shape[0]
    either(core, kept, sent, low[:length], low[length:])


def row_pieces(chips, block, places, pieces, out):
    chip, core = position()
    for (source, mine), piece in zip(places, pieces):
        rows = piece.shape[0]
        half = core if mine else 1 - core
        out[pl.ds(pl.multiple_of((chip ^ source) * block + half * rows, rows), rows), :] = piece[...]


def row_sums(heads, chips, block, places, real, units, grad_qkv, weight_mine, sums, up_sums, *refs):
    count = len(places)
    tokens, normed, inverse = refs[:count], refs[count : 2 * count], refs[2 * count : 3 * count]
    outs, scratch = refs[3 * count : -4], refs[-4:]
    row_tokens, row_normed, row_inverse, partial = scratch
    packed = outs[0]
    chip, core = position()
    mine = heads * HEAD_DIM
    row_pieces(chips, block, places, tokens, row_tokens)
    row_pieces(chips, block, places, inverse, row_inverse)
    if units is not None:
        row_pieces(chips, block, places, normed, row_normed)
        partial[...] = dot(grad_qkv[...], row_normed[...], 0, 0)
        sent, kept = outs[1:]
        share = kept.shape[1]
        small = 2 * packed.shape[0]

        def split(candidate):
            for for_core, for_replica, at, start, size in units[candidate]:

                @pl.when(core == for_core)
                def keep():
                    kept[for_replica, at : at + size] = partial[start : start + size]

                @pl.when(core != for_core)
                def send():
                    place = small + for_replica * share + at
                    sent[place : place + size, : partial.shape[1]] = partial[start : start + size].astype(BF16)

        for_each_chip(chip, chips, split)
    width = row_tokens.shape[1]
    packed[...] = jnp.zeros(packed.shape, F32)
    gain_sum = jnp.zeros((1, width), F32)
    for at in range(chips):
        rows = pl.ds(at * block, block)
        incoming = dot(grad_qkv[rows, :], weight_mine[...], 1, 1)
        gain_sum += jnp.sum(
            incoming * (row_tokens[rows, :].astype(F32) * row_inverse[rows, :]), axis=0, keepdims=True
        )
    packed[0:1, :width] = gain_sum
    query_sum = jnp.sum(grad_qkv[:, :mine].astype(F32), axis=0, keepdims=True)
    value_sum = jnp.sum(grad_qkv[:, 2 * mine :].astype(F32), axis=0, keepdims=True)

    def place(candidate):
        size = min(mine, real - candidate * mine)
        if size > 0:
            packed[1:2, candidate * mine : candidate * mine + size] = query_sum[:, :size]
            packed[2:3, candidate * mine : candidate * mine + size] = value_sum[:, :size]

    for_each_chip(chip, chips, place)
    packed[3:6, :width] = sums[0:3, :]
    for at in range(up_sums.shape[1] // real):
        packed[6 + at : 7 + at, :real] = up_sums[:, at * real : (at + 1) * real]
    if units is not None:
        put_small(packed, sent)


def put_small(packed, sent):
    rows = packed.shape[0]
    high = packed[...].astype(BF16)
    sent[:rows] = high
    sent[rows : 2 * rows] = (packed[...] - high.astype(F32)).astype(BF16)


def take_small(got, rows):
    return got[:rows].astype(F32) + got[rows : 2 * rows].astype(F32)


def finish_tokens(heads, chips, real, bundled, *refs):
    pieces = refs[:chips]
    tokens, gain, grad_res, weight, kept, sent, projected = refs[chips : chips + 7]
    halves = refs[chips + 7 :]
    chip, core = position()
    mine = heads * HEAD_DIM

    def place(candidate):
        for source in range(chips):
            start = (candidate ^ source) * mine
            size = min(mine, real - start)
            for part in range(3):
                if size > 0 and bundled[source] is None:
                    projected[:, part * real + start : part * real + start + size] = pieces[source][
                        :, part * mine : part * mine + size
                    ]
                elif size > 0:
                    cols = slice(part * real + start, part * real + start + size)
                    count = projected.shape[0]
                    most, last = unpack_piece(pieces[source], bundled[source], count, 3 * mine)
                    projected[: count * 3 // 4, cols] = most[:, part * mine : (part + 1) * mine]
                    projected[count * 3 // 4 :, cols] = last[part]

    for_each_chip(chip, chips, place)
    values = tokens[...].astype(F32)
    inverse, totals = inverse_rms(values)
    incoming = dot(projected[...], weight[...], 1, 1)
    grad, unused = norm_back(values, gain[...].astype(F32).reshape(1, -1), inverse, totals, incoming)
    low = (grad + grad_res[...]).astype(BF16)
    length = kept.shape[0]
    either(core, kept, sent, low[:length], low[length:])


def shared(chips, bit, at):
    chip, unused = position()
    return ((chip >> bit) & 1) == ((at >> bit) & 1), (at >> (bit + 1) << bit) | (at & ((1 << bit) - 1))


def stream_sums(chips, dp, bit, cut, columns, left, left_other, right, right_other, sent, kept, rest):
    start, rows, right_start = columns
    share = rows // dp
    for at in range(chips):
        cols = slice(start + at * rows, start + (at + 1) * rows)
        total = dot(left[:, cols], right[...], 0, 0) + dot(
            left_other[:, cols], right_other[:, right_start:], 0, 0
        )
        stays, place = shared(chips, bit, at)

        @pl.when(stays)
        def keep():
            for part in range(dp):
                kept[place, part] = total[part * share : part * share + cut]

        @pl.when(jnp.logical_not(stays))
        def send():
            for part in range(dp):
                sent[place, part] = total[part * share : part * share + cut].astype(BF16)

        for part in range(dp):
            rest[at, part] = total[part * share + cut : (part + 1) * share]


def third_sums(chips, dp, columns, left, left_other, right, right_other, down_rest, up_rest, sent, kept):
    start, rows, unused = columns
    share, down_more = rows // dp, down_rest.shape[2]
    more = down_more + up_rest.shape[2]
    mine = lax.axis_index("dp") & 1
    for at in range(chips):
        cols = slice(start + at * rows, start + (at + 1) * rows)
        total = dot(left[:, cols], right[...], 0, 0) + dot(left_other[:, cols], right_other[...], 0, 0)
        for part in range(dp):

            def store(ref, kind):
                ref[at, part >> 1, :down_more] = down_rest[at, part].astype(kind)
                ref[at, part >> 1, down_more:more] = up_rest[at, part].astype(kind)
                ref[at, part >> 1, more:] = total[part * share : (part + 1) * share].astype(kind)

            pl.when(mine == part & 1)(functools.partial(store, kept, F32))
            pl.when(mine != part & 1)(functools.partial(store, sent, BF16))


def fold(steps, *refs):
    count = len(steps)
    kepts, gots, sents, outs = (refs[at * count : (at + 1) * count] for at in range(4))
    for (axis, shift), kept, got, sent, out in zip(steps, kepts, gots, sents, outs):
        bit = (lax.axis_index(axis) >> shift) & 1
        for chip in range(out.shape[0]):
            for part in range(out.shape[1]):
                if axis == "seq":
                    mine, other = (2 * chip + bit, part), (2 * chip + 1 - bit, part)
                else:
                    mine, other = (chip, 2 * part + bit), (chip, 2 * part + 1 - bit)
                out[chip, part] = kept[mine] + got[mine].astype(F32)
                sent[chip, part] = (kept[other] + got[other].astype(F32)).astype(BF16)


def join_streams(step, *refs):
    kepts, gots, (sent, out) = refs[:3], refs[3:6], refs[6:]
    bit = (lax.axis_index(step[0]) >> step[1]) & 1
    start = 0
    for kept, got in zip(kepts, gots):
        rows = slice(start, start + kept.shape[2])
        start = rows.stop
        for part in range(out.shape[1]):
            mine, other = (0, 2 * part + bit), (0, 2 * part + 1 - bit)
            out[0, part, rows] = kept[mine] + got[mine].astype(F32)
            sent[0, part, rows] = (kept[other] + got[other].astype(F32)).astype(BF16)


def fold_inward(step, kept, got, packed, sent, out, packed_out):
    bit = (lax.axis_index(step[0]) >> step[1]) & 1
    rows, share, width = packed.shape[0], kept.shape[1], kept.shape[2]
    packed_out[...] = packed[...] + take_small(got, rows)
    put_small(packed_out, sent)
    for at in range(out.shape[0]):
        left, right = (
            kept[part] + got[2 * rows + part * share : 2 * rows + (part + 1) * share, :width].astype(F32)
            for part in (2 * at, 2 * at + 1)
        )
        start = 2 * rows + at * share
        out[at] = jnp.where(bit == 0, left, right)
        sent[start : start + share, :width] = jnp.where(bit == 0, right, left).astype(BF16)


def pack_piece(piece, out, start):
    count, wide = piece.shape
    rows, part = count * 3 // 4, wide // 3
    out[start : start + rows, :wide] = piece[:rows]
    for at in range(3):
        place = slice(start + at * rows // 3, start + (at + 1) * rows // 3)
        out[place, wide:] = piece[rows:, at * part : (at + 1) * part]


def unpack_piece(got, start, count, wide):
    rows, part = count * 3 // 4, wide // 3
    last = [got[start + at * rows // 3 : start + (at + 1) * rows // 3, wide : wide + part] for at in range(3)]
    return got[start : start + rows, :wide], last


def bundled_first(steps, *refs):
    kepts, gots, (in_kept, in_got, packed), ways = refs[:3], refs[3:6], refs[6:9], refs[9:11]
    sents, outs, (in_out, packed_out) = refs[11:14], refs[14:17], refs[17:]
    width = kepts[0].shape[3]
    ends = []
    for (axis, shift), kept, got, sent, out in zip(steps, kepts, gots, sents, outs):
        bit = (lax.axis_index(axis) >> shift) & 1
        rows, start = kept.shape[2], 0
        for chip in range(out.shape[0]):
            for part in range(out.shape[1]):
                if axis == "seq":
                    mine, other = (2 * chip + bit, part), (2 * chip + 1 - bit, part)
                else:
                    mine, other = (chip, 2 * part + bit), (chip, 2 * part + 1 - bit)
                out[chip, part] = kept[mine] + got[mine].astype(F32)
                sent[start : start + rows, :width] = (kept[other] + got[other].astype(F32)).astype(BF16)
                start += rows
        ends.append(start)
    fold_inward(steps[1], in_kept, in_got, packed, sents[1].at[ends[1] :], in_out, packed_out)
    pack_piece(ways[0], sents[2], ends[2])
    pack_piece(ways[1], sents[0], ends[0])


def bundled_second(steps, step, *refs):
    kepts, gots, (in_kept, packed) = refs[:3], refs[3:6], refs[6:8]
    sents, outs, rest = refs[8:11], refs[11:14], refs[14:]
    width = kepts[0].shape[3]
    for (axis, shift), kept, got, sent, out in zip(steps, kepts, gots, sents, outs):
        bit = (lax.axis_index(axis) >> shift) & 1
        rows, parts = kept.shape[2], kept.shape[1]

        def total(chip, part):
            start = pl.multiple_of((chip * parts + part) * rows, 8)
            return kept[chip, part] + got[pl.ds(start, rows), :width].astype(F32)

        for chip in range(out.shape[0]):
            for part in range(out.shape[1]):
                if axis == "seq":
                    mine, other = (2 * chip + bit, part), (2 * chip + 1 - bit, part)
                else:
                    mine, other = (chip, 2 * part + bit), (chip, 2 * part + 1 - bit)
                out[chip, part] = total(*mine)
                sent[chip, part] = total(*other).astype(BF16)
    start = kepts[1].shape[0] * kepts[1].shape[1] * kepts[1].shape[2]
    fold_inward(step, in_kept, gots[1].at[start:], packed, *rest)


def last_inward(kept, got, packed, share, low, packed_out):
    rows, count, width = packed.shape[0], share.shape[0], share.shape[1]
    total = kept[0] + got[2 * rows : 2 * rows + count, :width].astype(F32)
    share[...] = total
    low[2 * rows :, :width] = total.astype(BF16)
    packed_out[...] = packed[...] + take_small(got, rows)
    put_small(packed_out, low)


def last_wide(a_cut, b_cut, kept, got, down, up, outward):
    share = down.shape[0]

    def total(start, size):
        rows = slice(start, start + size)
        return kept[0, 0, rows] + got[0, 0, rows].astype(F32)

    down[:a_cut] = total(0, a_cut)
    up[:b_cut] = total(a_cut, b_cut)
    down[a_cut:] = total(a_cut + b_cut, share - a_cut)
    up[b_cut:] = total(b_cut + share, share - b_cut)
    outward[...] = total(2 * share, outward.shape[0])


def place_inward(chips, dp, size, real, table, share, packed, *refs):
    gots, out, outs, held = refs[: chips - 1], refs[chips - 1], refs[chips:-1], refs[-1]
    count, small = share.shape[0] // size, packed.shape[0]
    width = share.shape[1]
    sums = packed[...]
    for unit in range(count):
        held[0, unit] = share[unit * size : (unit + 1) * size]
        for at, piece in enumerate(gots):
            start = 2 * small + unit * size
            held[at + 1, unit] = piece[start : start + size, :width].astype(F32)
    for piece in gots:
        sums = sums + take_small(piece, small)
    put_sums(real, sums, *outs)
    device = lax.axis_index("seq") * dp + lax.axis_index("dp")
    for unit in range(count):
        place = 2 * (device * count + unit)
        out[unit * size : (unit + 1) * size] = held[table[place], table[place + 1]]


def put_sums(real, sums, gain_first, bias_in, bias_out, gain_second, bias_up, bias_down):
    width = gain_first.shape[0]
    gain_first[...] = sums[0:1, :width].reshape(width)
    bias_in[...] = sums[1:3, :real]
    bias_out[...] = sums[3:4, :width].reshape(width)
    gain_second[...] = sums[4:5, :width].reshape(width)
    bias_down[...] = sums[5:6, :width].reshape(width)
    for at in range(bias_up.shape[0] // real):
        bias_up[at * real : (at + 1) * real] = sums[6 + at : 7 + at, :real].reshape(real)


def last_small(real, packed, *outs):
    put_sums(real, packed[...], *outs)


def inward_units(chips, dp, real, mine):
    share = 3 * real // (2 * chips * dp)
    size = math.gcd(share, mine)
    count = share // size
    if chips != 4 or dp != 4 or chips * mine != real or size % 8:
        return None
    units, table = [], np.zeros((2 * chips * dp, count, 2), np.int32)
    for chip in range(chips):
        filled, own = {}, []
        for part in range(3):
            for at in range(mine // size):
                unit = (part * real + chip * mine) // size + at
                holder, place = unit // count, unit % count
                slot = ((holder // dp) & 1, holder % dp)
                here = filled.get(slot, 0)
                filled[slot] = here + 1
                own.append((*slot, here * size, part * mine + at * size, size))
                table[holder, place] = (holder // dp // 2) ^ chip, here
        if len(filled) != 2 * dp or set(filled.values()) != {count}:
            return None
        units.append(own)
    return size, units, table.reshape(-1)


def flip(value, mask, axis="seq"):
    return lax.ppermute(value, axis, [(at, at ^ mask) for at in range(lax.axis_size(axis))])


def bits_of(size):
    return [1 << at for at in range(size.bit_length() - 1)]


def local(
    tokens, doc_lengths, first_gain, inward_weight, inward_bias, outward_weight, outward_bias,
    second_gain, up_weight, up_bias, down_weight, down_bias, cotangent,
):
    rows, local_len, width = tokens.shape
    seq, dp = lax.axis_size("seq"), lax.axis_size("dp")
    chips = seq // 2
    block = rows * local_len
    length = seq * local_len
    real = HEADS * HEAD_DIM
    heads = -(-HEADS // chips)
    mine = heads * HEAD_DIM
    slots = chips * mine
    ff = up_weight.shape[1]
    chip_bits, dp_bits = bits_of(chips), bits_of(dp)

    def shape(*dims, kind=BF16):
        return jax.ShapeDtypeStruct(dims, kind)

    def call(kernel, name, outs, args, scratch=(), flops=1, mib=16, specs=None):
        return pl.pallas_call(
            kernel,
            out_shape=outs,
            in_specs=specs or [VMEM] * len(args),
            out_specs=jax.tree.map(lambda unused: VMEM, outs),
            scratch_shapes=scratch,
            compiler_params=pltpu.CompilerParams(vmem_limit_bytes=mib * 1024 * 1024),
            cost_estimate=pl.CostEstimate(flops=flops, bytes_accessed=1, transcendentals=0),
            name=name,
        )(*args)

    def after(value, earlier):
        return hold((value, earlier))[0]

    half_rows = (shape(local_len, width),) * 2

    def to_rows(value, name):
        kept, sent = call(split_rows, name, half_rows, (jnp.transpose(value, (2, 0, 1)),), mib=8)
        return kept, flip(sent, 1)

    def from_rows(kept, sent, name, parts=1):
        size = local_len // parts
        gots = [flip(sent[at * size : (at + 1) * size], 1) for at in range(parts)]
        out = call(join_rows, name, shape(width, rows, local_len), (kept, *gots), mib=8)
        return jnp.transpose(out, (1, 2, 0))

    def exchange(pieces):
        return [pieces[0]] + [flip(pieces[at], 2 * at) for at in range(1, chips)]

    kept, got = to_rows(tokens, "split_tokens")
    weight_mine = call(
        functools.partial(pick_weights, heads, chips, real), "pick_weights", shape(width, 3 * mine),
        (after(inward_weight, kept),),
    )
    places, pieces = [(0, 1), (0, 0)], [kept, got]
    if chips == 4:
        kept_one, kept_two = flip(kept, 2), flip(kept, 4)
        got_late = after(got, weight_mine)
        got_one, got_two = flip(got_late, 2), flip(got_late, 4)
        places += [(1, 1), (2, 1), (1, 0), (2, 0), (3, 1), (3, 0)]
        pieces += [kept_one, kept_two, got_one, got_two]
    else:
        for which, value in ((1, kept), (0, got)):
            held = value[None]
            for bit in chip_bits:
                held = jnp.concatenate([held, flip(held, 2 * bit)], axis=0)
            places += [(at, which) for at in range(1, chips)]
            pieces += [held[at] for at in range(1, chips)]
    projected = [shape(local_len, width), shape(local_len, 1, kind=F32), shape(local_len, 3 * mine)]
    bias_mine, scale, starts, normed_one, row_tokens, *parts = call(
        functools.partial(project_first, heads, chips, real), "project_first",
        [shape(1, 3 * mine, kind=F32), shape(1, width, kind=F32), shape(length, 1, kind=jnp.int32)]
        + [shape(block, width)] * 2 + projected * 2,
        (doc_lengths, kept, got, first_gain, inward_bias, weight_mine),
        flops=2 * block * width * 3 * mine, specs=[SMEM] + [VMEM] * 5,
    )
    if chips == 4:
        pieces.append(flip(after(kept_one, (kept_two, row_tokens)), 4))
        pieces.append(flip(after(got_two, row_tokens), 2))
    cot_kept, cot_got = to_rows(after(cotangent, pieces[3]), "split_cotangent")
    fresh = 2
    middle = pieces[2:-fresh]
    parts += call(
        functools.partial(project_more, len(middle)), "project_more", projected * len(middle),
        (*middle, weight_mine, bias_mine, scale), flops=block * len(middle) * width * 3 * mine,
    )
    row_cot, grad_active = call(
        active_cotangent, "active_cotangent", (shape(block, width), shape(block, ff, kind=F32)),
        (cot_kept, cot_got, down_weight), mib=16,
    )

    forward = call(
        functools.partial(attention_forward, heads, chips, block, places, fresh), "attention_forward",
        [shape(length, 3 * mine), shape(length, mine, kind=F32), shape(length, 8, kind=F32)]
        + [shape(block, mine)] * chips + projected * fresh,
        (*parts[2::3], *pieces[-fresh:], weight_mine, bias_mine, scale, starts),
        flops=8 * length * length * mine, mib=8 + length // 128,
    )
    qkv, attended, logs = forward[:3]
    parts += forward[3 + chips :]
    attended_in = exchange(forward[3 : 3 + chips])
    row_cot, grad_active = call(
        active_cotangent, "active_cotangent", (shape(block, width), shape(block, ff, kind=F32)),
        (after(cot_kept, forward[3]), cot_got, down_weight), flops=2 * block * width * ff,
    )

    cot_other = flip(row_cot, 1)
    residual, normed_two, att_low, active, grad_up, up_sums, kept, sent = call(
        functools.partial(up_branch, heads, chips, real), "up_branch",
        (
            shape(block, width, kind=F32), shape(block, width), shape(block, real), shape(block, ff),
            shape(block, ff), shape(1, ff, kind=F32), shape(block, ff + real // 2),
            shape(block, ff + real // 2 + width),
        ),
        (
            *attended_in, row_tokens, grad_active, outward_weight, outward_bias, second_gain,
            up_weight, up_bias,
        ),
        flops=2 * block * width * ff, mib=23,
    )
    other = flip(sent, 1)
    back = call(
        functools.partial(back_branch, heads, chips, real), "back_branch",
        (shape(block, mine),) * chips
        + (shape(block, width, kind=F32), shape(block, width), shape(8, width, kind=F32)),
        (residual, row_cot, grad_up, up_weight, outward_weight, second_gain),
        scratch=[pltpu.VMEM((block, slots), BF16)], flops=2 * block * width * ff, mib=16,
    )
    grad_res, grad_low, sums = back[chips:]
    low_other = flip(grad_low, 1)
    grad_in = exchange(back[:chips])

    share, out_share, in_share = ff // (seq * dp), real // (seq * dp), 3 * real // (seq * dp)
    a_cut, b_cut = share - share // 12, share - share // 4
    third = 2 * share - a_cut - b_cut + out_share
    x_bit, y_bit = 0, len(chip_bits) - 1

    def stream(name, bit, cut, columns, args):
        dims = (chips // 2, dp, cut, width)
        return call(
            functools.partial(stream_sums, chips, dp, bit, cut, columns), name,
            [shape(*dims), shape(*dims, kind=F32), shape(chips, dp, share - cut, width, kind=F32)], args,
            mib=18,
        )

    a_sent, a_kept, down_rest = stream(
        "down_sums", x_bit, a_cut, (0, ff // seq, 0), (kept, other, row_cot, cot_other)
    )
    b_sent, b_kept, up_rest = stream(
        "up_sums", y_bit, b_cut, (ff // 2, ff // seq, ff + real // 2), (after(kept, a_sent), other, normed_two, other)
    )
    c_dims = (chips, dp // 2, third, width)
    c_sent, c_kept = call(
        functools.partial(third_sums, chips, dp, (ff, real // seq, 0)), "out_sums",
        [shape(*c_dims), shape(*c_dims, kind=F32)],
        (after(kept, (b_sent, *grad_in[1:-1])), other, grad_low, low_other, down_rest, up_rest), mib=18,
    )
    a_got, b_got, c_got = flip(a_sent, 2 << x_bit), flip(b_sent, 2 << y_bit), flip(c_sent, 1, "dp")

    grad_in[0] = after(grad_in[0], c_sent)
    *grad_qkv, grad_all = call(
        functools.partial(attention_backward, heads, chips, block), "attention_backward",
        [shape(block, 3 * mine)] * chips + [shape(length, 3 * mine)],
        (starts, qkv, attended, logs, *grad_in),
        scratch=[
            pltpu.VMEM((length, mine), BF16), pltpu.VMEM((length, HEAD_DIM), F32),
            pltpu.VMEM((length, HEAD_DIM), F32),
        ],
        flops=200 * length * length * mine, mib=8 + length // 128,
    )
    plan = inward_units(chips, dp, real, mine)
    small_rows = -(-(6 + ff // real) // 16) * 16
    packed_shape = shape(small_rows, real, kind=F32)
    row_outs = [packed_shape]
    if plan is not None:
        row_outs += [shape(2 * small_rows + dp * in_share, real), shape(dp, in_share, width, kind=F32)]
    packed, *inward = call(
        functools.partial(row_sums, heads, chips, block, places, real, plan and plan[1]), "row_sums", row_outs,
        (grad_all, weight_mine, sums, up_sums, *pieces, *parts[0::3], *parts[1::3]),
        scratch=[
            pltpu.VMEM((length, width), BF16), pltpu.VMEM((length, width), BF16),
            pltpu.VMEM((length, 1), F32), pltpu.VMEM((3 * mine, width), F32),
        ],
        flops=12 * length * mine * width, mib=8 + length // 128 + 2,
    )

    def hop(value, step):
        return flip(value, 1 << step[1], step[0])

    chip_steps = [("seq", 1 + at) for at in range(len(chip_bits))]
    dp_steps = [("dp", at) for at in range(len(dp_bits))]
    rounds = list(zip(
        [step for step in chip_steps if step[1] != 1 + x_bit] + dp_steps[:1],
        dp_steps[:1] + [step for step in chip_steps if step[1] != 1 + y_bit],
        chip_steps,
    ))
    kepts, gots = [a_kept, b_kept, c_kept], [a_got, b_got, c_got]
    earlier = packed
    if plan is not None:
        in_sent, in_kept = inward
        in_got, small = flip(in_sent, 1), packed

    def half_dims(at):
        dims = [list(kept.shape) for kept in kepts]
        for dim, step in zip(dims, rounds[at]):
            dim[step[0] == "dp"] //= 2
        return dims

    sums_shapes = [shape(width, kind=F32), shape(2, real, kind=F32), shape(width, kind=F32)]
    sums_shapes += [shape(width, kind=F32), shape(ff, kind=F32), shape(width, kind=F32)]
    out_kept, out_sent = call(
        finish_output, "finish_output", half_rows, (residual, after(active, earlier), down_weight, down_bias),
    )
    output_tokens = from_rows(out_kept, out_sent, "join_output")
    bundled = [None] * chips
    if plan is not None:
        half = (in_kept.shape[0] // 2,) + in_kept.shape[1:]
        dims = half_dims(0)
        counts = [math.prod(dim[:3]) for dim in dims]
        more = [block * 3 // 4, 2 * small_rows + half[0] * in_share, block * 3 // 4]
        outs = call(
            functools.partial(bundled_first, rounds[0]), "round_0",
            [shape(count + rest, real) for count, rest in zip(counts, more)]
            + [shape(*dim, kind=F32) for dim in dims] + [shape(*half, kind=F32), packed_shape],
            (after(kepts[0], out_sent), *kepts[1:], *gots, in_kept, in_got, small, grad_qkv[1], grad_qkv[2]),
        )
        gots = [hop(sent, step) for sent, step in zip(outs[:3], rounds[0])]
        kepts, in_kept, small = outs[3:6], outs[6], outs[7]
        queries_in = [grad_qkv[0], gots[2], gots[0]]
        bundled = [None, counts[2], counts[0], None]
        half = (half[0] // 2,) + half[1:]
        dims = half_dims(1)
        outs = call(
            functools.partial(bundled_second, rounds[1], dp_steps[1]), "round_1",
            [shape(*dim) for dim in dims] + [shape(*dim, kind=F32) for dim in dims]
            + [shape(2 * small_rows + half[0] * in_share, real), shape(*half, kind=F32), packed_shape],
            (after(kepts[0], output_tokens), *kepts[1:], *gots, in_kept, small),
        )
        gots = [hop(sent, step) for sent, step in zip(outs[:3], rounds[1])]
        kepts, in_got, in_kept, small = outs[3:6], hop(outs[6], dp_steps[1]), outs[7], outs[8]
        earlier = outs[0]
    else:
        for at in range(len(rounds)):
            dims = half_dims(at)
            outs = call(
                functools.partial(fold, rounds[at]), f"round_{at}",
                [shape(*dim) for dim in dims] + [shape(*dim, kind=F32) for dim in dims], (*kepts, *gots),
            )
            kepts, gots = outs[3:], [hop(sent, step) for sent, step in zip(outs[:3], rounds[at])]
        queries_in = exchange(grad_qkv)
    if plan is not None:
        share_sum, low, small = call(
            last_inward, "last_inward",
            [shape(in_share, width, kind=F32), shape(2 * small_rows + in_share, real), packed_shape],
            (after(in_kept, earlier), in_got, small),
        )
        earlier = low
    dims = (1, kepts[0].shape[1] // 2, a_cut + b_cut + third, width)
    sent, kept = call(
        functools.partial(join_streams, dp_steps[1]), "join_streams", [shape(*dims), shape(*dims, kind=F32)],
        (after(kepts[0], earlier), *kepts[1:], *gots),
    )
    got = hop(sent, dp_steps[1])
    earlier = sent
    for step in dp_steps[2:]:
        dims = (1, kept.shape[1] // 2) + kept.shape[2:]
        sent, kept = call(
            functools.partial(fold, (step,)), "fold_joined", [shape(*dims), shape(*dims, kind=F32)], (kept, got)
        )
        got = hop(sent, step)
    if plan is not None:
        queries_in.append(flip(after(grad_qkv[3], sent), 6))
        low = after(low, sent)
        in_pieces = [share_sum, small] + [flip(low, 2 * at) for at in range(1, chips)]

    extra = [] if plan is not None else [shape(block, 3 * real)]
    rows_kept, rows_sent, *flat = call(
        functools.partial(finish_tokens, heads, chips, real, bundled), "finish_tokens", list(half_rows) + extra,
        (*queries_in, after(row_tokens, earlier), first_gain, grad_res, inward_weight),
        scratch=[] if extra else [pltpu.VMEM((block, 3 * real), BF16)],
        mib=16,
    )
    if plan is not None:
        size, unused, table = plan
        in_out, *sums_out = call(
            functools.partial(place_inward, chips, dp, size, real), "place_inward",
            [shape(in_share, width, kind=F32)] + sums_shapes, (jnp.asarray(table), in_pieces[0], *in_pieces[1:]),
            scratch=[pltpu.VMEM((chips, in_share // size, size, width), F32)],
            specs=[SMEM] + [VMEM] * (chips + 1),
        )
    else:
        in_out = lax.psum_scatter(dot(flat[0], normed_one, 0, 0), ("seq", "dp"), scatter_dimension=0, tiled=True)
        for step in [("seq", 0)] + chip_steps + dp_steps:
            packed = packed + hop(packed, step)
        sums_out = call(functools.partial(last_small, real), "last_small", sums_shapes, (packed,))
    grad_tokens = from_rows(after(rows_kept, in_out), rows_sent, "join_tokens", 2)
    down_share, up_share, out_out = call(
        functools.partial(last_wide, a_cut, b_cut), "last_wide",
        [shape(share, width, kind=F32), shape(share, width, kind=F32), shape(out_share, width, kind=F32)],
        (after(kept, in_out), got),
    )

    gain_first, bias_in, bias_out, gain_second, bias_up, bias_down = sums_out
    return (
        output_tokens, grad_tokens, gain_first, in_out.T, bias_in, out_out, bias_out, gain_second,
        up_share.T, bias_up, down_share, bias_down,
    )


def solution(mesh):
    return jax.shard_map(
        local,
        mesh=mesh,
        in_specs=(P("dp", "seq", None), P("dp", None)) + (P(),) * 10 + (P("dp", "seq", None),),
        out_specs=(
            P("dp", "seq", None),
            P("dp", "seq", None),
            P(),
            P(None, ("seq", "dp")),
            P(),
            P(("seq", "dp"), None),
            P(),
            P(),
            P(None, ("seq", "dp")),
            P(),
            P(("seq", "dp"), None),
            P(),
        ),
        check_vma=False,
    )
```

```python
import functools
import math

import jax
import jax.numpy as jnp
import numpy as np
from jax import lax
from jax.experimental import pallas as pl
from jax.experimental.pallas import tpu as pltpu
from jax.sharding import PartitionSpec as P

HEADS = 12
HEAD_DIM = 64
EPSILON = 1e-05
FLOOR = -1e30
SCALE = HEAD_DIM**-0.5
QB = 256
F32 = jnp.float32
BF16 = jnp.bfloat16
VMEM = pl.BlockSpec(memory_space=pltpu.VMEM)
SMEM = pl.BlockSpec(memory_space=pltpu.SMEM)
hold = lax.optimization_barrier

def inverse_rms(values):
    squares = jnp.sum(values * values, axis=-1, keepdims=True)
    totals = jnp.sum(values, axis=-1, keepdims=True)
    return lax.rsqrt((squares + totals * totals) / (values.shape[-1] + 1) + EPSILON), totals


def norm_back(values, gain, inverse, totals, incoming):
    weighted = incoming * gain
    dots = jnp.sum(weighted * values, axis=-1, keepdims=True)
    factor = inverse * inverse * inverse * dots / (values.shape[-1] + 1)
    grad = inverse * weighted - factor * (values + totals)
    return grad, jnp.sum(incoming * values * inverse, axis=0, keepdims=True)


def dot(left, right, left_dim, right_dim):
    return lax.dot_general(
        left, right, (((left_dim,), (right_dim,)), ((), ())), preferred_element_type=F32
    )


def gelu_both(value):
    linear = 0.7978845608028654 * value
    cubic = linear * (0.044715 * (value * value))
    curve = jnp.tanh(linear + cubic)
    half = 0.5 + 0.5 * curve
    slope = half * (1.0 + (linear + 3.0 * cubic) * (1.0 - curve))
    return value * half, slope


def at_block(index, block):
    return pl.ds(pl.multiple_of(index * block, block), block)


def position():
    me = lax.axis_index("seq")
    return me >> 1, me & 1


def either(flag, first, second, left, right):
    @pl.when(flag == 0)
    def straight():
        first[...] = left
        second[...] = right

    @pl.when(flag != 0)
    def crossed():
        first[...] = right
        second[...] = left


def for_each_chip(chip, chips, body):
    for candidate in range(chips):
        pl.when(chip == candidate)(functools.partial(body, candidate))


def allowed_block(starts, query_start, keys):
    query_pos = query_start + lax.broadcasted_iota(jnp.int32, (QB, 1), 0)
    key_pos = lax.broadcasted_iota(jnp.int32, (1, keys), 1)
    return (key_pos <= query_pos) & (key_pos >= starts)


def split_rows(value, kept, sent):
    unused, core = position()
    length = value.shape[2]
    turned = value[...].reshape(value.shape[0], 2 * length).T
    either(core, kept, sent, turned[:length], turned[length:])


def join_rows(kept, *refs):
    gots, out = refs[:-1], refs[-1]
    unused, core = position()
    mine, other = [kept[...]], [got[...] for got in gots]

    def store(parts):
        out[...] = jnp.concatenate(parts, axis=0).T.reshape(out.shape)

    pl.when(core == 0)(lambda: store(mine + other))
    pl.when(core != 0)(lambda: store(other + mine))


def project(piece, scale, weight, bias, normed, inverse, qkv):
    values = piece[...].astype(F32)
    factor, unused = inverse_rms(values)
    low = (values * scale[...] * factor).astype(BF16)
    normed[...] = low
    inverse[...] = factor
    qkv[...] = (dot(low, weight[...], 1, 0) + bias[...]).astype(BF16)


def pick_weights(heads, chips, real, weight, weight_mine):
    width = heads * HEAD_DIM
    chip, unused = position()

    def choose(candidate):
        size = max(min(width, real - candidate * width), 0)
        for part in range(3):
            at, start = part * width, part * real + candidate * width
            if size > 0:
                weight_mine[:, at : at + size] = weight[:, start : start + size]
            if size < width:
                weight_mine[:, at + size : at + width] = jnp.zeros((weight.shape[0], width - size), BF16)

    for_each_chip(chip, chips, choose)


def project_first(heads, chips, real, docs, kept, got, gain, bias, weight, *refs):
    bias_mine, scale, starts, normed_own, own = refs[:5]
    width = heads * HEAD_DIM
    chip, core = position()

    def choose(candidate):
        size = max(min(width, real - candidate * width), 0)
        for part in (0, 2):
            if size > 0:
                bias_mine[:, part * width : part * width + size] = bias[
                    part // 2 : part // 2 + 1, candidate * width : candidate * width + size
                ].astype(F32)

    bias_mine[...] = jnp.zeros(bias_mine.shape, F32)
    for_each_chip(chip, chips, choose)
    scale[...] = gain[...].astype(F32).reshape(1, -1)
    places = lax.broadcasted_iota(jnp.int32, starts.shape, 0)
    start, end = jnp.zeros_like(places), jnp.int32(0)
    for at in range(3):
        end = end + docs[core, at]
        start = jnp.where(places >= end, end, start)
    starts[...] = start
    rows = kept.shape[0]
    for at, (piece, half) in enumerate(((kept, core), (got, 1 - core))):
        normed, inverse, qkv = refs[5 + 3 * at : 8 + 3 * at]
        project(piece, scale, weight, bias_mine, normed, inverse, qkv)
        normed_own[at_block(half, rows), :] = normed[...]
        own[at_block(half, rows), :] = piece[...]


def project_more(count, *refs):
    pieces, (weight, bias, scale), outs = refs[:count], refs[count : count + 3], refs[count + 3 :]
    for at, piece in enumerate(pieces):
        project(piece, scale, weight, bias, *outs[3 * at : 3 * at + 3])


def attention_forward(heads, chips, block, places, fresh, *refs):
    count = len(places)
    done, pieces = refs[: count - fresh], refs[count - fresh : count]
    (weight, bias, scale, starts), outs = refs[count : count + 4], refs[count + 4 :]
    qkv, attended, logs = outs[:3]
    sends, parts = outs[3 : 3 + chips], outs[3 + chips :]
    width = heads * HEAD_DIM
    chip, core = position()
    for at, (source, mine) in enumerate(places):
        part = done[at] if at < count - fresh else parts[3 * (at - count + fresh) + 2]
        if at >= count - fresh:
            at_parts = 3 * (at - count + fresh)
            project(pieces[at - count + fresh], scale, weight, bias, *parts[at_parts : at_parts + 3])
        rows = part.shape[0]
        half = core if mine else 1 - core
        start = pl.multiple_of((chip ^ source) * block + half * rows, rows)
        qkv[pl.ds(start, rows), :] = part[...]
    for at_query in range(chips * block // QB):
        rows = pl.ds(at_query * QB, QB)
        keys = (at_query + 1) * QB
        allowed = allowed_block(starts[rows, :], at_query * QB, keys)
        for head in range(heads):
            at = head * HEAD_DIM
            query = qkv[rows, at : at + HEAD_DIM] * BF16(SCALE)
            key = qkv[:keys, width + at : width + at + HEAD_DIM]
            value = qkv[:keys, 2 * width + at : 2 * width + at + HEAD_DIM]
            scores = jnp.where(allowed, dot(query, key, 1, 1), FLOOR)
            top = jnp.max(scores, axis=-1, keepdims=True)
            weights = jnp.exp(scores - top)
            total = jnp.sum(weights, axis=-1, keepdims=True)
            attended[rows, at : at + HEAD_DIM] = dot(weights.astype(BF16), value, 1, 0) / total
            logs[rows, head : head + 1] = top + jnp.log(total)
    for source in range(chips):
        sends[source][...] = attended[at_block(chip ^ source, block), :].astype(BF16)


def attention_backward(heads, chips, block, starts, qkv, attended, logs, *refs):
    grads, sends = refs[:chips], refs[chips : 2 * chips]
    out, grad_row, key_grad, value_grad = refs[2 * chips :]
    width = heads * HEAD_DIM
    chip, core = position()
    for source in range(chips):
        grad_row[at_block(chip ^ source, block), :] = grads[source][...]
    blocks = chips * block // QB
    for head in range(heads):
        at = head * HEAD_DIM
        for at_query in reversed(range(blocks)):
            rows = pl.ds(at_query * QB, QB)
            keys = (at_query + 1) * QB
            allowed = allowed_block(starts[rows, :], at_query * QB, keys)
            query = qkv[rows, at : at + HEAD_DIM] * BF16(SCALE)
            key = qkv[:keys, width + at : width + at + HEAD_DIM]
            value = qkv[:keys, 2 * width + at : 2 * width + at + HEAD_DIM]
            grad = grad_row[rows, at : at + HEAD_DIM]
            delta = jnp.sum(
                grad.astype(F32) * attended[rows, at : at + HEAD_DIM], axis=-1, keepdims=True
            )
            scores = dot(query, key, 1, 1)
            weights = jnp.where(allowed, jnp.exp(scores - logs[rows, head : head + 1]), 0.0)
            grad_weights = dot(grad, value, 1, 1)
            grad_scores = (weights * (grad_weights - delta)).astype(BF16)
            out[rows, at : at + HEAD_DIM] = (dot(grad_scores, key, 1, 0) * SCALE).astype(BF16)
            key_part = dot(grad_scores, query, 0, 0)
            value_part = dot(weights.astype(BF16), grad, 0, 0)
            if at_query == blocks - 1:
                key_grad[...] = key_part
                value_grad[...] = value_part
            else:
                key_grad[:keys, :] += key_part
                value_grad[:keys, :] += value_part
        out[:, width + at : width + at + HEAD_DIM] = key_grad[...].astype(BF16)
        out[:, 2 * width + at : 2 * width + at + HEAD_DIM] = value_grad[...].astype(BF16)
    for source in range(chips):
        sends[source][...] = out[at_block(chip ^ source, block), :]


def active_cotangent(kept, got, weight, row, out):
    unused, core = position()
    length = kept.shape[0]
    row[at_block(core, length), :] = kept[...]
    row[at_block(1 - core, length), :] = got[...]
    out[...] = dot(row[...], weight[...], 1, 1)


def up_branch(heads, chips, real, *refs):
    pieces = refs[:chips]
    tokens, grad_active, out_weight, out_bias, gain, up_weight, up_bias = refs[chips : chips + 7]
    residual, normed, active, grad_up, up_sums, kept, sent = refs[chips + 7 :]
    chip, core = position()
    mine = heads * HEAD_DIM
    ff = up_weight.shape[1]

    values = tokens[...].astype(F32) + out_bias[...].astype(F32).reshape(1, -1)
    for source, piece in enumerate(pieces):
        values = values + dot(piece[...], out_weight[at_block(chip ^ source, mine), :], 1, 0)
    residual[...] = values
    inverse, unused = inverse_rms(values)
    low = (values * gain[...].astype(F32).reshape(1, -1) * inverse).astype(BF16)
    normed[...] = low
    sent[:, ff + mine * chips // 2 :] = low

    def share(start, size, at, left, right):
        place = slice(start + at * size, start + (at + 1) * size)
        kept[:, place] = jnp.where(core == 0, left, right)
        sent[:, place] = jnp.where(core == 0, right, left)

    for source, piece in enumerate(pieces):
        share(ff, mine // 2, source, piece[:, : mine // 2], piece[:, mine // 2 :])
    tile = ff // chips
    piece = tile // 2
    for at in range(chips):
        cols = slice(at * tile, (at + 1) * tile)
        upward = dot(normed[...], up_weight[:, cols], 1, 0) + up_bias[cols].astype(F32).reshape(1, -1)
        act, slope = gelu_both(upward)
        low = act.astype(BF16)
        active[:, cols] = low
        share(0, piece, at, low[:, :piece], low[:, piece:])
        back = (grad_active[:, cols] * slope).astype(BF16)
        grad_up[:, cols] = back
        share(ff // 2, piece, at, back[:, :piece], back[:, piece:])
        up_sums[:, cols] = jnp.sum(back.astype(F32), axis=0, keepdims=True)


def back_branch(heads, chips, real, residual, cotangent, grad_up, up_weight, out_weight, gain, *refs):
    sends = refs[:chips]
    grad_res, grad_low, sums = refs[chips:]
    chip, unused = position()
    mine = heads * HEAD_DIM
    values = residual[...]
    inverse, totals = inverse_rms(values)
    incoming = dot(grad_up[...], up_weight[...], 1, 1)
    grad, gain_sum = norm_back(values, gain[...].astype(F32).reshape(1, -1), inverse, totals, incoming)
    cot = cotangent[...].astype(F32)
    grad = grad + cot
    grad_res[...] = grad
    low = grad.astype(BF16)
    grad_low[...] = low
    sums[0:1, :] = jnp.sum(low.astype(F32), axis=0, keepdims=True)
    sums[1:2, :] = gain_sum
    sums[2:3, :] = jnp.sum(cot, axis=0, keepdims=True)
    for source in range(chips):
        sends[source][...] = dot(low, out_weight[at_block(chip ^ source, mine), :], 1, 1).astype(BF16)


def finish_output(residual, active, weight, bias, kept, sent):
    unused, core = position()
    values = residual[...] + dot(active[...], weight[...], 1, 0) + bias[...].astype(F32).reshape(1, -1)
    low = values.astype(BF16)
    length = kept.shape[0]
    either(core, kept, sent, low[:length], low[length:])


def row_pieces(chips, block, places, pieces, out):
    chip, core = position()
    for (source, mine), piece in zip(places, pieces):
        rows = piece.shape[0]
        half = core if mine else 1 - core
        out[pl.ds(pl.multiple_of((chip ^ source) * block + half * rows, rows), rows), :] = piece[...]


def row_sums(heads, chips, block, places, real, units, grad_qkv, weight_mine, sums, up_sums, *refs):
    count = len(places)
    tokens, normed, inverse = refs[:count], refs[count : 2 * count], refs[2 * count : 3 * count]
    outs, scratch = refs[3 * count : -4], refs[-4:]
    row_tokens, row_normed, row_inverse, partial = scratch
    packed = outs[0]
    chip, core = position()
    mine = heads * HEAD_DIM
    row_pieces(chips, block, places, tokens, row_tokens)
    row_pieces(chips, block, places, inverse, row_inverse)
    if units is not None:
        row_pieces(chips, block, places, normed, row_normed)
        partial[...] = dot(grad_qkv[...], row_normed[...], 0, 0)
        sent, kept = outs[1:]
        share = kept.shape[1]
        small = 2 * packed.shape[0]

        def split(candidate):
            for for_core, for_replica, at, start, size in units[candidate]:

                @pl.when(core == for_core)
                def keep():
                    kept[for_replica, at : at + size] = partial[start : start + size]

                @pl.when(core != for_core)
                def send():
                    place = small + for_replica * share + at
                    sent[place : place + size, : partial.shape[1]] = partial[start : start + size].astype(BF16)

        for_each_chip(chip, chips, split)
    width = row_tokens.shape[1]
    packed[...] = jnp.zeros(packed.shape, F32)
    gain_sum = jnp.zeros((1, width), F32)
    for at in range(chips):
        rows = pl.ds(at * block, block)
        incoming = dot(grad_qkv[rows, :], weight_mine[...], 1, 1)
        gain_sum += jnp.sum(
            incoming * (row_tokens[rows, :].astype(F32) * row_inverse[rows, :]), axis=0, keepdims=True
        )
    packed[0:1, :width] = gain_sum
    query_sum = jnp.sum(grad_qkv[:, :mine].astype(F32), axis=0, keepdims=True)
    value_sum = jnp.sum(grad_qkv[:, 2 * mine :].astype(F32), axis=0, keepdims=True)

    def place(candidate):
        size = min(mine, real - candidate * mine)
        if size > 0:
            packed[1:2, candidate * mine : candidate * mine + size] = query_sum[:, :size]
            packed[2:3, candidate * mine : candidate * mine + size] = value_sum[:, :size]

    for_each_chip(chip, chips, place)
    packed[3:6, :width] = sums[0:3, :]
    for at in range(up_sums.shape[1] // real):
        packed[6 + at : 7 + at, :real] = up_sums[:, at * real : (at + 1) * real]
    if units is not None:
        put_small(packed, sent)


def put_small(packed, sent):
    rows = packed.shape[0]
    high = packed[...].astype(BF16)
    sent[:rows] = high
    sent[rows : 2 * rows] = (packed[...] - high.astype(F32)).astype(BF16)


def take_small(got, rows):
    return got[:rows].astype(F32) + got[rows : 2 * rows].astype(F32)


def finish_tokens(heads, chips, real, bundled, *refs):
    pieces = refs[:chips]
    tokens, gain, grad_res, weight, kept, sent, projected = refs[chips : chips + 7]
    halves = refs[chips + 7 :]
    chip, core = position()
    mine = heads * HEAD_DIM

    def place(candidate):
        for source in range(chips):
            start = (candidate ^ source) * mine
            size = min(mine, real - start)
            for part in range(3):
                if size > 0 and bundled[source] is None:
                    projected[:, part * real + start : part * real + start + size] = pieces[source][
                        :, part * mine : part * mine + size
                    ]
                elif size > 0:
                    cols = slice(part * real + start, part * real + start + size)
                    count = projected.shape[0]
                    most, last = unpack_piece(pieces[source], bundled[source], count, 3 * mine)
                    projected[: count * 3 // 4, cols] = most[:, part * mine : (part + 1) * mine]
                    projected[count * 3 // 4 :, cols] = last[part]

    for_each_chip(chip, chips, place)
    values = tokens[...].astype(F32)
    inverse, totals = inverse_rms(values)
    incoming = dot(projected[...], weight[...], 1, 1)
    grad, unused = norm_back(values, gain[...].astype(F32).reshape(1, -1), inverse, totals, incoming)
    low = (grad + grad_res[...]).astype(BF16)
    length = kept.shape[0]
    either(core, kept, sent, low[:length], low[length:])


def shared(chips, bit, at):
    chip, unused = position()
    return ((chip >> bit) & 1) == ((at >> bit) & 1), (at >> (bit + 1) << bit) | (at & ((1 << bit) - 1))


def stream_sums(chips, dp, bit, cut, columns, left, left_other, right, right_other, sent, kept, rest):
    start, rows, right_start = columns
    share = rows // dp
    chip, unused = position()
    mine = (chip >> bit) & 1
    step = math.gcd(start, rows)

    def make(out, place, at, cols, kind):
        total = dot(left[:, cols], right[...], 0, 0) + dot(left_other[:, cols], right_other[:, right_start:], 0, 0)
        for part in range(dp):
            out[place, part] = total[part * share : part * share + cut].astype(kind)
            rest[at, part] = total[part * share + cut : (part + 1) * share]

    for out, stays, kind in ((sent, False, BF16), (kept, True, F32)):
        for place in range(chips // 2):
            side = mine if stays else 1 - mine
            low, high = place & ((1 << bit) - 1), place >> bit << (bit + 1)
            if step % 128 == 0:
                at = high | (side << bit) | low
                make(out, place, at, pl.ds(pl.multiple_of(start + at * rows, step), rows), kind)
                continue
            for value in range(2):
                at = high | (value << bit) | low
                cols = slice(start + at * rows, start + (at + 1) * rows)
                pl.when(side == value)(functools.partial(make, out, place, at, cols, kind))


def third_sums(chips, dp, share, columns, left, left_other, right, right_other, down_rest, up_rest, sent, kept, held):
    start, rows, unused = columns
    down_more = down_rest.shape[2]
    more = down_more + up_rest.shape[2]
    chip, unused = position()
    mine = lax.axis_index("dp") & 1
    total = dot(left[:, start : start + chips * rows], right[...], 0, 0) + dot(
        left_other[:, start : start + chips * rows], right_other[...], 0, 0
    )
    for source in range(chips):
        at = chip ^ source
        for part in range(dp):
            held[part] = total[source * rows + part * share : source * rows + (part + 1) * share]
        for place in range(dp // 2):
            for ref, part, kind in ((kept, 2 * place + mine, F32), (sent, 2 * place + 1 - mine, BF16)):
                ref[at, place, :down_more] = down_rest[at, part].astype(kind)
                ref[at, place, down_more:more] = up_rest[at, part].astype(kind)
                ref[at, place, more:] = held[part].astype(kind)


def fold(steps, *refs):
    count = len(steps)
    kepts, gots, sents, outs = (refs[at * count : (at + 1) * count] for at in range(4))
    for (axis, shift), kept, got, sent, out in zip(steps, kepts, gots, sents, outs):
        bit = (lax.axis_index(axis) >> shift) & 1
        for chip in range(out.shape[0]):
            for part in range(out.shape[1]):
                if axis == "seq":
                    mine, other = (2 * chip + bit, part), (2 * chip + 1 - bit, part)
                else:
                    mine, other = (chip, 2 * part + bit), (chip, 2 * part + 1 - bit)
                out[chip, part] = kept[mine] + got[mine].astype(F32)
                sent[chip, part] = (kept[other] + got[other].astype(F32)).astype(BF16)


def join_streams(step, *refs):
    kepts, gots, (sent, out) = refs[:3], refs[3:6], refs[6:]
    bit = (lax.axis_index(step[0]) >> step[1]) & 1
    start = 0
    for kept, got in zip(kepts, gots):
        size, width = kept.shape[2], kept.shape[3]
        rows = slice(start, start + size)
        start = rows.stop

        def total(part):
            if len(got.shape) == 4:
                return kept[0, part] + got[0, part].astype(F32)
            return kept[0, part] + got[pl.ds(pl.multiple_of(part * size, 8), size), :width].astype(F32)

        for part in range(out.shape[1]):
            out[0, part, rows] = total(2 * part + bit)
            sent[0, part, rows] = total(2 * part + 1 - bit).astype(BF16)


def fold_inward(step, kept, got, packed, sent, out, packed_out):
    bit = (lax.axis_index(step[0]) >> step[1]) & 1
    rows, share, width = packed.shape[0], kept.shape[1], kept.shape[2]
    packed_out[...] = packed[...] + take_small(got, rows)
    put_small(packed_out, sent)
    for at in range(out.shape[0]):
        left, right = (
            kept[part] + got[2 * rows + part * share : 2 * rows + (part + 1) * share, :width].astype(F32)
            for part in (at, out.shape[0] + at)
        )
        start = 2 * rows + at * share
        out[at] = jnp.where(bit == 0, left, right)
        sent[start : start + share, :width] = jnp.where(bit == 0, right, left).astype(BF16)


def pack_piece(piece, out, start):
    count, wide = piece.shape
    rows, part = count * 3 // 4, wide // 3
    out[start : start + rows, :wide] = piece[:rows]
    for at in range(3):
        place = slice(start + at * rows // 3, start + (at + 1) * rows // 3)
        out[place, wide:] = piece[rows:, at * part : (at + 1) * part]


def unpack_piece(got, start, count, wide):
    rows, part = count * 3 // 4, wide // 3
    last = [got[start + at * rows // 3 : start + (at + 1) * rows // 3, wide : wide + part] for at in range(3)]
    return got[start : start + rows, :wide], last


def bundled_first(steps, step, *refs):
    kepts, gots, (in_kept, in_got, packed), ways = refs[:3], refs[3:6], refs[6:9], refs[9:11]
    sents, outs, rest = refs[11:14], refs[14:17], refs[17:]
    width = kepts[0].shape[3]
    ends = []
    for (axis, shift), kept, got, sent, out in zip(steps, kepts, gots, sents, outs):
        bit = (lax.axis_index(axis) >> shift) & 1
        rows, start = kept.shape[2], 0
        for chip in range(out.shape[0]):
            for part in range(out.shape[1]):
                if axis == "seq":
                    mine, other = (2 * chip + bit, part), (2 * chip + 1 - bit, part)
                else:
                    mine, other = (chip, 2 * part + bit), (chip, 2 * part + 1 - bit)
                out[chip, part] = kept[mine] + got[mine].astype(F32)
                sent[start : start + rows, :width] = (kept[other] + got[other].astype(F32)).astype(BF16)
                start += rows
        ends.append(start)
    fold_inward(step, in_kept, in_got, packed, *rest)
    pack_piece(ways[0], sents[2], ends[2])
    pack_piece(ways[1], sents[0], ends[0])


def bundled_second(steps, step, *refs):
    kepts, gots, (in_kept, in_got, packed) = refs[:3], refs[3:6], refs[6:9]
    sents, outs, (in_out, packed_out) = refs[9:12], refs[12:15], refs[15:]
    width = kepts[0].shape[3]
    ends = []
    for (axis, shift), kept, got, sent, out in zip(steps, kepts, gots, sents, outs):
        bit = (lax.axis_index(axis) >> shift) & 1
        rows, parts, start = kept.shape[2], kept.shape[1], 0

        def total(chip, part):
            place = pl.multiple_of((chip * parts + part) * rows, 8)
            return kept[chip, part] + got[pl.ds(place, rows), :width].astype(F32)

        for chip in range(out.shape[0]):
            for part in range(out.shape[1]):
                if axis == "seq":
                    mine, other = (2 * chip + bit, part), (2 * chip + 1 - bit, part)
                else:
                    mine, other = (chip, 2 * part + bit), (chip, 2 * part + 1 - bit)
                out[chip, part] = total(*mine)
                sent[start : start + rows, :width] = total(*other).astype(BF16)
                start += rows
        ends.append(start)
    fold_inward(step, in_kept, in_got, packed, sents[0].at[ends[0] :], in_out, packed_out)


def last_inward(start, kept, message, packed, way, share, low, packed_out, far):
    rows, count, width = packed.shape[0], share.shape[0], share.shape[1]
    got = message.at[start:]
    total = kept[0] + got[2 * rows : 2 * rows + count, :width].astype(F32)
    share[...] = total
    low[2 * rows :, :width] = total.astype(BF16)
    packed_out[...] = packed[...] + take_small(got, rows)
    put_small(packed_out, low)
    pack_piece(way, far, 0)
    put_small(packed_out, far.at[way.shape[0] * 3 // 4 :])


def last_wide(a_cut, b_cut, kept, got, down, up, outward):
    share = down.shape[0]

    def total(start, size):
        rows = slice(start, start + size)
        return kept[0, 0, rows] + got[0, 0, rows].astype(F32)

    down[:a_cut] = total(0, a_cut)
    up[:b_cut] = total(a_cut, b_cut)
    down[a_cut:] = total(a_cut + b_cut, share - a_cut)
    up[b_cut:] = total(b_cut + share, share - b_cut)
    outward[...] = total(2 * share, outward.shape[0])


def place_inward(dp, size, real, table, share, packed, *refs):
    gots, far, out, outs, held = refs[:2], refs[2], refs[3], refs[4:-1], refs[-1]
    count, small = share.shape[0] // size, packed.shape[0]
    width = share.shape[1]
    sums = packed[...] + take_small(far.at[far.shape[0] - 2 * small :], small)
    for unit in range(count):
        held[0, unit] = share[unit * size : (unit + 1) * size]
        for at, piece in enumerate(gots):
            start = 2 * small + unit * size
            held[at + 1, unit] = piece[start : start + size, :width].astype(F32)
    for piece in gots:
        sums = sums + take_small(piece, small)
    put_sums(real, sums, *outs)
    device = lax.axis_index("seq") * dp + lax.axis_index("dp")
    for unit in range(count):
        place = 2 * (device * count + unit)
        out[unit * size : (unit + 1) * size] = held[table[place], table[place + 1]]


def put_sums(real, sums, gain_first, bias_in, bias_out, gain_second, bias_up, bias_down):
    width = gain_first.shape[0]
    gain_first[...] = sums[0:1, :width].reshape(width)
    bias_in[...] = sums[1:3, :real]
    bias_out[...] = sums[3:4, :width].reshape(width)
    gain_second[...] = sums[4:5, :width].reshape(width)
    bias_down[...] = sums[5:6, :width].reshape(width)
    for at in range(bias_up.shape[0] // real):
        bias_up[at * real : (at + 1) * real] = sums[6 + at : 7 + at, :real].reshape(real)


def last_small(real, packed, *outs):
    put_sums(real, packed[...], *outs)


def inward_units(chips, dp, real, mine):
    share = 3 * real // (2 * chips * dp)
    size = math.gcd(share, mine)
    count = share // size
    if chips != 4 or dp != 4 or chips * mine != real or size % 8:
        return None
    units, table = [], np.zeros((2 * chips * dp, count, 2), np.int32)
    for chip in range(chips):
        filled, own = {}, []
        for part in range(3):
            for at in range(mine // size):
                unit = (part * real + chip * mine) // size + at
                holder, place = unit // count, unit % count
                slot = ((holder // dp) & 1, holder % dp)
                here = filled.get(slot, 0)
                filled[slot] = here + 1
                own.append((*slot, here * size, part * mine + at * size, size))
                table[holder, place] = (holder // dp // 2) ^ chip, here
        if len(filled) != 2 * dp or set(filled.values()) != {count}:
            return None
        units.append(own)
    if table[:, :, 0].max() > 2:
        return None
    return size, units, table.reshape(-1)


def flip(value, mask, axis="seq"):
    return lax.ppermute(value, axis, [(at, at ^ mask) for at in range(lax.axis_size(axis))])


def bits_of(size):
    return [1 << at for at in range(size.bit_length() - 1)]


def local(
    tokens, doc_lengths, first_gain, inward_weight, inward_bias, outward_weight, outward_bias,
    second_gain, up_weight, up_bias, down_weight, down_bias, cotangent,
):
    rows, local_len, width = tokens.shape
    seq, dp = lax.axis_size("seq"), lax.axis_size("dp")
    chips = seq // 2
    block = rows * local_len
    length = seq * local_len
    real = HEADS * HEAD_DIM
    heads = -(-HEADS // chips)
    mine = heads * HEAD_DIM
    slots = chips * mine
    ff = up_weight.shape[1]
    chip_bits, dp_bits = bits_of(chips), bits_of(dp)

    def shape(*dims, kind=BF16):
        return jax.ShapeDtypeStruct(dims, kind)

    def call(kernel, name, outs, args, scratch=(), flops=1, mib=16, specs=None):
        return pl.pallas_call(
            kernel,
            out_shape=outs,
            in_specs=specs or [VMEM] * len(args),
            out_specs=jax.tree.map(lambda unused: VMEM, outs),
            scratch_shapes=scratch,
            compiler_params=pltpu.CompilerParams(vmem_limit_bytes=mib * 1024 * 1024),
            cost_estimate=pl.CostEstimate(flops=flops, bytes_accessed=1, transcendentals=0),
            name=name,
        )(*args)

    def after(value, earlier):
        return hold((value, earlier))[0]

    half_rows = (shape(local_len, width),) * 2

    def to_rows(value, name):
        kept, sent = call(split_rows, name, half_rows, (jnp.transpose(value, (2, 0, 1)),), mib=8)
        return kept, flip(sent, 1)

    def from_rows(kept, sent, name, parts=1):
        size = local_len // parts
        gots = [flip(sent[at * size : (at + 1) * size], 1) for at in range(parts)]
        out = call(join_rows, name, shape(width, rows, local_len), (kept, *gots), mib=8)
        return jnp.transpose(out, (1, 2, 0))

    def exchange(pieces):
        return [pieces[0]] + [flip(pieces[at], 2 * at) for at in range(1, chips)]

    kept, got = to_rows(tokens, "split_tokens")
    weight_mine = call(
        functools.partial(pick_weights, heads, chips, real), "pick_weights", shape(width, 3 * mine),
        (after(inward_weight, kept),),
    )
    places, pieces = [(0, 1), (0, 0)], [kept, got]
    if chips == 4:
        kept_one, kept_two = flip(kept, 2), flip(kept, 4)
        got_late = after(got, weight_mine)
        got_one, got_two = flip(got_late, 2), flip(got_late, 4)
        places += [(1, 1), (2, 1), (1, 0), (2, 0), (3, 1), (3, 0)]
        pieces += [kept_one, kept_two, got_one, got_two]
    else:
        for which, value in ((1, kept), (0, got)):
            held = value[None]
            for bit in chip_bits:
                held = jnp.concatenate([held, flip(held, 2 * bit)], axis=0)
            places += [(at, which) for at in range(1, chips)]
            pieces += [held[at] for at in range(1, chips)]
    projected = [shape(local_len, width), shape(local_len, 1, kind=F32), shape(local_len, 3 * mine)]
    bias_mine, scale, starts, normed_one, row_tokens, *parts = call(
        functools.partial(project_first, heads, chips, real), "project_first",
        [shape(1, 3 * mine, kind=F32), shape(1, width, kind=F32), shape(length, 1, kind=jnp.int32)]
        + [shape(block, width)] * 2 + projected * 2,
        (doc_lengths, kept, got, first_gain, inward_bias, weight_mine),
        flops=2 * block * width * 3 * mine, specs=[SMEM] + [VMEM] * 5,
    )
    if chips == 4:
        pieces.append(flip(after(kept_one, (kept_two, row_tokens)), 4))
        pieces.append(flip(after(got_two, row_tokens), 2))
    cot_kept, cot_got = to_rows(after(cotangent, pieces[3]), "split_cotangent")
    fresh = 2
    middle = pieces[2:-fresh]
    parts += call(
        functools.partial(project_more, len(middle)), "project_more", projected * len(middle),
        (*middle, weight_mine, bias_mine, scale), flops=block * len(middle) * width * 3 * mine,
    )
    row_cot, grad_active = call(
        active_cotangent, "active_cotangent", (shape(block, width), shape(block, ff, kind=F32)),
        (cot_kept, cot_got, down_weight), mib=16,
    )

    outward_pad = outward_weight
    if slots != real:
        outward_pad = jnp.pad(outward_weight, ((0, slots - real), (0, 0)))

    forward = call(
        functools.partial(attention_forward, heads, chips, block, places, fresh), "attention_forward",
        [shape(length, 3 * mine), shape(length, mine, kind=F32), shape(length, 8, kind=F32)]
        + [shape(block, mine)] * chips + projected * fresh,
        (*parts[2::3], *pieces[-fresh:], weight_mine, bias_mine, scale, starts),
        flops=8 * length * length * mine, mib=8 + length // 128,
    )
    qkv, attended, logs = forward[:3]
    parts += forward[3 + chips :]
    attended_in = exchange(forward[3 : 3 + chips])
    row_cot, grad_active = call(
        active_cotangent, "active_cotangent", (shape(block, width), shape(block, ff, kind=F32)),
        (after(cot_kept, forward[3]), cot_got, down_weight), flops=2 * block * width * ff,
    )

    cot_other = flip(row_cot, 1)
    residual, normed_two, active, grad_up, up_sums, kept, sent = call(
        functools.partial(up_branch, heads, chips, real), "up_branch",
        (
            shape(block, width, kind=F32), shape(block, width), shape(block, ff), shape(block, ff),
            shape(1, ff, kind=F32), shape(block, ff + slots // 2), shape(block, ff + slots // 2 + width),
        ),
        (
            *attended_in, row_tokens, grad_active, outward_pad, outward_bias, second_gain,
            up_weight, up_bias,
        ),
        flops=2 * block * width * ff, mib=23,
    )
    other = flip(sent, 1)
    back = call(
        functools.partial(back_branch, heads, chips, real), "back_branch",
        (shape(block, mine),) * chips
        + (shape(block, width, kind=F32), shape(block, width), shape(8, width, kind=F32)),
        (residual, row_cot, grad_up, up_weight, outward_pad, second_gain),
        flops=2 * block * width * ff, mib=16,
    )
    grad_res, grad_low, sums = back[chips:]
    low_other = flip(grad_low, 1)
    grad_in = exchange(back[:chips])

    share, out_share, in_share = ff // (seq * dp), real // (seq * dp), 3 * real // (seq * dp)
    a_cut, b_cut = share - share // 4, share - share // 4
    third = 2 * share - a_cut - b_cut + out_share
    x_bit, y_bit = 0, len(chip_bits) - 1

    def stream(name, bit, cut, columns, args):
        dims = (chips // 2, dp, cut, width)
        return call(
            functools.partial(stream_sums, chips, dp, bit, cut, columns), name,
            [shape(*dims), shape(*dims, kind=F32), shape(chips, dp, share - cut, width, kind=F32)], args,
            mib=18,
        )

    a_sent, a_kept, down_rest = stream(
        "down_sums", x_bit, a_cut, (0, ff // seq, 0), (kept, other, row_cot, cot_other)
    )
    b_sent, b_kept, up_rest = stream(
        "up_sums", y_bit, b_cut, (ff // 2, ff // seq, ff + slots // 2), (after(kept, a_sent), other, normed_two, other)
    )
    c_dims = (chips, dp // 2, third, width)
    c_sent, c_kept = call(
        functools.partial(third_sums, chips, dp, out_share, (ff, mine // 2, 0)), "out_sums",
        [shape(*c_dims), shape(*c_dims, kind=F32)],
        (after(kept, (b_sent, *grad_in[1:-1])), other, grad_low, low_other, down_rest, up_rest),
        scratch=[pltpu.VMEM((dp, out_share, width), F32)], mib=18,
    )
    a_got, b_got, c_got = flip(a_sent, 2 << x_bit), flip(b_sent, 2 << y_bit), flip(c_sent, 1, "dp")

    grad_in[0] = after(grad_in[0], c_sent)
    *grad_qkv, grad_all = call(
        functools.partial(attention_backward, heads, chips, block), "attention_backward",
        [shape(block, 3 * mine)] * chips + [shape(length, 3 * mine)],
        (starts, qkv, attended, logs, *grad_in),
        scratch=[
            pltpu.VMEM((length, mine), BF16), pltpu.VMEM((length, HEAD_DIM), F32),
            pltpu.VMEM((length, HEAD_DIM), F32),
        ],
        flops=200 * length * length * mine, mib=8 + length // 128,
    )
    plan = inward_units(chips, dp, real, mine)
    small_rows = -(-(6 + ff // real) // 16) * 16
    packed_shape = shape(small_rows, real, kind=F32)
    row_outs = [packed_shape]
    if plan is not None:
        row_outs += [shape(2 * small_rows + dp * in_share, real), shape(dp, in_share, width, kind=F32)]
    packed, *inward = call(
        functools.partial(row_sums, heads, chips, block, places, real, plan and plan[1]), "row_sums", row_outs,
        (grad_all, weight_mine, sums, up_sums, *pieces, *parts[0::3], *parts[1::3]),
        scratch=[
            pltpu.VMEM((length, width), BF16), pltpu.VMEM((length, width), BF16),
            pltpu.VMEM((length, 1), F32), pltpu.VMEM((3 * mine, width), F32),
        ],
        flops=12 * length * mine * width, mib=8 + length // 128 + 2,
    )

    def hop(value, step):
        return flip(value, 1 << step[1], step[0])

    chip_steps = [("seq", 1 + at) for at in range(len(chip_bits))]
    dp_steps = [("dp", at) for at in range(len(dp_bits))]
    rounds = list(zip(
        [step for step in chip_steps if step[1] != 1 + x_bit] + dp_steps[:1],
        dp_steps[:1] + [step for step in chip_steps if step[1] != 1 + y_bit],
        chip_steps,
    ))
    kepts, gots = [a_kept, b_kept, c_kept], [a_got, b_got, c_got]
    earlier = packed
    if plan is not None:
        in_sent, in_kept = inward
        in_got, small = flip(in_sent, 1), packed

    def half_dims(at):
        dims = [list(kept.shape) for kept in kepts]
        for dim, step in zip(dims, rounds[at]):
            dim[step[0] == "dp"] //= 2
        return dims

    sums_shapes = [shape(width, kind=F32), shape(2, real, kind=F32), shape(width, kind=F32)]
    sums_shapes += [shape(width, kind=F32), shape(ff, kind=F32), shape(width, kind=F32)]
    out_kept, out_sent = call(
        finish_output, "finish_output", half_rows, (residual, after(active, earlier), down_weight, down_bias),
    )
    output_tokens = from_rows(out_kept, out_sent, "join_output")
    bundled = [None] * chips
    if plan is not None:
        half = (in_kept.shape[0] // 2,) + in_kept.shape[1:]
        dims = half_dims(0)
        counts = [math.prod(dim[:3]) for dim in dims]
        more = [block * 3 // 4, 0, block * 3 // 4]
        outs = call(
            functools.partial(bundled_first, rounds[0], dp_steps[1]), "round_0",
            [shape(count + rest, real) for count, rest in zip(counts, more)]
            + [shape(*dim, kind=F32) for dim in dims]
            + [shape(2 * small_rows + half[0] * in_share, real), shape(*half, kind=F32), packed_shape],
            (after(kepts[0], out_sent), *kepts[1:], *gots, in_kept, in_got, small, grad_qkv[1], grad_qkv[2]),
        )
        gots = [hop(sent, step) for sent, step in zip(outs[:3], rounds[0])]
        kepts, in_got, in_kept, small = outs[3:6], hop(outs[6], dp_steps[1]), outs[7], outs[8]
        queries_in, bundled = [grad_qkv[0], gots[2], gots[0]], [None, counts[2], counts[0], 0]
        half = (half[0] // 2,) + half[1:]
        dims = half_dims(1)
        counts = [math.prod(dim[:3]) for dim in dims]
        more = [2 * small_rows + half[0] * in_share, 0, 0]
        outs = call(
            functools.partial(bundled_second, rounds[1], dp_steps[0]), "round_1",
            [shape(count + rest, real) for count, rest in zip(counts, more)]
            + [shape(*dim, kind=F32) for dim in dims] + [shape(*half, kind=F32), packed_shape],
            (after(kepts[0], output_tokens), *kepts[1:], *gots, in_kept, in_got, small),
        )
        gots = [hop(sent, step) for sent, step in zip(outs[:3], rounds[1])]
        kepts, in_kept, small = outs[3:6], outs[6], outs[7]
        earlier = outs[0]
    else:
        for at in range(len(rounds)):
            dims = half_dims(at)
            outs = call(
                functools.partial(fold, rounds[at]), f"round_{at}",
                [shape(*dim) for dim in dims] + [shape(*dim, kind=F32) for dim in dims], (*kepts, *gots),
            )
            kepts, gots = outs[3:], [hop(sent, step) for sent, step in zip(outs[:3], rounds[at])]
        queries_in = exchange(grad_qkv)
    if plan is not None:
        share_sum, low, small, far = call(
            functools.partial(last_inward, counts[0]), "last_inward",
            [
                shape(in_share, width, kind=F32), shape(2 * small_rows + in_share, real), packed_shape,
                shape(block * 3 // 4 + 2 * small_rows, real),
            ],
            (after(in_kept, earlier), gots[0], small, grad_qkv[3]),
        )
        earlier = low
    dims = (1, kepts[0].shape[1] // 2, a_cut + b_cut + third, width)
    sent, kept = call(
        functools.partial(join_streams, dp_steps[1]), "join_streams", [shape(*dims), shape(*dims, kind=F32)],
        (after(kepts[0], earlier), *kepts[1:], *gots),
    )
    got = hop(sent, dp_steps[1])
    earlier = sent
    for step in dp_steps[2:]:
        dims = (1, kept.shape[1] // 2) + kept.shape[2:]
        sent, kept = call(
            functools.partial(fold, (step,)), "fold_joined", [shape(*dims), shape(*dims, kind=F32)], (kept, got)
        )
        got = hop(sent, step)
    if plan is not None:
        low = after(low, sent)
        queries_in.append(flip(after(far, sent), 6))
        in_pieces = [share_sum, small, flip(low, 2), flip(low, 4), queries_in[3]]

    extra = [] if plan is not None else [shape(block, 3 * real)]
    rows_kept, rows_sent, *flat = call(
        functools.partial(finish_tokens, heads, chips, real, bundled), "finish_tokens", list(half_rows) + extra,
        (*queries_in, after(row_tokens, earlier), first_gain, grad_res, inward_weight),
        scratch=[] if extra else [pltpu.VMEM((block, 3 * real), BF16)],
        mib=16,
    )
    if plan is not None:
        size, unused, table = plan
        in_out, *sums_out = call(
            functools.partial(place_inward, dp, size, real), "place_inward",
            [shape(in_share, width, kind=F32)] + sums_shapes, (jnp.asarray(table), in_pieces[0], *in_pieces[1:]),
            scratch=[pltpu.VMEM((3, in_share // size, size, width), F32)],
            specs=[SMEM] + [VMEM] * (chips + 1),
        )
    else:
        in_out = lax.psum_scatter(dot(flat[0], normed_one, 0, 0), ("seq", "dp"), scatter_dimension=0, tiled=True)
        for step in [("seq", 0)] + chip_steps + dp_steps:
            packed = packed + hop(packed, step)
        sums_out = call(functools.partial(last_small, real), "last_small", sums_shapes, (packed,))
    grad_tokens = from_rows(after(rows_kept, in_out), rows_sent, "join_tokens", 2)
    down_share, up_share, out_out = call(
        functools.partial(last_wide, a_cut, b_cut), "last_wide",
        [shape(share, width, kind=F32), shape(share, width, kind=F32), shape(out_share, width, kind=F32)],
        (after(kept, grad_tokens), got),
    )

    gain_first, bias_in, bias_out, gain_second, bias_up, bias_down = sums_out
    return (
        output_tokens, grad_tokens, gain_first, in_out.T, bias_in, out_out, bias_out, gain_second,
        up_share.T, bias_up, down_share, bias_down,
    )


def solution(mesh):
    return jax.shard_map(
        local,
        mesh=mesh,
        in_specs=(P("dp", "seq", None), P("dp", None)) + (P(),) * 10 + (P("dp", "seq", None),),
        out_specs=(
            P("dp", "seq", None),
            P("dp", "seq", None),
            P(),
            P(None, ("seq", "dp")),
            P(),
            P(("seq", "dp"), None),
            P(),
            P(),
            P(None, ("seq", "dp")),
            P(),
            P(("seq", "dp"), None),
            P(),
        ),
        check_vma=False,
    )
```

```python
import functools
import math

import jax
import jax.numpy as jnp
import numpy as np
from jax import lax
from jax.experimental import pallas as pl
from jax.experimental.pallas import tpu as pltpu
from jax.sharding import PartitionSpec as P

HEADS = 12
HEAD_DIM = 64
EPSILON = 1e-05
FLOOR = -1e30
SCALE = HEAD_DIM**-0.5
QB = 256
F32 = jnp.float32
BF16 = jnp.bfloat16
VMEM = pl.BlockSpec(memory_space=pltpu.VMEM)
SMEM = pl.BlockSpec(memory_space=pltpu.SMEM)
hold = lax.optimization_barrier

def inverse_rms(values):
    squares = jnp.sum(values * values, axis=-1, keepdims=True)
    totals = jnp.sum(values, axis=-1, keepdims=True)
    return lax.rsqrt((squares + totals * totals) / (values.shape[-1] + 1) + EPSILON), totals


def norm_back(values, gain, inverse, totals, incoming):
    weighted = incoming * gain
    dots = jnp.sum(weighted * values, axis=-1, keepdims=True)
    factor = inverse * inverse * inverse * dots / (values.shape[-1] + 1)
    grad = inverse * weighted - factor * (values + totals)
    return grad, jnp.sum(incoming * values * inverse, axis=0, keepdims=True)


def dot(left, right, left_dim, right_dim):
    return lax.dot_general(
        left, right, (((left_dim,), (right_dim,)), ((), ())), preferred_element_type=F32
    )


def gelu_both(value):
    linear = 0.7978845608028654 * value
    cubic = linear * (0.044715 * (value * value))
    curve = jnp.tanh(linear + cubic)
    half = 0.5 + 0.5 * curve
    slope = half * (1.0 + (linear + 3.0 * cubic) * (1.0 - curve))
    return value * half, slope


def at_block(index, block):
    return pl.ds(pl.multiple_of(index * block, block), block)


def position():
    me = lax.axis_index("seq")
    return me >> 1, me & 1


def either(flag, first, second, left, right):
    @pl.when(flag == 0)
    def straight():
        first[...] = left
        second[...] = right

    @pl.when(flag != 0)
    def crossed():
        first[...] = right
        second[...] = left


def for_each_chip(chip, chips, body):
    for candidate in range(chips):
        pl.when(chip == candidate)(functools.partial(body, candidate))


def allowed_block(starts, query_start, keys):
    query_pos = query_start + lax.broadcasted_iota(jnp.int32, (QB, 1), 0)
    key_pos = lax.broadcasted_iota(jnp.int32, (1, keys), 1)
    return (key_pos <= query_pos) & (key_pos >= starts)


def split_rows(value, kept, sent):
    unused, core = position()
    length = value.shape[2]
    turned = value[...].reshape(value.shape[0], 2 * length).T
    either(core, kept, sent, turned[:length], turned[length:])


def join_rows(kept, *refs):
    gots, out = refs[:-1], refs[-1]
    unused, core = position()
    mine, other = [kept[...]], [got[...] for got in gots]

    def store(parts):
        out[...] = jnp.concatenate(parts, axis=0).T.reshape(out.shape)

    pl.when(core == 0)(lambda: store(mine + other))
    pl.when(core != 0)(lambda: store(other + mine))


def project(piece, scale, weight, bias, normed, inverse, qkv):
    values = piece[...].astype(F32)
    factor, unused = inverse_rms(values)
    low = (values * scale[...] * factor).astype(BF16)
    normed[...] = low
    inverse[...] = factor
    qkv[...] = (dot(low, weight[...], 1, 0) + bias[...]).astype(BF16)


def pick_weights(heads, chips, real, weight, weight_mine):
    width = heads * HEAD_DIM
    chip, unused = position()

    def choose(candidate):
        size = max(min(width, real - candidate * width), 0)
        for part in range(3):
            at, start = part * width, part * real + candidate * width
            if size > 0:
                weight_mine[:, at : at + size] = weight[:, start : start + size]
            if size < width:
                weight_mine[:, at + size : at + width] = jnp.zeros((weight.shape[0], width - size), BF16)

    for_each_chip(chip, chips, choose)


def project_first(heads, chips, real, docs, kept, got, gain, bias, weight, *refs):
    bias_mine, scale, starts, normed_own, own = refs[:5]
    width = heads * HEAD_DIM
    chip, core = position()

    def choose(candidate):
        size = max(min(width, real - candidate * width), 0)
        for part in (0, 2):
            if size > 0:
                bias_mine[:, part * width : part * width + size] = bias[
                    part // 2 : part // 2 + 1, candidate * width : candidate * width + size
                ].astype(F32)

    bias_mine[...] = jnp.zeros(bias_mine.shape, F32)
    for_each_chip(chip, chips, choose)
    scale[...] = gain[...].astype(F32).reshape(1, -1)
    places = lax.broadcasted_iota(jnp.int32, starts.shape, 0)
    start, end = jnp.zeros_like(places), jnp.int32(0)
    for at in range(3):
        end = end + docs[core, at]
        start = jnp.where(places >= end, end, start)
    starts[...] = start
    rows = kept.shape[0]
    for at, (piece, half) in enumerate(((kept, core), (got, 1 - core))):
        normed, inverse, qkv = refs[5 + 3 * at : 8 + 3 * at]
        project(piece, scale, weight, bias_mine, normed, inverse, qkv)
        normed_own[at_block(half, rows), :] = normed[...]
        own[at_block(half, rows), :] = piece[...]


def project_more(count, *refs):
    pieces, (weight, bias, scale), outs = refs[:count], refs[count : count + 3], refs[count + 3 :]
    for at, piece in enumerate(pieces):
        project(piece, scale, weight, bias, *outs[3 * at : 3 * at + 3])


def attention_forward(heads, chips, block, places, fresh, *refs):
    count = len(places)
    done, pieces = refs[: count - fresh], refs[count - fresh : count]
    (weight, bias, scale, starts), outs = refs[count : count + 4], refs[count + 4 :]
    qkv, attended, logs = outs[:3]
    sends, parts = outs[3 : 3 + chips], outs[3 + chips :]
    width = heads * HEAD_DIM
    chip, core = position()
    for at, (source, mine) in enumerate(places):
        part = done[at] if at < count - fresh else parts[3 * (at - count + fresh) + 2]
        if at >= count - fresh:
            at_parts = 3 * (at - count + fresh)
            project(pieces[at - count + fresh], scale, weight, bias, *parts[at_parts : at_parts + 3])
        rows = part.shape[0]
        half = core if mine else 1 - core
        start = pl.multiple_of((chip ^ source) * block + half * rows, rows)
        qkv[pl.ds(start, rows), :] = part[...]
    for at_query in range(chips * block // QB):
        rows = pl.ds(at_query * QB, QB)
        keys = (at_query + 1) * QB
        allowed = allowed_block(starts[rows, :], at_query * QB, keys)
        for head in range(heads):
            at = head * HEAD_DIM
            query = qkv[rows, at : at + HEAD_DIM] * BF16(SCALE)
            key = qkv[:keys, width + at : width + at + HEAD_DIM]
            value = qkv[:keys, 2 * width + at : 2 * width + at + HEAD_DIM]
            scores = jnp.where(allowed, dot(query, key, 1, 1), FLOOR)
            top = jnp.max(scores, axis=-1, keepdims=True)
            weights = jnp.exp(scores - top)
            total = jnp.sum(weights, axis=-1, keepdims=True)
            attended[rows, at : at + HEAD_DIM] = dot(weights.astype(BF16), value, 1, 0) / total
            logs[rows, head : head + 1] = top + jnp.log(total)
    for source in range(chips):
        sends[source][...] = attended[at_block(chip ^ source, block), :].astype(BF16)


def attention_backward(heads, chips, block, starts, qkv, attended, logs, *refs):
    grads, sends = refs[:chips], refs[chips : 2 * chips]
    out, grad_row, key_grad, value_grad = refs[2 * chips :]
    width = heads * HEAD_DIM
    chip, core = position()
    for source in range(chips):
        grad_row[at_block(chip ^ source, block), :] = grads[source][...]
    blocks = chips * block // QB
    for head in range(heads):
        at = head * HEAD_DIM
        turned_query = (qkv[:, at : at + HEAD_DIM] * BF16(SCALE)).T
        turned_grad = grad_row[:, at : at + HEAD_DIM].T
        for at_query in reversed(range(blocks)):
            lanes = slice(at_query * QB, (at_query + 1) * QB)
            rows = pl.ds(at_query * QB, QB)
            keys = (at_query + 1) * QB
            allowed = allowed_block(starts[rows, :], at_query * QB, keys)
            query = qkv[rows, at : at + HEAD_DIM] * BF16(SCALE)
            key = qkv[:keys, width + at : width + at + HEAD_DIM]
            value = qkv[:keys, 2 * width + at : 2 * width + at + HEAD_DIM]
            grad = grad_row[rows, at : at + HEAD_DIM]
            delta = jnp.sum(
                grad.astype(F32) * attended[rows, at : at + HEAD_DIM], axis=-1, keepdims=True
            )
            scores = dot(query, key, 1, 1)
            weights = jnp.where(allowed, jnp.exp(scores - logs[rows, head : head + 1]), 0.0)
            grad_weights = dot(grad, value, 1, 1)
            grad_scores = (weights * (grad_weights - delta)).astype(BF16)
            out[rows, at : at + HEAD_DIM] = (dot(grad_scores, key, 1, 0) * SCALE).astype(BF16)
            key_part = dot(turned_query[:, lanes], grad_scores, 1, 0)
            value_part = dot(turned_grad[:, lanes], weights.astype(BF16), 1, 0)
            if at_query == blocks - 1:
                key_grad[...] = key_part
                value_grad[...] = value_part
            else:
                key_grad[:, :keys] += key_part
                value_grad[:, :keys] += value_part
        out[:, width + at : width + at + HEAD_DIM] = key_grad[...].astype(BF16).T
        out[:, 2 * width + at : 2 * width + at + HEAD_DIM] = value_grad[...].astype(BF16).T
    for source in range(chips):
        sends[source][...] = out[at_block(chip ^ source, block), :]


def active_cotangent(kept, got, weight, row, out):
    unused, core = position()
    length = kept.shape[0]
    row[at_block(core, length), :] = kept[...]
    row[at_block(1 - core, length), :] = got[...]
    out[...] = dot(row[...], weight[...], 1, 1)


def up_branch(heads, chips, real, *refs):
    pieces = refs[:chips][::-1]
    tokens, grad_active, out_weight, out_bias, gain, up_weight, up_bias = refs[chips : chips + 7]
    residual, normed, active, grad_up, kept, sent = refs[chips + 7 :]
    chip, core = position()
    mine = heads * HEAD_DIM
    ff = up_weight.shape[1]

    values = tokens[...].astype(F32) + out_bias[...].astype(F32).reshape(1, -1)
    for source, piece in enumerate(pieces):
        values = values + dot(piece[...], out_weight[at_block(chip ^ source, mine), :], 1, 0)
    residual[...] = values
    inverse, unused = inverse_rms(values)
    low = (values * gain[...].astype(F32).reshape(1, -1) * inverse).astype(BF16)
    normed[...] = low
    sent[:, ff + mine * chips // 2 :] = low

    def share(start, size, at, left, right):
        place = slice(start + at * size, start + (at + 1) * size)
        kept[:, place] = jnp.where(core == 0, left, right)
        sent[:, place] = jnp.where(core == 0, right, left)

    for source, piece in enumerate(pieces):
        share(ff, mine // 2, source, piece[:, : mine // 2], piece[:, mine // 2 :])
    tile = ff // chips
    piece = tile // 2
    for at in range(chips):
        cols = slice(at * tile, (at + 1) * tile)
        upward = dot(normed[...], up_weight[:, cols], 1, 0) + up_bias[cols].astype(F32).reshape(1, -1)
        act, slope = gelu_both(upward)
        low = act.astype(BF16)
        active[:, cols] = low
        share(0, piece, at, low[:, :piece], low[:, piece:])
        back = (grad_active[:, cols] * slope).astype(BF16)
        grad_up[:, cols] = back
        share(ff // 2, piece, at, back[:, :piece], back[:, piece:])


def back_branch(heads, chips, real, residual, cotangent, grad_up, up_weight, out_weight, gain, *refs):
    sends = refs[:chips]
    grad_res, grad_low, gain_grad = refs[chips:]
    chip, unused = position()
    mine = heads * HEAD_DIM
    values = residual[...]
    inverse, totals = inverse_rms(values)
    incoming = dot(grad_up[...], up_weight[...], 1, 1)
    grad, gain_sum = norm_back(values, gain[...].astype(F32).reshape(1, -1), inverse, totals, incoming)
    cot = cotangent[...].astype(F32)
    grad = grad + cot
    grad_res[...] = grad
    low = grad.astype(BF16)
    grad_low[...] = low
    gain_grad[...] = gain_sum
    for source in range(chips):
        sends[source][...] = dot(low, out_weight[at_block(chip ^ source, mine), :], 1, 1).astype(BF16)


def finish_output(residual, active, weight, bias, kept, sent):
    unused, core = position()
    values = residual[...] + dot(active[...], weight[...], 1, 0) + bias[...].astype(F32).reshape(1, -1)
    low = values.astype(BF16)
    length = kept.shape[0]
    either(core, kept, sent, low[:length], low[length:])


def row_pieces(chips, block, places, pieces, out):
    chip, core = position()
    for (source, mine), piece in zip(places, pieces):
        rows = piece.shape[0]
        half = core if mine else 1 - core
        out[pl.ds(pl.multiple_of((chip ^ source) * block + half * rows, rows), rows), :] = piece[...]


def whole_rows(chips, block, places, *refs):
    count = len(places)
    tokens, normed, inverse = refs[:count], refs[count : 2 * count], refs[2 * count : 3 * count]
    row_normed, row_scaled = refs[3 * count :]
    row_pieces(chips, block, places, normed, row_normed)
    chip, core = position()
    for (source, mine), piece, factor in zip(places, tokens, inverse):
        rows = piece.shape[0]
        half = core if mine else 1 - core
        start = pl.multiple_of((chip ^ source) * block + half * rows, rows)
        row_scaled[pl.ds(start, rows), :] = piece[...].astype(F32) * factor[...]


def row_sums(heads, chips, block, real, units, grad_qkv, weight_mine, gain_grad, low, cotangent, grad_up, *refs):
    (row_normed, row_scaled), outs, partial = refs[:2], refs[2:-1], refs[-1]
    packed = outs[0]
    chip, core = position()
    mine = heads * HEAD_DIM
    if units is not None:
        partial[...] = dot(grad_qkv[...], row_normed[...], 0, 0)
        sent, kept = outs[1:]
        share = kept.shape[1]

        def split(candidate):
            for for_core, for_replica, at, start, size in units[candidate]:

                @pl.when(core == for_core)
                def keep():
                    kept[for_replica, at : at + size] = partial[start : start + size]

                @pl.when(core != for_core)
                def send():
                    place = for_replica * share + at
                    sent[place : place + size, : partial.shape[1]] = partial[start : start + size].astype(BF16)

        for_each_chip(chip, chips, split)
    width = row_scaled.shape[1]
    packed[...] = jnp.zeros(packed.shape, F32)
    gain_sum = jnp.zeros((1, width), F32)
    for at in range(chips):
        rows = pl.ds(at * block, block)
        incoming = dot(grad_qkv[rows, :], weight_mine[...], 1, 1)
        gain_sum += jnp.sum(
            incoming * row_scaled[rows, :], axis=0, keepdims=True
        )
    packed[0:1, :width] = gain_sum
    query_sum = jnp.sum(grad_qkv[:, :mine].astype(F32), axis=0, keepdims=True)
    value_sum = jnp.sum(grad_qkv[:, 2 * mine :].astype(F32), axis=0, keepdims=True)

    def place(candidate):
        size = min(mine, real - candidate * mine)
        if size > 0:
            packed[1:2, candidate * mine : candidate * mine + size] = query_sum[:, :size]
            packed[2:3, candidate * mine : candidate * mine + size] = value_sum[:, :size]

    for_each_chip(chip, chips, place)
    packed[3:4, :width] = jnp.sum(low[...].astype(F32), axis=0, keepdims=True)
    packed[4:5, :width] = gain_grad[...]
    packed[5:6, :width] = jnp.sum(cotangent[...].astype(F32), axis=0, keepdims=True)
    for at in range(grad_up.shape[1] // real):
        part = grad_up[:, at * real : (at + 1) * real].astype(F32)
        packed[6 + at : 7 + at, :real] = jnp.sum(part, axis=0, keepdims=True)
    if units is not None:
        put_small(packed, sent)


def put_small(packed, sent):
    rows, start = packed.shape[0], sent.shape[0] - 2 * packed.shape[0]
    high = packed[...].astype(BF16)
    sent[start : start + rows] = high
    sent[start + rows : start + 2 * rows] = (packed[...] - high.astype(F32)).astype(BF16)


def take_small(got, rows):
    start = got.shape[0] - 2 * rows
    return got[start : start + rows].astype(F32) + got[start + rows : start + 2 * rows].astype(F32)


def finish_tokens(heads, chips, real, *refs):
    placed, far, tokens, gain, grad_res, weight, kept, sent, projected = refs
    chip, core = position()
    mine = heads * HEAD_DIM
    projected[...] = placed[...]
    if far is not None:

        def place(candidate):
            for part in range(3):
                start = part * real + (candidate ^ (chips - 1)) * mine
                projected[:, start : start + mine] = far[:, part * mine : (part + 1) * mine]

        for_each_chip(chip, chips, place)
    values = tokens[...].astype(F32)
    inverse, totals = inverse_rms(values)
    incoming = dot(projected[...], weight[...], 1, 1)
    grad, unused = norm_back(values, gain[...].astype(F32).reshape(1, -1), inverse, totals, incoming)
    low = (grad + grad_res[...]).astype(BF16)
    length = kept.shape[0]
    either(core, kept, sent, low[:length], low[length:])


def finish_near(heads, chips, real, placed, *refs):
    finish_tokens(heads, chips, real, placed, None, *refs)


def shared(chips, bit, at):
    chip, unused = position()
    return ((chip >> bit) & 1) == ((at >> bit) & 1), (at >> (bit + 1) << bit) | (at & ((1 << bit) - 1))


def stream_sums(chips, dp, bit, cut, columns, left, left_other, right, right_other, sent, kept, rest):
    start, rows, right_start = columns
    share = rows // dp
    chip, unused = position()
    mine = (chip >> bit) & 1
    step = math.gcd(start, rows)

    def make(out, place, at, cols, kind):
        total = dot(left[:, cols], right[...], 0, 0) + dot(left_other[:, cols], right_other[:, right_start:], 0, 0)
        for part in range(dp):
            out[place, part] = total[part * share : part * share + cut].astype(kind)
            rest[at, part] = total[part * share + cut : (part + 1) * share]

    for out, stays, kind in ((sent, False, BF16), (kept, True, F32)):
        for place in range(chips // 2):
            side = mine if stays else 1 - mine
            low, high = place & ((1 << bit) - 1), place >> bit << (bit + 1)
            if step % 128 == 0:
                at = high | (side << bit) | low
                make(out, place, at, pl.ds(pl.multiple_of(start + at * rows, step), rows), kind)
                continue
            for value in range(2):
                at = high | (value << bit) | low
                cols = slice(start + at * rows, start + (at + 1) * rows)
                pl.when(side == value)(functools.partial(make, out, place, at, cols, kind))


def third_sums(chips, dp, share, columns, left, left_other, right, right_other, down_rest, up_rest, sent, kept, held):
    start, rows, unused = columns
    down_more = down_rest.shape[2]
    more = down_more + up_rest.shape[2]
    chip, unused = position()
    mine = lax.axis_index("dp") & 1
    total = dot(left[:, start : start + chips * rows], right[...], 0, 0) + dot(
        left_other[:, start : start + chips * rows], right_other[...], 0, 0
    )
    for source in range(chips):
        at = chip ^ source
        for part in range(dp):
            held[part] = total[source * rows + part * share : source * rows + (part + 1) * share]
        for place in range(dp // 2):
            for ref, part, kind in ((kept, 2 * place + mine, F32), (sent, 2 * place + 1 - mine, BF16)):
                ref[at, place, :down_more] = down_rest[at, part].astype(kind)
                ref[at, place, down_more:more] = up_rest[at, part].astype(kind)
                ref[at, place, more:] = held[part].astype(kind)


def fold(steps, *refs):
    count = len(steps)
    kepts, gots, sents, outs = (refs[at * count : (at + 1) * count] for at in range(4))
    for (axis, shift), kept, got, sent, out in zip(steps, kepts, gots, sents, outs):
        bit = (lax.axis_index(axis) >> shift) & 1
        for chip in range(out.shape[0]):
            for part in range(out.shape[1]):
                if axis == "seq":
                    mine, other = (2 * chip + bit, part), (2 * chip + 1 - bit, part)
                else:
                    mine, other = (chip, 2 * part + bit), (chip, 2 * part + 1 - bit)
                out[chip, part] = kept[mine] + got[mine].astype(F32)
                sent[chip, part] = (kept[other] + got[other].astype(F32)).astype(BF16)


def join_streams(step, *refs):
    kepts, gots, (sent, out) = refs[:3], refs[3:6], refs[6:]
    bit = (lax.axis_index(step[0]) >> step[1]) & 1
    start = 0
    for kept, got in zip(kepts, gots):
        size, width = kept.shape[2], kept.shape[3]
        rows = slice(start, start + size)
        start = rows.stop

        def total(part):
            if len(got.shape) == 4:
                return kept[0, part] + got[0, part].astype(F32)
            return kept[0, part] + got[pl.ds(pl.multiple_of(part * size, 8), size), :width].astype(F32)

        for part in range(out.shape[1]):
            out[0, part, rows] = total(2 * part + bit)
            sent[0, part, rows] = total(2 * part + 1 - bit).astype(BF16)


def fold_inward(step, kept, got, packed, sent, out, packed_out):
    bit = (lax.axis_index(step[0]) >> step[1]) & 1
    rows, share, width = packed.shape[0], kept.shape[1], kept.shape[2]
    packed_out[...] = packed[...] + take_small(got, rows)
    put_small(packed_out, sent)
    for at in range(out.shape[0]):
        left, right = (
            kept[part] + got[part * share : (part + 1) * share, :width].astype(F32)
            for part in (at, out.shape[0] + at)
        )
        start = at * share
        out[at] = jnp.where(bit == 0, left, right)
        sent[start : start + share, :width] = jnp.where(bit == 0, right, left).astype(BF16)


def place_pieces(heads, chips, real, *refs):
    pieces, projected = refs[:-1], refs[-1]
    chip, unused = position()
    mine = heads * HEAD_DIM

    def place(candidate):
        for source, piece in enumerate(pieces):
            start = (candidate ^ source) * mine
            size = min(mine, real - start)
            for part in range(3):
                if size > 0:
                    projected[:, part * real + start : part * real + start + size] = piece[
                        :, part * mine : part * mine + size
                    ]

    for_each_chip(chip, chips, place)


def second_step(steps, *refs):
    kepts, gots, in_sent = refs[:3], refs[3:6], refs[6]
    (message, *sents), outs = refs[7:10], refs[10:]
    fold(steps[1:], *kepts[1:], *gots[1:], *sents, *outs[1:])
    (axis, shift), kept, got, out = steps[0], kepts[0], gots[0], outs[0]
    bit = (lax.axis_index(axis) >> shift) & 1
    rows, start = kept.shape[2], 0
    for part in range(out.shape[1]):
        mine, other = (0, 2 * part + bit), (0, 2 * part + 1 - bit)
        out[0, part] = kept[mine] + got[mine].astype(F32)
        message[start : start + rows, : kept.shape[3]] = (kept[other] + got[other].astype(F32)).astype(BF16)
        start += rows
    message[start:] = in_sent[...]


def last_inward(start, kept, message, packed, share, low, packed_out, far):
    rows, count, width = packed.shape[0], share.shape[0], share.shape[1]
    got = message.at[start:]
    total = kept[0] + got[:count, :width].astype(F32)
    share[...] = total
    low[:count, :width] = total.astype(BF16)
    packed_out[...] = packed[...] + take_small(got, rows)
    put_small(packed_out, low)
    put_small(packed_out, far)


def last_wide(a_cut, b_cut, kept, got, down, up, outward):
    share = down.shape[0]

    def total(start, size):
        rows = slice(start, start + size)
        return kept[0, 0, rows] + got[0, 0, rows].astype(F32)

    down[:a_cut] = total(0, a_cut)
    up[:b_cut] = total(a_cut, b_cut)
    down[a_cut:] = total(a_cut + b_cut, share - a_cut)
    up[b_cut:] = total(b_cut + share, share - b_cut)
    outward[...] = total(2 * share, outward.shape[0])


def place_inward(dp, size, real, table, share, packed, *refs):
    gots, far, out, outs, held = refs[:2], refs[2], refs[3], refs[4:-1], refs[-1]
    count, small = share.shape[0] // size, packed.shape[0]
    width = share.shape[1]
    sums = packed[...] + take_small(far, small)
    for unit in range(count):
        held[0, unit] = share[unit * size : (unit + 1) * size]
        for at, piece in enumerate(gots):
            start = unit * size
            held[at + 1, unit] = piece[start : start + size, :width].astype(F32)
    for piece in gots:
        sums = sums + take_small(piece, small)
    put_sums(real, sums, *outs)
    device = lax.axis_index("seq") * dp + lax.axis_index("dp")
    for unit in range(count):
        place = 2 * (device * count + unit)
        out[unit * size : (unit + 1) * size] = held[table[place], table[place + 1]]


def put_sums(real, sums, gain_first, bias_in, bias_out, gain_second, bias_up, bias_down):
    width = gain_first.shape[0]
    gain_first[...] = sums[0:1, :width].reshape(width)
    bias_in[...] = sums[1:3, :real]
    bias_out[...] = sums[3:4, :width].reshape(width)
    gain_second[...] = sums[4:5, :width].reshape(width)
    bias_down[...] = sums[5:6, :width].reshape(width)
    for at in range(bias_up.shape[0] // real):
        bias_up[at * real : (at + 1) * real] = sums[6 + at : 7 + at, :real].reshape(real)


def last_small(real, packed, *outs):
    put_sums(real, packed[...], *outs)


def inward_units(chips, dp, real, mine):
    share = 3 * real // (2 * chips * dp)
    size = math.gcd(share, mine)
    count = share // size
    if chips != 4 or dp != 4 or chips * mine != real or size % 8:
        return None
    units, table = [], np.zeros((2 * chips * dp, count, 2), np.int32)
    for chip in range(chips):
        filled, own = {}, []
        for part in range(3):
            for at in range(mine // size):
                unit = (part * real + chip * mine) // size + at
                holder, place = unit // count, unit % count
                slot = ((holder // dp) & 1, holder % dp)
                here = filled.get(slot, 0)
                filled[slot] = here + 1
                own.append((*slot, here * size, part * mine + at * size, size))
                table[holder, place] = (holder // dp // 2) ^ chip, here
        if len(filled) != 2 * dp or set(filled.values()) != {count}:
            return None
        units.append(own)
    if table[:, :, 0].max() > 2:
        return None
    return size, units, table.reshape(-1)


def flip(value, mask, axis="seq"):
    return lax.ppermute(value, axis, [(at, at ^ mask) for at in range(lax.axis_size(axis))])


def bits_of(size):
    return [1 << at for at in range(size.bit_length() - 1)]


def local(
    tokens, doc_lengths, first_gain, inward_weight, inward_bias, outward_weight, outward_bias,
    second_gain, up_weight, up_bias, down_weight, down_bias, cotangent,
):
    rows, local_len, width = tokens.shape
    seq, dp = lax.axis_size("seq"), lax.axis_size("dp")
    chips = seq // 2
    block = rows * local_len
    length = seq * local_len
    real = HEADS * HEAD_DIM
    heads = -(-HEADS // chips)
    mine = heads * HEAD_DIM
    slots = chips * mine
    ff = up_weight.shape[1]
    chip_bits, dp_bits = bits_of(chips), bits_of(dp)

    def shape(*dims, kind=BF16):
        return jax.ShapeDtypeStruct(dims, kind)

    def call(kernel, name, outs, args, scratch=(), flops=1, mib=16, specs=None):
        return pl.pallas_call(
            kernel,
            out_shape=outs,
            in_specs=specs or [VMEM] * len(args),
            out_specs=jax.tree.map(lambda unused: VMEM, outs),
            scratch_shapes=scratch,
            compiler_params=pltpu.CompilerParams(vmem_limit_bytes=mib * 1024 * 1024),
            cost_estimate=pl.CostEstimate(flops=flops, bytes_accessed=1, transcendentals=0),
            name=name,
        )(*args)

    def after(value, earlier):
        return hold((value, earlier))[0]

    half_rows = (shape(local_len, width),) * 2

    def to_rows(value, name):
        kept, sent = call(split_rows, name, half_rows, (jnp.transpose(value, (2, 0, 1)),), mib=8)
        return kept, flip(sent, 1)

    def from_rows(kept, sent, name, parts=1):
        size = local_len // parts
        gots = [flip(sent[at * size : (at + 1) * size], 1) for at in range(parts)]
        out = call(join_rows, name, shape(width, rows, local_len), (kept, *gots), mib=8)
        return jnp.transpose(out, (1, 2, 0))

    def exchange(pieces):
        return [pieces[0]] + [flip(pieces[at], 2 * at) for at in range(1, chips)]

    kept, got = to_rows(tokens, "split_tokens")
    weight_mine = call(
        functools.partial(pick_weights, heads, chips, real), "pick_weights", shape(width, 3 * mine),
        (after(inward_weight, kept),),
    )
    places, pieces = [(0, 1), (0, 0)], [kept, got]
    if chips == 4:
        kept_one, kept_two = flip(kept, 2), flip(kept, 4)
        got_late = after(got, weight_mine)
        got_one, got_two = flip(got_late, 2), flip(got_late, 4)
        places += [(1, 1), (2, 1), (1, 0), (2, 0), (3, 1), (3, 0)]
        pieces += [kept_one, kept_two, got_one, got_two]
    else:
        for which, value in ((1, kept), (0, got)):
            held = value[None]
            for bit in chip_bits:
                held = jnp.concatenate([held, flip(held, 2 * bit)], axis=0)
            places += [(at, which) for at in range(1, chips)]
            pieces += [held[at] for at in range(1, chips)]
    projected = [shape(local_len, width), shape(local_len, 1, kind=F32), shape(local_len, 3 * mine)]
    bias_mine, scale, starts, normed_one, row_tokens, *parts = call(
        functools.partial(project_first, heads, chips, real), "project_first",
        [shape(1, 3 * mine, kind=F32), shape(1, width, kind=F32), shape(length, 1, kind=jnp.int32)]
        + [shape(block, width)] * 2 + projected * 2,
        (doc_lengths, kept, got, first_gain, inward_bias, weight_mine),
        flops=2 * block * width * 3 * mine, specs=[SMEM] + [VMEM] * 5,
    )
    if chips == 4:
        pieces.append(flip(after(kept_one, (kept_two, row_tokens)), 4))
        pieces.append(flip(after(got_two, row_tokens), 2))
    cot_kept, cot_got = to_rows(after(cotangent, pieces[3]), "split_cotangent")
    fresh = 2
    middle = pieces[2:-fresh]
    parts += call(
        functools.partial(project_more, len(middle)), "project_more", projected * len(middle),
        (*middle, weight_mine, bias_mine, scale), flops=block * len(middle) * width * 3 * mine,
    )
    row_cot, grad_active = call(
        active_cotangent, "active_cotangent", (shape(block, width), shape(block, ff, kind=F32)),
        (cot_kept, cot_got, down_weight), mib=16,
    )

    outward_pad = outward_weight
    if slots != real:
        outward_pad = jnp.pad(outward_weight, ((0, slots - real), (0, 0)))

    forward = call(
        functools.partial(attention_forward, heads, chips, block, places, fresh), "attention_forward",
        [shape(length, 3 * mine), shape(length, mine, kind=F32), shape(length, 8, kind=F32)]
        + [shape(block, mine)] * chips + projected * fresh,
        (*parts[2::3], *pieces[-fresh:], weight_mine, bias_mine, scale, starts),
        flops=8 * length * length * mine, mib=8 + length // 128,
    )
    qkv, attended, logs = forward[:3]
    parts += forward[3 + chips :]
    attended_in = exchange(forward[3 : 3 + chips])
    row_cot, grad_active = call(
        active_cotangent, "active_cotangent", (shape(block, width), shape(block, ff, kind=F32)),
        (after(cot_kept, forward[3]), cot_got, down_weight), flops=2 * block * width * ff,
    )

    whole = call(
        functools.partial(whole_rows, chips, block, places), "whole_rows",
        [shape(length, width), shape(length, width, kind=F32)],
        (after(pieces[0], grad_active), *pieces[1:], *parts[0::3], *parts[1::3]), mib=8 + length // 128 + 2,
    )

    cot_other = flip(row_cot, 1)
    residual, normed_two, active, grad_up, kept, sent = call(
        functools.partial(up_branch, heads, chips, real), "up_branch",
        (
            shape(block, width, kind=F32), shape(block, width), shape(block, ff), shape(block, ff),
            shape(block, ff + slots // 2), shape(block, ff + slots // 2 + width),
        ),
        (
            *attended_in[::-1], after(row_tokens, whole[0]), grad_active, outward_pad, outward_bias, second_gain,
            up_weight, up_bias,
        ),
        flops=2 * block * width * ff, mib=23,
    )
    other = flip(sent, 1)
    back = call(
        functools.partial(back_branch, heads, chips, real), "back_branch",
        (shape(block, mine),) * chips
        + (shape(block, width, kind=F32), shape(block, width), shape(1, width, kind=F32)),
        (residual, row_cot, grad_up, up_weight, outward_pad, second_gain),
        flops=2 * block * width * ff, mib=16,
    )
    grad_res, grad_low, gain_grad = back[chips:]
    low_other = flip(grad_low, 1)
    grad_in = exchange(back[:chips])

    share, out_share, in_share = ff // (seq * dp), real // (seq * dp), 3 * real // (seq * dp)
    a_cut, b_cut = share - share // 4, share - share // 4
    third = 2 * share - a_cut - b_cut + out_share
    x_bit, y_bit = 0, len(chip_bits) - 1

    def stream(name, bit, cut, columns, args):
        dims = (chips // 2, dp, cut, width)
        return call(
            functools.partial(stream_sums, chips, dp, bit, cut, columns), name,
            [shape(*dims), shape(*dims, kind=F32), shape(chips, dp, share - cut, width, kind=F32)], args,
            mib=18,
        )

    a_sent, a_kept, down_rest = stream(
        "down_sums", x_bit, a_cut, (0, ff // seq, 0), (kept, other, row_cot, cot_other)
    )
    b_sent, b_kept, up_rest = stream(
        "up_sums", y_bit, b_cut, (ff // 2, ff // seq, ff + slots // 2), (after(kept, a_sent), other, normed_two, other)
    )
    c_dims = (chips, dp // 2, third, width)
    c_sent, c_kept = call(
        functools.partial(third_sums, chips, dp, out_share, (ff, mine // 2, 0)), "out_sums",
        [shape(*c_dims), shape(*c_dims, kind=F32)],
        (after(kept, (b_sent, *grad_in[1:-1])), other, grad_low, low_other, down_rest, up_rest),
        scratch=[pltpu.VMEM((dp, out_share, width), F32)], mib=18,
    )
    a_got, b_got, c_got = flip(a_sent, 2 << x_bit), flip(b_sent, 2 << y_bit), flip(c_sent, 1, "dp")

    grad_in[0] = after(grad_in[0], c_sent)
    *grad_qkv, grad_all = call(
        functools.partial(attention_backward, heads, chips, block), "attention_backward",
        [shape(block, 3 * mine)] * chips + [shape(length, 3 * mine)],
        (starts, qkv, attended, logs, *grad_in),
        scratch=[
            pltpu.VMEM((length, mine), BF16), pltpu.VMEM((HEAD_DIM, length), F32),
            pltpu.VMEM((HEAD_DIM, length), F32),
        ],
        flops=200 * length * length * mine, mib=8 + length // 128,
    )
    plan = inward_units(chips, dp, real, mine)
    small_rows = 6 + ff // real
    packed_shape = shape(small_rows, real, kind=F32)
    row_outs = [packed_shape]
    if plan is not None:
        row_outs += [shape(2 * small_rows + dp * in_share, real), shape(dp, in_share, width, kind=F32)]
    packed, *inward = call(
        functools.partial(row_sums, heads, chips, block, real, plan and plan[1]), "row_sums", row_outs,
        (grad_all, weight_mine, gain_grad, grad_low, row_cot, grad_up, *whole),
        scratch=[
            pltpu.VMEM((3 * mine, width), F32),
        ],
        flops=12 * length * mine * width, mib=8 + length // 128 + 2,
    )

    def hop(value, step):
        return flip(value, 1 << step[1], step[0])

    chip_steps = [("seq", 1 + at) for at in range(len(chip_bits))]
    dp_steps = [("dp", at) for at in range(len(dp_bits))]
    rounds = list(zip(
        [step for step in chip_steps if step[1] != 1 + x_bit] + dp_steps[:1],
        dp_steps[:1] + [step for step in chip_steps if step[1] != 1 + y_bit],
        chip_steps,
    ))
    kepts, gots = [a_kept, b_kept, c_kept], [a_got, b_got, c_got]
    earlier = packed
    if plan is not None:
        in_sent, in_kept = inward
        in_got, small = flip(in_sent, 1), packed

    def half_dims(at):
        dims = [list(kept.shape) for kept in kepts]
        for dim, step in zip(dims, rounds[at]):
            dim[step[0] == "dp"] //= 2
        return dims

    sums_shapes = [shape(width, kind=F32), shape(2, real, kind=F32), shape(width, kind=F32)]
    sums_shapes += [shape(width, kind=F32), shape(ff, kind=F32), shape(width, kind=F32)]
    def finish_outputs(earlier):
        out_kept, out_sent = call(
            finish_output, "finish_output", half_rows, (residual, after(active, earlier), down_weight, down_bias),
        )
        return from_rows(out_kept, out_sent, "join_output")

    if plan is not None:
        half = (in_kept.shape[0] // 2,) + in_kept.shape[1:]
        in_sent, in_kept, small = call(
            functools.partial(fold_inward, dp_steps[1]), "fold_inward",
            [shape(2 * small_rows + half[0] * in_share, real), shape(*half, kind=F32), packed_shape],
            (in_kept, in_got, small),
        )
        in_got = hop(in_sent, dp_steps[1])
        near = [grad_qkv[0], flip(grad_qkv[1], 2), flip(grad_qkv[2], 4)]
        dims = half_dims(0)
        outs = call(
            functools.partial(fold, rounds[0]), "round_0",
            [shape(*dim) for dim in dims] + [shape(*dim, kind=F32) for dim in dims],
            (after(kepts[0], in_sent), *kepts[1:], *gots),
        )
        gots = [hop(sent, step) for sent, step in zip(outs[:3], rounds[0])]
        kepts = outs[3:]
        placed = call(
            functools.partial(place_pieces, heads, chips, real), "place_pieces", shape(block, 3 * real),
            (after(near[0], outs[0]), *near[1:]), flops=20 * 10**9,
        )
        output_tokens = finish_outputs(placed)
        half = (half[0] // 2,) + half[1:]
        in_sent, in_kept, small = call(
            functools.partial(fold_inward, dp_steps[0]), "fold_inward",
            [shape(2 * small_rows + half[0] * in_share, real), shape(*half, kind=F32), packed_shape],
            (after(in_kept, output_tokens), in_got, small),
        )
        dims = half_dims(1)
        counts = [math.prod(dim[:3]) for dim in dims]
        outs = call(
            functools.partial(second_step, rounds[1]), "round_1",
            [shape(counts[0] + in_sent.shape[0], real)] + [shape(*dim) for dim in dims[1:]]
            + [shape(*dim, kind=F32) for dim in dims],
            (*kepts, *gots, in_sent),
        )
        gots = [hop(sent, step) for sent, step in zip(outs[:3], rounds[1])]
        kepts = outs[3:]
        earlier = outs[0]
        across = flip(after(grad_qkv[3], (gots[1], gots[2])), 6)
    else:
        for at in range(len(rounds)):
            dims = half_dims(at)
            outs = call(
                functools.partial(fold, rounds[at]), f"round_{at}",
                [shape(*dim) for dim in dims] + [shape(*dim, kind=F32) for dim in dims], (*kepts, *gots),
            )
            kepts, gots = outs[3:], [hop(sent, step) for sent, step in zip(outs[:3], rounds[at])]
        placed = call(
            functools.partial(place_pieces, heads, chips, real), "place_pieces", shape(block, 3 * real),
            tuple(exchange(grad_qkv)),
        )
        output_tokens = finish_outputs(placed)
    if plan is not None:
        share_sum, low, small, far = call(
            functools.partial(last_inward, counts[0]), "last_inward",
            [
                shape(in_share, width, kind=F32), shape(2 * small_rows + in_share, real), packed_shape,
                shape(2 * small_rows, real),
            ],
            (after(in_kept, earlier), gots[0], small),
        )
        earlier = low
    dims = (1, kepts[0].shape[1] // 2, a_cut + b_cut + third, width)
    sent, kept = call(
        functools.partial(join_streams, dp_steps[1]), "join_streams", [shape(*dims), shape(*dims, kind=F32)],
        (after(kepts[0], earlier), *kepts[1:], *gots),
    )
    got = hop(sent, dp_steps[1])
    earlier = sent
    for step in dp_steps[2:]:
        dims = (1, kept.shape[1] // 2) + kept.shape[2:]
        sent, kept = call(
            functools.partial(fold, (step,)), "fold_joined", [shape(*dims), shape(*dims, kind=F32)], (kept, got)
        )
        got = hop(sent, step)
    if plan is not None:
        low = after(low, sent)
        far = flip(after(far, sent), 6)
        in_pieces = [share_sum, small, flip(low, 2), flip(low, 4), far]

    rows_kept, rows_sent = call(
        functools.partial(finish_tokens if plan is not None else finish_near, heads, chips, real), "finish_tokens",
        list(half_rows),
        (placed, *([across] if plan is not None else []), after(row_tokens, earlier), first_gain, grad_res, inward_weight),
        scratch=[pltpu.VMEM((block, 3 * real), BF16)],
        mib=16,
    )
    if plan is not None:
        size, unused, table = plan
        in_out, *sums_out = call(
            functools.partial(place_inward, dp, size, real), "place_inward",
            [shape(in_share, width, kind=F32)] + sums_shapes, (jnp.asarray(table), in_pieces[0], *in_pieces[1:]),
            scratch=[pltpu.VMEM((3, in_share // size, size, width), F32)],
            specs=[SMEM] + [VMEM] * (chips + 1),
        )
    else:
        in_out = lax.psum_scatter(dot(placed, normed_one, 0, 0), ("seq", "dp"), scatter_dimension=0, tiled=True)
        for step in [("seq", 0)] + chip_steps + dp_steps:
            packed = packed + hop(packed, step)
        sums_out = call(functools.partial(last_small, real), "last_small", sums_shapes, (packed,))
    grad_tokens = from_rows(after(rows_kept, in_out), rows_sent, "join_tokens", 2)
    down_share, up_share, out_out = call(
        functools.partial(last_wide, a_cut, b_cut), "last_wide",
        [shape(share, width, kind=F32), shape(share, width, kind=F32), shape(out_share, width, kind=F32)],
        (after(kept, grad_tokens), got),
    )

    gain_first, bias_in, bias_out, gain_second, bias_up, bias_down = sums_out
    return (
        output_tokens, grad_tokens, gain_first, in_out.T, bias_in, out_out, bias_out, gain_second,
        up_share.T, bias_up, down_share, bias_down,
    )


def solution(mesh):
    return jax.shard_map(
        local,
        mesh=mesh,
        in_specs=(P("dp", "seq", None), P("dp", None)) + (P(),) * 10 + (P("dp", "seq", None),),
        out_specs=(
            P("dp", "seq", None),
            P("dp", "seq", None),
            P(),
            P(None, ("seq", "dp")),
            P(),
            P(("seq", "dp"), None),
            P(),
            P(),
            P(None, ("seq", "dp")),
            P(),
            P(("seq", "dp"), None),
            P(),
        ),
        check_vma=False,
    )
```

```python
import functools
import math

import jax
import jax.numpy as jnp
import numpy as np
from jax import lax
from jax.experimental import pallas as pl
from jax.experimental.pallas import tpu as pltpu
from jax.sharding import PartitionSpec as P

HEADS = 12
HEAD_DIM = 64
EPSILON = 1e-05
FLOOR = -1e30
SCALE = HEAD_DIM**-0.5
QB = 256
F32 = jnp.float32
BF16 = jnp.bfloat16
VMEM = pl.BlockSpec(memory_space=pltpu.VMEM)
SMEM = pl.BlockSpec(memory_space=pltpu.SMEM)
hold = lax.optimization_barrier

def inverse_rms(values):
    squares = jnp.sum(values * values, axis=-1, keepdims=True)
    totals = jnp.sum(values, axis=-1, keepdims=True)
    return lax.rsqrt((squares + totals * totals) / (values.shape[-1] + 1) + EPSILON), totals


def norm_back(values, gain, inverse, totals, incoming):
    weighted = incoming * gain
    dots = jnp.sum(weighted * values, axis=-1, keepdims=True)
    factor = inverse * inverse * inverse * dots / (values.shape[-1] + 1)
    grad = inverse * weighted - factor * (values + totals)
    return grad, jnp.sum(incoming * values * inverse, axis=0, keepdims=True)


def dot(left, right, left_dim, right_dim):
    return lax.dot_general(
        left, right, (((left_dim,), (right_dim,)), ((), ())), preferred_element_type=F32
    )


def gelu_both(value):
    linear = 0.7978845608028654 * value
    cubic = linear * (0.044715 * (value * value))
    curve = jnp.tanh(linear + cubic)
    half = 0.5 + 0.5 * curve
    slope = half * (1.0 + (linear + 3.0 * cubic) * (1.0 - curve))
    return value * half, slope


def at_block(index, block):
    return pl.ds(pl.multiple_of(index * block, block), block)


def position():
    me = lax.axis_index("seq")
    return me >> 1, me & 1


def either(flag, first, second, left, right):
    @pl.when(flag == 0)
    def straight():
        first[...] = left
        second[...] = right

    @pl.when(flag != 0)
    def crossed():
        first[...] = right
        second[...] = left


def for_each_chip(chip, chips, body):
    for candidate in range(chips):
        pl.when(chip == candidate)(functools.partial(body, candidate))


def allowed_block(starts, query_start, keys):
    query_pos = query_start + lax.broadcasted_iota(jnp.int32, (QB, 1), 0)
    key_pos = lax.broadcasted_iota(jnp.int32, (1, keys), 1)
    return (key_pos <= query_pos) & (key_pos >= starts)


def split_rows(value, kept, sent):
    unused, core = position()
    length = value.shape[2]
    turned = value[...].reshape(value.shape[0], 2 * length).T
    either(core, kept, sent, turned[:length], turned[length:])


def join_rows(kept, *refs):
    gots, out = refs[:-1], refs[-1]
    unused, core = position()
    mine, other = [kept[...]], [got[...] for got in gots]

    def store(parts):
        out[...] = jnp.concatenate(parts, axis=0).T.reshape(out.shape)

    pl.when(core == 0)(lambda: store(mine + other))
    pl.when(core != 0)(lambda: store(other + mine))


def project(piece, scale, weight, bias, normed, inverse, qkv):
    values = piece[...].astype(F32)
    factor, unused = inverse_rms(values)
    low = (values * scale[...] * factor).astype(BF16)
    normed[...] = low
    inverse[...] = factor
    qkv[...] = (dot(low, weight[...], 1, 0) + bias[...]).astype(BF16)


def pick_weights(heads, chips, real, weight, weight_mine):
    width = heads * HEAD_DIM
    chip, unused = position()

    def choose(candidate):
        size = max(min(width, real - candidate * width), 0)
        for part in range(3):
            at, start = part * width, part * real + candidate * width
            if size > 0:
                weight_mine[:, at : at + size] = weight[:, start : start + size]
            if size < width:
                weight_mine[:, at + size : at + width] = jnp.zeros((weight.shape[0], width - size), BF16)

    for_each_chip(chip, chips, choose)


def project_first(heads, chips, real, docs, kept, got, gain, bias, weight, *refs):
    bias_mine, scale, starts, normed_own, own = refs[:5]
    width = heads * HEAD_DIM
    chip, core = position()

    def choose(candidate):
        size = max(min(width, real - candidate * width), 0)
        for part in (0, 2):
            if size > 0:
                bias_mine[:, part * width : part * width + size] = bias[
                    part // 2 : part // 2 + 1, candidate * width : candidate * width + size
                ].astype(F32)

    bias_mine[...] = jnp.zeros(bias_mine.shape, F32)
    for_each_chip(chip, chips, choose)
    scale[...] = gain[...].astype(F32).reshape(1, -1)
    places = lax.broadcasted_iota(jnp.int32, starts.shape, 0)
    start, end = jnp.zeros_like(places), jnp.int32(0)
    for at in range(3):
        end = end + docs[core, at]
        start = jnp.where(places >= end, end, start)
    starts[...] = start
    rows = kept.shape[0]
    for at, (piece, half) in enumerate(((kept, core), (got, 1 - core))):
        normed, inverse, qkv = refs[5 + 3 * at : 8 + 3 * at]
        project(piece, scale, weight, bias_mine, normed, inverse, qkv)
        normed_own[at_block(half, rows), :] = normed[...]
        own[at_block(half, rows), :] = piece[...]


def project_more(count, *refs):
    pieces, (weight, bias, scale), outs = refs[:count], refs[count : count + 3], refs[count + 3 :]
    for at, piece in enumerate(pieces):
        project(piece, scale, weight, bias, *outs[3 * at : 3 * at + 3])


def attention_forward(heads, chips, block, places, fresh, *refs):
    count = len(places)
    done, pieces = refs[: count - fresh], refs[count - fresh : count]
    (weight, bias, scale, starts), outs = refs[count : count + 4], refs[count + 4 :]
    qkv, attended, logs = outs[:3]
    sends, parts = outs[3 : 3 + chips], outs[3 + chips :]
    width = heads * HEAD_DIM
    chip, core = position()
    for at, (source, mine) in enumerate(places):
        part = done[at] if at < count - fresh else parts[3 * (at - count + fresh) + 2]
        if at >= count - fresh:
            at_parts = 3 * (at - count + fresh)
            project(pieces[at - count + fresh], scale, weight, bias, *parts[at_parts : at_parts + 3])
        rows = part.shape[0]
        half = core if mine else 1 - core
        start = pl.multiple_of((chip ^ source) * block + half * rows, rows)
        qkv[pl.ds(start, rows), :] = part[...]
    for at_query in range(chips * block // QB):
        rows = pl.ds(at_query * QB, QB)
        keys = (at_query + 1) * QB
        allowed = allowed_block(starts[rows, :], at_query * QB, keys)
        for head in range(heads):
            at = head * HEAD_DIM
            query = qkv[rows, at : at + HEAD_DIM] * BF16(SCALE)
            key = qkv[:keys, width + at : width + at + HEAD_DIM]
            value = qkv[:keys, 2 * width + at : 2 * width + at + HEAD_DIM]
            scores = jnp.where(allowed, dot(query, key, 1, 1), FLOOR)
            top = jnp.max(scores, axis=-1, keepdims=True)
            weights = jnp.exp(scores - top)
            total = jnp.sum(weights, axis=-1, keepdims=True)
            attended[rows, at : at + HEAD_DIM] = dot(weights.astype(BF16), value, 1, 0) / total
            logs[rows, head : head + 1] = top + jnp.log(total)
    for source in range(chips):
        sends[source][...] = attended[at_block(chip ^ source, block), :].astype(BF16)


def attention_backward(heads, chips, block, starts, qkv, attended, logs, *refs):
    grads, sends = refs[:chips], refs[chips : 2 * chips]
    out, grad_row, key_grad, value_grad = refs[2 * chips :]
    width = heads * HEAD_DIM
    chip, core = position()
    for source in range(chips):
        grad_row[at_block(chip ^ source, block), :] = grads[source][...]
    blocks = chips * block // QB
    for head in range(heads):
        at = head * HEAD_DIM
        turned_query = (qkv[:, at : at + HEAD_DIM] * BF16(SCALE)).T
        turned_grad = grad_row[:, at : at + HEAD_DIM].T
        for at_query in reversed(range(blocks)):
            lanes = slice(at_query * QB, (at_query + 1) * QB)
            rows = pl.ds(at_query * QB, QB)
            keys = (at_query + 1) * QB
            allowed = allowed_block(starts[rows, :], at_query * QB, keys)
            query = qkv[rows, at : at + HEAD_DIM] * BF16(SCALE)
            key = qkv[:keys, width + at : width + at + HEAD_DIM]
            value = qkv[:keys, 2 * width + at : 2 * width + at + HEAD_DIM]
            grad = grad_row[rows, at : at + HEAD_DIM]
            delta = jnp.sum(
                grad.astype(F32) * attended[rows, at : at + HEAD_DIM], axis=-1, keepdims=True
            )
            scores = dot(query, key, 1, 1)
            weights = jnp.where(allowed, jnp.exp(scores - logs[rows, head : head + 1]), 0.0)
            grad_weights = dot(grad, value, 1, 1)
            grad_scores = (weights * (grad_weights - delta)).astype(BF16)
            out[rows, at : at + HEAD_DIM] = (dot(grad_scores, key, 1, 0) * SCALE).astype(BF16)
            key_part = dot(turned_query[:, lanes], grad_scores, 1, 0)
            value_part = dot(turned_grad[:, lanes], weights.astype(BF16), 1, 0)
            if at_query == blocks - 1:
                key_grad[...] = key_part
                value_grad[...] = value_part
            else:
                key_grad[:, :keys] += key_part
                value_grad[:, :keys] += value_part
        out[:, width + at : width + at + HEAD_DIM] = key_grad[...].astype(BF16).T
        out[:, 2 * width + at : 2 * width + at + HEAD_DIM] = value_grad[...].astype(BF16).T
    for source in range(chips):
        sends[source][...] = out[at_block(chip ^ source, block), :]


def active_cotangent(kept, got, weight, row, out):
    unused, core = position()
    length = kept.shape[0]
    row[at_block(core, length), :] = kept[...]
    row[at_block(1 - core, length), :] = got[...]
    out[...] = dot(row[...], weight[...], 1, 1)


def up_branch(heads, chips, real, *refs):
    pieces = refs[:chips][::-1]
    tokens, grad_active, out_weight, out_bias, gain, up_weight, up_bias = refs[chips : chips + 7]
    residual, normed, active, grad_up, kept, sent = refs[chips + 7 : chips + 13]
    held = refs[chips + 13 :]
    chip, core = position()
    mine = heads * HEAD_DIM
    ff = up_weight.shape[1]

    values = tokens[...].astype(F32) + out_bias[...].astype(F32).reshape(1, -1)
    for source, piece in enumerate(pieces):
        values = values + dot(piece[...], out_weight[at_block(chip ^ source, mine), :], 1, 0)
    residual[...] = values
    inverse, unused = inverse_rms(values)
    low = (values * gain[...].astype(F32).reshape(1, -1) * inverse).astype(BF16)
    normed[...] = low
    sent[:, ff + real // 2 :] = low

    def share(start, size, at, left, right):
        place = slice(start + at * size, start + (at + 1) * size)
        kept[:, place] = jnp.where(core == 0, left, right)
        sent[:, place] = jnp.where(core == 0, right, left)

    if not held:
        for source, piece in enumerate(pieces):
            share(ff, mine // 2, source, piece[:, : mine // 2], piece[:, mine // 2 :])
    else:

        def place(candidate):
            for source, piece in enumerate(pieces):
                start = (candidate ^ source) * mine
                size = min(mine, real - start)
                if size > 0:
                    held[0][:, start : start + size] = piece[:, :size]

        for_each_chip(chip, chips, place)
        piece = real // (2 * chips)
        for at in range(chips):
            start = 2 * at * piece
            share(ff, piece, at, held[0][:, start : start + piece], held[0][:, start + piece : start + 2 * piece])
    tile = ff // chips
    piece = tile // 2
    for at in range(chips):
        cols = slice(at * tile, (at + 1) * tile)
        upward = dot(normed[...], up_weight[:, cols], 1, 0) + up_bias[cols].astype(F32).reshape(1, -1)
        act, slope = gelu_both(upward)
        low = act.astype(BF16)
        active[:, cols] = low
        share(0, piece, at, low[:, :piece], low[:, piece:])
        back = (grad_active[:, cols] * slope).astype(BF16)
        grad_up[:, cols] = back
        share(ff // 2, piece, at, back[:, :piece], back[:, piece:])


def back_branch(heads, chips, real, residual, cotangent, grad_up, up_weight, out_weight, gain, *refs):
    sends = refs[:chips]
    grad_res, grad_low, gain_grad = refs[chips:]
    chip, unused = position()
    mine = heads * HEAD_DIM
    values = residual[...]
    inverse, totals = inverse_rms(values)
    incoming = dot(grad_up[...], up_weight[...], 1, 1)
    grad, gain_sum = norm_back(values, gain[...].astype(F32).reshape(1, -1), inverse, totals, incoming)
    cot = cotangent[...].astype(F32)
    grad = grad + cot
    grad_res[...] = grad
    low = grad.astype(BF16)
    grad_low[...] = low
    gain_grad[...] = gain_sum
    for source in range(chips):
        sends[source][...] = dot(low, out_weight[at_block(chip ^ source, mine), :], 1, 1).astype(BF16)


def finish_output(residual, active, weight, bias, kept, sent):
    unused, core = position()
    values = residual[...] + dot(active[...], weight[...], 1, 0) + bias[...].astype(F32).reshape(1, -1)
    low = values.astype(BF16)
    length = kept.shape[0]
    either(core, kept, sent, low[:length], low[length:])


def row_pieces(chips, block, places, pieces, out):
    chip, core = position()
    for (source, mine), piece in zip(places, pieces):
        rows = piece.shape[0]
        half = core if mine else 1 - core
        out[pl.ds(pl.multiple_of((chip ^ source) * block + half * rows, rows), rows), :] = piece[...]


def whole_rows(chips, block, places, *refs):
    count = len(places)
    tokens, normed, inverse = refs[:count], refs[count : 2 * count], refs[2 * count : 3 * count]
    row_normed, row_scaled = refs[3 * count :]
    row_pieces(chips, block, places, normed, row_normed)
    chip, core = position()
    for (source, mine), piece, factor in zip(places, tokens, inverse):
        rows = piece.shape[0]
        half = core if mine else 1 - core
        start = pl.multiple_of((chip ^ source) * block + half * rows, rows)
        row_scaled[pl.ds(start, rows), :] = piece[...].astype(F32) * factor[...]


def row_sums(heads, chips, block, real, units, grad_qkv, weight_mine, gain_grad, low, cotangent, grad_up, *refs):
    (row_normed, row_scaled), outs, partial = refs[:2], refs[2:-1], refs[-1]
    packed = outs[0]
    chip, core = position()
    mine = heads * HEAD_DIM
    if units is not None:
        partial[...] = dot(grad_qkv[...], row_normed[...], 0, 0)
        sent, kept = outs[1:]
        share = kept.shape[1]

        def split(candidate):
            for for_core, for_replica, at, start, size in units[candidate]:

                @pl.when(core == for_core)
                def keep():
                    kept[for_replica, at : at + size] = partial[start : start + size]

                @pl.when(core != for_core)
                def send():
                    place = for_replica * share + at
                    sent[place : place + size, : partial.shape[1]] = partial[start : start + size].astype(BF16)

        for_each_chip(chip, chips, split)
    width = row_scaled.shape[1]
    packed[...] = jnp.zeros(packed.shape, F32)
    gain_sum = jnp.zeros((1, width), F32)
    for at in range(chips):
        rows = pl.ds(at * block, block)
        incoming = dot(grad_qkv[rows, :], weight_mine[...], 1, 1)
        gain_sum += jnp.sum(
            incoming * row_scaled[rows, :], axis=0, keepdims=True
        )
    packed[0:1, :width] = gain_sum
    query_sum = jnp.sum(grad_qkv[:, :mine].astype(F32), axis=0, keepdims=True)
    value_sum = jnp.sum(grad_qkv[:, 2 * mine :].astype(F32), axis=0, keepdims=True)

    def place(candidate):
        size = min(mine, real - candidate * mine)
        if size > 0:
            packed[1:2, candidate * mine : candidate * mine + size] = query_sum[:, :size]
            packed[2:3, candidate * mine : candidate * mine + size] = value_sum[:, :size]

    for_each_chip(chip, chips, place)
    packed[3:4, :width] = jnp.sum(low[...].astype(F32), axis=0, keepdims=True)
    packed[4:5, :width] = gain_grad[...]
    packed[5:6, :width] = jnp.sum(cotangent[...].astype(F32), axis=0, keepdims=True)
    for at in range(grad_up.shape[1] // real):
        part = grad_up[:, at * real : (at + 1) * real].astype(F32)
        packed[6 + at : 7 + at, :real] = jnp.sum(part, axis=0, keepdims=True)
    if units is not None:
        put_small(packed, sent)


def put_small(packed, sent):
    rows, start = packed.shape[0], sent.shape[0] - 2 * packed.shape[0]
    high = packed[...].astype(BF16)
    sent[start : start + rows] = high
    sent[start + rows : start + 2 * rows] = (packed[...] - high.astype(F32)).astype(BF16)


def take_small(got, rows):
    start = got.shape[0] - 2 * rows
    return got[start : start + rows].astype(F32) + got[start + rows : start + 2 * rows].astype(F32)


def finish_tokens(heads, chips, real, *refs):
    placed, far, tokens, gain, grad_res, weight, kept, sent, projected = refs
    chip, core = position()
    mine = heads * HEAD_DIM
    projected[...] = placed[...]
    if far is not None:

        def place(candidate):
            for part in range(3):
                start = part * real + (candidate ^ (chips - 1)) * mine
                projected[:, start : start + mine] = far[:, part * mine : (part + 1) * mine]

        for_each_chip(chip, chips, place)
    values = tokens[...].astype(F32)
    inverse, totals = inverse_rms(values)
    incoming = dot(projected[...], weight[...], 1, 1)
    grad, unused = norm_back(values, gain[...].astype(F32).reshape(1, -1), inverse, totals, incoming)
    low = (grad + grad_res[...]).astype(BF16)
    length = kept.shape[0]
    either(core, kept, sent, low[:length], low[length:])


def finish_near(heads, chips, real, placed, *refs):
    finish_tokens(heads, chips, real, placed, None, *refs)


def shared(chips, bit, at):
    chip, unused = position()
    return ((chip >> bit) & 1) == ((at >> bit) & 1), (at >> (bit + 1) << bit) | (at & ((1 << bit) - 1))


def stream_sums(chips, dp, bit, cut, columns, left, left_other, right, right_other, sent, kept, rest):
    start, rows, right_start = columns
    share = rows // dp
    chip, unused = position()
    mine = (chip >> bit) & 1
    step = math.gcd(start, rows)

    def make(out, place, at, cols, kind):
        total = dot(left[:, cols], right[...], 0, 0) + dot(left_other[:, cols], right_other[:, right_start:], 0, 0)
        for part in range(dp):
            out[place, part] = total[part * share : part * share + cut].astype(kind)
            rest[at, part] = total[part * share + cut : (part + 1) * share]

    for out, stays, kind in ((sent, False, BF16), (kept, True, F32)):
        for place in range(chips // 2):
            side = mine if stays else 1 - mine
            low, high = place & ((1 << bit) - 1), place >> bit << (bit + 1)
            if step % 128 == 0:
                at = high | (side << bit) | low
                make(out, place, at, pl.ds(pl.multiple_of(start + at * rows, step), rows), kind)
                continue
            for value in range(2):
                at = high | (value << bit) | low
                cols = slice(start + at * rows, start + (at + 1) * rows)
                pl.when(side == value)(functools.partial(make, out, place, at, cols, kind))


def third_sums(chips, dp, share, mixed, columns, left, left_other, right, right_other, down_rest, up_rest, sent, kept, held):
    start, rows, unused = columns
    down_more = down_rest.shape[2]
    more = down_more + up_rest.shape[2]
    chip, unused = position()
    mine = lax.axis_index("dp") & 1
    total = dot(left[:, start : start + chips * rows], right[...], 0, 0) + dot(
        left_other[:, start : start + chips * rows], right_other[...], 0, 0
    )
    for source in range(chips):
        at = chip ^ source if mixed else source
        for part in range(dp):
            held[part] = total[source * rows + part * share : source * rows + (part + 1) * share]
        for place in range(dp // 2):
            for ref, part, kind in ((kept, 2 * place + mine, F32), (sent, 2 * place + 1 - mine, BF16)):
                ref[at, place, :down_more] = down_rest[at, part].astype(kind)
                ref[at, place, down_more:more] = up_rest[at, part].astype(kind)
                ref[at, place, more:] = held[part].astype(kind)


def fold(steps, *refs):
    count = len(steps)
    kepts, gots, sents, outs = (refs[at * count : (at + 1) * count] for at in range(4))
    for (axis, shift), kept, got, sent, out in zip(steps, kepts, gots, sents, outs):
        bit = (lax.axis_index(axis) >> shift) & 1
        for chip in range(out.shape[0]):
            for part in range(out.shape[1]):
                if axis == "seq":
                    mine, other = (2 * chip + bit, part), (2 * chip + 1 - bit, part)
                else:
                    mine, other = (chip, 2 * part + bit), (chip, 2 * part + 1 - bit)
                out[chip, part] = kept[mine] + got[mine].astype(F32)
                sent[chip, part] = (kept[other] + got[other].astype(F32)).astype(BF16)


def join_streams(step, *refs):
    kepts, gots, (sent, out) = refs[:3], refs[3:6], refs[6:]
    bit = (lax.axis_index(step[0]) >> step[1]) & 1
    start = 0
    for kept, got in zip(kepts, gots):
        size, width = kept.shape[2], kept.shape[3]
        rows = slice(start, start + size)
        start = rows.stop

        def total(part):
            if len(got.shape) == 4:
                return kept[0, part] + got[0, part].astype(F32)
            return kept[0, part] + got[pl.ds(pl.multiple_of(part * size, 8), size), :width].astype(F32)

        for part in range(out.shape[1]):
            out[0, part, rows] = total(2 * part + bit)
            sent[0, part, rows] = total(2 * part + 1 - bit).astype(BF16)


def fold_inward(step, kept, got, packed, sent, out, packed_out):
    bit = (lax.axis_index(step[0]) >> step[1]) & 1
    rows, share, width = packed.shape[0], kept.shape[1], kept.shape[2]
    packed_out[...] = packed[...] + take_small(got, rows)
    put_small(packed_out, sent)
    for at in range(out.shape[0]):
        left, right = (
            kept[part] + got[part * share : (part + 1) * share, :width].astype(F32)
            for part in (at, out.shape[0] + at)
        )
        start = at * share
        out[at] = jnp.where(bit == 0, left, right)
        sent[start : start + share, :width] = jnp.where(bit == 0, right, left).astype(BF16)


def place_pieces(heads, chips, real, *refs):
    pieces, projected = refs[:-1], refs[-1]
    chip, unused = position()
    mine = heads * HEAD_DIM

    def place(candidate):
        for source, piece in enumerate(pieces):
            start = (candidate ^ source) * mine
            size = min(mine, real - start)
            for part in range(3):
                if size > 0:
                    projected[:, part * real + start : part * real + start + size] = piece[
                        :, part * mine : part * mine + size
                    ]

    for_each_chip(chip, chips, place)


def second_step(steps, *refs):
    kepts, gots, in_sent = refs[:3], refs[3:6], refs[6]
    (message, *sents), outs = refs[7:10], refs[10:]
    fold(steps[1:], *kepts[1:], *gots[1:], *sents, *outs[1:])
    (axis, shift), kept, got, out = steps[0], kepts[0], gots[0], outs[0]
    bit = (lax.axis_index(axis) >> shift) & 1
    rows, start = kept.shape[2], 0
    for part in range(out.shape[1]):
        mine, other = (0, 2 * part + bit), (0, 2 * part + 1 - bit)
        out[0, part] = kept[mine] + got[mine].astype(F32)
        message[start : start + rows, : kept.shape[3]] = (kept[other] + got[other].astype(F32)).astype(BF16)
        start += rows
    message[start:] = in_sent[...]


def last_inward(start, kept, message, packed, share, low, packed_out, far):
    rows, count, width = packed.shape[0], share.shape[0], share.shape[1]
    got = message.at[start:]
    total = kept[0] + got[:count, :width].astype(F32)
    share[...] = total
    low[:count, :width] = total.astype(BF16)
    packed_out[...] = packed[...] + take_small(got, rows)
    put_small(packed_out, low)
    put_small(packed_out, far)


def last_wide(a_cut, b_cut, kept, got, down, up, outward):
    share = down.shape[0]

    def total(start, size):
        rows = slice(start, start + size)
        return kept[0, 0, rows] + got[0, 0, rows].astype(F32)

    down[:a_cut] = total(0, a_cut)
    up[:b_cut] = total(a_cut, b_cut)
    down[a_cut:] = total(a_cut + b_cut, share - a_cut)
    up[b_cut:] = total(b_cut + share, share - b_cut)
    outward[...] = total(2 * share, outward.shape[0])


def place_inward(dp, size, real, table, share, packed, *refs):
    gots, far, out, outs, held = refs[:2], refs[2], refs[3], refs[4:-1], refs[-1]
    count, small = share.shape[0] // size, packed.shape[0]
    width = share.shape[1]
    sums = packed[...] + take_small(far, small)
    for unit in range(count):
        held[0, unit] = share[unit * size : (unit + 1) * size]
        for at, piece in enumerate(gots):
            start = unit * size
            held[at + 1, unit] = piece[start : start + size, :width].astype(F32)
    for piece in gots:
        sums = sums + take_small(piece, small)
    put_sums(real, sums, *outs)
    device = lax.axis_index("seq") * dp + lax.axis_index("dp")
    for unit in range(count):
        place = 2 * (device * count + unit)
        out[unit * size : (unit + 1) * size] = held[table[place], table[place + 1]]


def put_sums(real, sums, gain_first, bias_in, bias_out, gain_second, bias_up, bias_down):
    width = gain_first.shape[0]
    gain_first[...] = sums[0:1, :width].reshape(width)
    bias_in[...] = sums[1:3, :real]
    bias_out[...] = sums[3:4, :width].reshape(width)
    gain_second[...] = sums[4:5, :width].reshape(width)
    bias_down[...] = sums[5:6, :width].reshape(width)
    for at in range(bias_up.shape[0] // real):
        bias_up[at * real : (at + 1) * real] = sums[6 + at : 7 + at, :real].reshape(real)


def last_small(real, packed, *outs):
    put_sums(real, packed[...], *outs)


def inward_units(chips, dp, real, mine):
    share = 3 * real // (2 * chips * dp)
    size = math.gcd(share, mine)
    count = share // size
    if chips != 4 or dp != 4 or chips * mine != real or size % 8:
        return None
    units, table = [], np.zeros((2 * chips * dp, count, 2), np.int32)
    for chip in range(chips):
        filled, own = {}, []
        for part in range(3):
            for at in range(mine // size):
                unit = (part * real + chip * mine) // size + at
                holder, place = unit // count, unit % count
                slot = ((holder // dp) & 1, holder % dp)
                here = filled.get(slot, 0)
                filled[slot] = here + 1
                own.append((*slot, here * size, part * mine + at * size, size))
                table[holder, place] = (holder // dp // 2) ^ chip, here
        if len(filled) != 2 * dp or set(filled.values()) != {count}:
            return None
        units.append(own)
    if table[:, :, 0].max() > 2:
        return None
    return size, units, table.reshape(-1)


def flip(value, mask, axis="seq"):
    return lax.ppermute(value, axis, [(at, at ^ mask) for at in range(lax.axis_size(axis))])


def bits_of(size):
    return [1 << at for at in range(size.bit_length() - 1)]


def local(
    tokens, doc_lengths, first_gain, inward_weight, inward_bias, outward_weight, outward_bias,
    second_gain, up_weight, up_bias, down_weight, down_bias, cotangent,
):
    rows, local_len, width = tokens.shape
    seq, dp = lax.axis_size("seq"), lax.axis_size("dp")
    chips = seq // 2
    block = rows * local_len
    length = seq * local_len
    real = HEADS * HEAD_DIM
    heads = -(-HEADS // chips)
    mine = heads * HEAD_DIM
    slots = chips * mine
    ff = up_weight.shape[1]
    chip_bits, dp_bits = bits_of(chips), bits_of(dp)

    def shape(*dims, kind=BF16):
        return jax.ShapeDtypeStruct(dims, kind)

    def call(kernel, name, outs, args, scratch=(), flops=1, mib=16, specs=None):
        return pl.pallas_call(
            kernel,
            out_shape=outs,
            in_specs=specs or [VMEM] * len(args),
            out_specs=jax.tree.map(lambda unused: VMEM, outs),
            scratch_shapes=scratch,
            compiler_params=pltpu.CompilerParams(vmem_limit_bytes=mib * 1024 * 1024),
            cost_estimate=pl.CostEstimate(flops=flops, bytes_accessed=1, transcendentals=0),
            name=name,
        )(*args)

    def after(value, earlier):
        return hold((value, earlier))[0]

    half_rows = (shape(local_len, width),) * 2

    def to_rows(value, name):
        kept, sent = call(split_rows, name, half_rows, (jnp.transpose(value, (2, 0, 1)),), mib=8)
        return kept, flip(sent, 1)

    def from_rows(kept, sent, name, parts=1):
        size = local_len // parts
        gots = [flip(sent[at * size : (at + 1) * size], 1) for at in range(parts)]
        out = call(join_rows, name, shape(width, rows, local_len), (kept, *gots), mib=8)
        return jnp.transpose(out, (1, 2, 0))

    def exchange(pieces):
        return [pieces[0]] + [flip(pieces[at], 2 * at) for at in range(1, chips)]

    kept, got = to_rows(tokens, "split_tokens")
    weight_mine = call(
        functools.partial(pick_weights, heads, chips, real), "pick_weights", shape(width, 3 * mine),
        (after(inward_weight, kept),),
    )
    places, pieces = [(0, 1), (0, 0)], [kept, got]
    if chips == 4:
        kept_one, kept_two = flip(kept, 2), flip(kept, 4)
        got_late = after(got, weight_mine)
        got_one, got_two = flip(got_late, 2), flip(got_late, 4)
        places += [(1, 1), (2, 1), (1, 0), (2, 0), (3, 1), (3, 0)]
        pieces += [kept_one, kept_two, got_one, got_two]
    else:
        for which, value in ((1, kept), (0, got)):
            held = value[None]
            for bit in chip_bits:
                held = jnp.concatenate([held, flip(held, 2 * bit)], axis=0)
            places += [(at, which) for at in range(1, chips)]
            pieces += [held[at] for at in range(1, chips)]
    projected = [shape(local_len, width), shape(local_len, 1, kind=F32), shape(local_len, 3 * mine)]
    bias_mine, scale, starts, normed_one, row_tokens, *parts = call(
        functools.partial(project_first, heads, chips, real), "project_first",
        [shape(1, 3 * mine, kind=F32), shape(1, width, kind=F32), shape(length, 1, kind=jnp.int32)]
        + [shape(block, width)] * 2 + projected * 2,
        (doc_lengths, kept, got, first_gain, inward_bias, weight_mine),
        flops=2 * block * width * 3 * mine, specs=[SMEM] + [VMEM] * 5,
    )
    if chips == 4:
        pieces.append(flip(after(kept_one, (kept_two, row_tokens)), 4))
        pieces.append(flip(after(got_two, row_tokens), 2))
    cot_kept, cot_got = to_rows(after(cotangent, pieces[3]), "split_cotangent")
    fresh = 2
    middle = pieces[2:-fresh]
    parts += call(
        functools.partial(project_more, len(middle)), "project_more", projected * len(middle),
        (*middle, weight_mine, bias_mine, scale), flops=block * len(middle) * width * 3 * mine,
    )
    row_cot, grad_active = call(
        active_cotangent, "active_cotangent", (shape(block, width), shape(block, ff, kind=F32)),
        (cot_kept, cot_got, down_weight), mib=16,
    )

    outward_pad = outward_weight
    if slots != real:
        outward_pad = jnp.pad(outward_weight, ((0, slots - real), (0, 0)))

    forward = call(
        functools.partial(attention_forward, heads, chips, block, places, fresh), "attention_forward",
        [shape(length, 3 * mine), shape(length, mine, kind=F32), shape(length, 8, kind=F32)]
        + [shape(block, mine)] * chips + projected * fresh,
        (*parts[2::3], *pieces[-fresh:], weight_mine, bias_mine, scale, starts),
        flops=8 * length * length * mine, mib=8 + length // 128,
    )
    qkv, attended, logs = forward[:3]
    parts += forward[3 + chips :]
    attended_in = exchange(forward[3 : 3 + chips])
    row_cot, grad_active = call(
        active_cotangent, "active_cotangent", (shape(block, width), shape(block, ff, kind=F32)),
        (after(cot_kept, forward[3]), cot_got, down_weight), flops=2 * block * width * ff,
    )

    whole = call(
        functools.partial(whole_rows, chips, block, places), "whole_rows",
        [shape(length, width), shape(length, width, kind=F32)],
        (after(pieces[0], grad_active), *pieces[1:], *parts[0::3], *parts[1::3]), mib=8 + length // 128 + 2,
    )

    cot_other = flip(row_cot, 1)
    residual, normed_two, active, grad_up, kept, sent = call(
        functools.partial(up_branch, heads, chips, real), "up_branch",
        (
            shape(block, width, kind=F32), shape(block, width), shape(block, ff), shape(block, ff),
            shape(block, ff + real // 2), shape(block, ff + real // 2 + width),
        ),
        (
            *attended_in[::-1], after(row_tokens, whole[0]), grad_active, outward_pad, outward_bias, second_gain,
            up_weight, up_bias,
        ),
        scratch=[] if slots == real else [pltpu.VMEM((block, real), BF16)],
        flops=2 * block * width * ff, mib=23,
    )
    other = flip(sent, 1)
    back = call(
        functools.partial(back_branch, heads, chips, real), "back_branch",
        (shape(block, mine),) * chips
        + (shape(block, width, kind=F32), shape(block, width), shape(1, width, kind=F32)),
        (residual, row_cot, grad_up, up_weight, outward_pad, second_gain),
        flops=2 * block * width * ff, mib=16,
    )
    grad_res, grad_low, gain_grad = back[chips:]
    low_other = flip(grad_low, 1)
    grad_in = exchange(back[:chips])

    share, out_share, in_share = ff // (seq * dp), real // (seq * dp), 3 * real // (seq * dp)
    a_cut, b_cut = share - share // 4, share - share // 4
    third = 2 * share - a_cut - b_cut + out_share
    x_bit, y_bit = 0, len(chip_bits) - 1

    def stream(name, bit, cut, columns, args):
        dims = (chips // 2, dp, cut, width)
        return call(
            functools.partial(stream_sums, chips, dp, bit, cut, columns), name,
            [shape(*dims), shape(*dims, kind=F32), shape(chips, dp, share - cut, width, kind=F32)], args,
            mib=18,
        )

    a_sent, a_kept, down_rest = stream(
        "down_sums", x_bit, a_cut, (0, ff // seq, 0), (kept, other, row_cot, cot_other)
    )
    b_sent, b_kept, up_rest = stream(
        "up_sums", y_bit, b_cut, (ff // 2, ff // seq, ff + real // 2), (after(kept, a_sent), other, normed_two, other)
    )
    c_dims = (chips, dp // 2, third, width)
    c_sent, c_kept = call(
        functools.partial(third_sums, chips, dp, out_share, slots == real, (ff, real // seq, 0)), "out_sums",
        [shape(*c_dims), shape(*c_dims, kind=F32)],
        (after(kept, (b_sent, *grad_in[1:-1])), other, grad_low, low_other, down_rest, up_rest),
        scratch=[pltpu.VMEM((dp, out_share, width), F32)], mib=18,
    )
    a_got, b_got, c_got = flip(a_sent, 2 << x_bit), flip(b_sent, 2 << y_bit), flip(c_sent, 1, "dp")

    grad_in[0] = after(grad_in[0], c_sent)
    *grad_qkv, grad_all = call(
        functools.partial(attention_backward, heads, chips, block), "attention_backward",
        [shape(block, 3 * mine)] * chips + [shape(length, 3 * mine)],
        (starts, qkv, attended, logs, *grad_in),
        scratch=[
            pltpu.VMEM((length, mine), BF16), pltpu.VMEM((HEAD_DIM, length), F32),
            pltpu.VMEM((HEAD_DIM, length), F32),
        ],
        flops=200 * length * length * mine, mib=8 + length // 128,
    )
    plan = inward_units(chips, dp, real, mine)
    small_rows = 6 + ff // real
    packed_shape = shape(small_rows, real, kind=F32)
    row_outs = [packed_shape]
    if plan is not None:
        row_outs += [shape(2 * small_rows + dp * in_share, real), shape(dp, in_share, width, kind=F32)]
    packed, *inward = call(
        functools.partial(row_sums, heads, chips, block, real, plan and plan[1]), "row_sums", row_outs,
        (grad_all, weight_mine, gain_grad, grad_low, row_cot, grad_up, *whole),
        scratch=[
            pltpu.VMEM((3 * mine, width), F32),
        ],
        flops=12 * length * mine * width, mib=8 + length // 128 + 2,
    )

    def hop(value, step):
        return flip(value, 1 << step[1], step[0])

    chip_steps = [("seq", 1 + at) for at in range(len(chip_bits))]
    dp_steps = [("dp", at) for at in range(len(dp_bits))]
    rounds = list(zip(
        [step for step in chip_steps if step[1] != 1 + x_bit] + dp_steps[:1],
        dp_steps[:1] + [step for step in chip_steps if step[1] != 1 + y_bit],
        chip_steps,
    ))
    kepts, gots = [a_kept, b_kept, c_kept], [a_got, b_got, c_got]
    earlier = packed
    if plan is not None:
        in_sent, in_kept = inward
        in_got, small = flip(in_sent, 1), packed

    def half_dims(at):
        dims = [list(kept.shape) for kept in kepts]
        for dim, step in zip(dims, rounds[at]):
            dim[step[0] == "dp"] //= 2
        return dims

    sums_shapes = [shape(width, kind=F32), shape(2, real, kind=F32), shape(width, kind=F32)]
    sums_shapes += [shape(width, kind=F32), shape(ff, kind=F32), shape(width, kind=F32)]
    def finish_outputs(earlier):
        out_kept, out_sent = call(
            finish_output, "finish_output", half_rows, (residual, after(active, earlier), down_weight, down_bias),
        )
        return from_rows(out_kept, out_sent, "join_output")

    if plan is not None:
        half = (in_kept.shape[0] // 2,) + in_kept.shape[1:]
        in_sent, in_kept, small = call(
            functools.partial(fold_inward, dp_steps[1]), "fold_inward",
            [shape(2 * small_rows + half[0] * in_share, real), shape(*half, kind=F32), packed_shape],
            (in_kept, in_got, small),
        )
        in_got = hop(in_sent, dp_steps[1])
        near = [grad_qkv[0], flip(grad_qkv[1], 2), flip(grad_qkv[2], 4)]
        dims = half_dims(0)
        outs = call(
            functools.partial(fold, rounds[0]), "round_0",
            [shape(*dim) for dim in dims] + [shape(*dim, kind=F32) for dim in dims],
            (after(kepts[0], in_sent), *kepts[1:], *gots),
        )
        gots = [hop(sent, step) for sent, step in zip(outs[:3], rounds[0])]
        kepts = outs[3:]
        placed = call(
            functools.partial(place_pieces, heads, chips, real), "place_pieces", shape(block, 3 * real),
            (after(near[0], outs[0]), *near[1:]), flops=20 * 10**9,
        )
        output_tokens = finish_outputs(placed)
        half = (half[0] // 2,) + half[1:]
        in_sent, in_kept, small = call(
            functools.partial(fold_inward, dp_steps[0]), "fold_inward",
            [shape(2 * small_rows + half[0] * in_share, real), shape(*half, kind=F32), packed_shape],
            (after(in_kept, output_tokens), in_got, small),
        )
        dims = half_dims(1)
        counts = [math.prod(dim[:3]) for dim in dims]
        outs = call(
            functools.partial(second_step, rounds[1]), "round_1",
            [shape(counts[0] + in_sent.shape[0], real)] + [shape(*dim) for dim in dims[1:]]
            + [shape(*dim, kind=F32) for dim in dims],
            (*kepts, *gots, in_sent),
        )
        gots = [hop(sent, step) for sent, step in zip(outs[:3], rounds[1])]
        kepts = outs[3:]
        earlier = outs[0]
        across = flip(after(grad_qkv[3], (gots[1], gots[2])), 6)
    else:
        for at in range(len(rounds)):
            dims = half_dims(at)
            outs = call(
                functools.partial(fold, rounds[at]), f"round_{at}",
                [shape(*dim) for dim in dims] + [shape(*dim, kind=F32) for dim in dims], (*kepts, *gots),
            )
            kepts, gots = outs[3:], [hop(sent, step) for sent, step in zip(outs[:3], rounds[at])]
        placed = call(
            functools.partial(place_pieces, heads, chips, real), "place_pieces", shape(block, 3 * real),
            tuple(exchange(grad_qkv)),
        )
        output_tokens = finish_outputs(placed)
    if plan is not None:
        share_sum, low, small, far = call(
            functools.partial(last_inward, counts[0]), "last_inward",
            [
                shape(in_share, width, kind=F32), shape(2 * small_rows + in_share, real), packed_shape,
                shape(2 * small_rows, real),
            ],
            (after(in_kept, earlier), gots[0], small),
        )
        earlier = low
    dims = (1, kepts[0].shape[1] // 2, a_cut + b_cut + third, width)
    sent, kept = call(
        functools.partial(join_streams, dp_steps[1]), "join_streams", [shape(*dims), shape(*dims, kind=F32)],
        (after(kepts[0], earlier), *kepts[1:], *gots),
    )
    got = hop(sent, dp_steps[1])
    earlier = sent
    for step in dp_steps[2:]:
        dims = (1, kept.shape[1] // 2) + kept.shape[2:]
        sent, kept = call(
            functools.partial(fold, (step,)), "fold_joined", [shape(*dims), shape(*dims, kind=F32)], (kept, got)
        )
        got = hop(sent, step)
    if plan is not None:
        low = after(low, sent)
        far = flip(after(far, sent), 6)
        in_pieces = [share_sum, small, flip(low, 2), flip(low, 4), far]

    rows_kept, rows_sent = call(
        functools.partial(finish_tokens if plan is not None else finish_near, heads, chips, real), "finish_tokens",
        list(half_rows),
        (placed, *([across] if plan is not None else []), after(row_tokens, earlier), first_gain, grad_res, inward_weight),
        scratch=[pltpu.VMEM((block, 3 * real), BF16)],
        mib=16,
    )
    if plan is not None:
        size, unused, table = plan
        in_out, *sums_out = call(
            functools.partial(place_inward, dp, size, real), "place_inward",
            [shape(in_share, width, kind=F32)] + sums_shapes, (jnp.asarray(table), in_pieces[0], *in_pieces[1:]),
            scratch=[pltpu.VMEM((3, in_share // size, size, width), F32)],
            specs=[SMEM] + [VMEM] * (chips + 1),
        )
    else:
        in_out = lax.psum_scatter(dot(placed, normed_one, 0, 0), ("seq", "dp"), scatter_dimension=0, tiled=True)
        for step in [("seq", 0)] + chip_steps + dp_steps:
            packed = packed + hop(packed, step)
        sums_out = call(functools.partial(last_small, real), "last_small", sums_shapes, (packed,))
    grad_tokens = from_rows(after(rows_kept, in_out), rows_sent, "join_tokens", 2)
    down_share, up_share, out_out = call(
        functools.partial(last_wide, a_cut, b_cut), "last_wide",
        [shape(share, width, kind=F32), shape(share, width, kind=F32), shape(out_share, width, kind=F32)],
        (after(kept, grad_tokens), got),
    )

    gain_first, bias_in, bias_out, gain_second, bias_up, bias_down = sums_out
    return (
        output_tokens, grad_tokens, gain_first, in_out.T, bias_in, out_out, bias_out, gain_second,
        up_share.T, bias_up, down_share, bias_down,
    )


def solution(mesh):
    return jax.shard_map(
        local,
        mesh=mesh,
        in_specs=(P("dp", "seq", None), P("dp", None)) + (P(),) * 10 + (P("dp", "seq", None),),
        out_specs=(
            P("dp", "seq", None),
            P("dp", "seq", None),
            P(),
            P(None, ("seq", "dp")),
            P(),
            P(("seq", "dp"), None),
            P(),
            P(),
            P(None, ("seq", "dp")),
            P(),
            P(("seq", "dp"), None),
            P(),
        ),
        check_vma=False,
    )
```

```python
import functools
import math

import jax
import jax.numpy as jnp
import numpy as np
from jax import lax
from jax.experimental import pallas as pl
from jax.experimental.pallas import tpu as pltpu
from jax.sharding import PartitionSpec as P

HEADS = 12
HEAD_DIM = 64
EPSILON = 1e-05
FLOOR = -1e30
SCALE = HEAD_DIM**-0.5
QB = 256
F32 = jnp.float32
BF16 = jnp.bfloat16
VMEM = pl.BlockSpec(memory_space=pltpu.VMEM)
SMEM = pl.BlockSpec(memory_space=pltpu.SMEM)
hold = lax.optimization_barrier

def inverse_rms(values):
    squares = jnp.sum(values * values, axis=-1, keepdims=True)
    totals = jnp.sum(values, axis=-1, keepdims=True)
    return lax.rsqrt((squares + totals * totals) / (values.shape[-1] + 1) + EPSILON), totals


def norm_back(values, gain, inverse, totals, incoming):
    weighted = incoming * gain
    dots = jnp.sum(weighted * values, axis=-1, keepdims=True)
    factor = inverse * inverse * inverse * dots / (values.shape[-1] + 1)
    grad = inverse * weighted - factor * (values + totals)
    return grad, jnp.sum(incoming * values * inverse, axis=0, keepdims=True)


def dot(left, right, left_dim, right_dim):
    return lax.dot_general(
        left, right, (((left_dim,), (right_dim,)), ((), ())), preferred_element_type=F32
    )


def gelu_both(value):
    linear = 0.7978845608028654 * value
    cubic = linear * (0.044715 * (value * value))
    curve = jnp.tanh(linear + cubic)
    half = 0.5 + 0.5 * curve
    slope = half * (1.0 + (linear + 3.0 * cubic) * (1.0 - curve))
    return value * half, slope


def at_block(index, block):
    return pl.ds(pl.multiple_of(index * block, block), block)


def position():
    me = lax.axis_index("seq")
    return me >> 1, me & 1


def either(flag, first, second, left, right):
    @pl.when(flag == 0)
    def straight():
        first[...] = left
        second[...] = right

    @pl.when(flag != 0)
    def crossed():
        first[...] = right
        second[...] = left


def for_each_chip(chip, chips, body):
    for candidate in range(chips):
        pl.when(chip == candidate)(functools.partial(body, candidate))


def allowed_block(starts, query_start, keys):
    query_pos = query_start + lax.broadcasted_iota(jnp.int32, (QB, 1), 0)
    key_pos = lax.broadcasted_iota(jnp.int32, (1, keys), 1)
    return (key_pos <= query_pos) & (key_pos >= starts)


def split_rows(value, kept, sent):
    unused, core = position()
    length = value.shape[2]
    turned = value[...].reshape(value.shape[0], 2 * length).T
    either(core, kept, sent, turned[:length], turned[length:])


def join_rows(kept, *refs):
    gots, out = refs[:-1], refs[-1]
    unused, core = position()
    mine, other = [kept[...]], [got[...] for got in gots]

    def store(parts):
        out[...] = jnp.concatenate(parts, axis=0).T.reshape(out.shape)

    pl.when(core == 0)(lambda: store(mine + other))
    pl.when(core != 0)(lambda: store(other + mine))


def project(piece, scale, weight, bias, normed, inverse, qkv):
    values = piece[...].astype(F32)
    factor, unused = inverse_rms(values)
    low = (values * scale[...] * factor).astype(BF16)
    normed[...] = low
    inverse[...] = factor
    qkv[...] = (dot(low, weight[...], 1, 0) + bias[...]).astype(BF16)


def pick_weights(heads, chips, real, weight, weight_mine):
    width = heads * HEAD_DIM
    chip, unused = position()

    def choose(candidate):
        size = max(min(width, real - candidate * width), 0)
        for part in range(3):
            at, start = part * width, part * real + candidate * width
            if size > 0:
                weight_mine[:, at : at + size] = weight[:, start : start + size]
            if size < width:
                weight_mine[:, at + size : at + width] = jnp.zeros((weight.shape[0], width - size), BF16)

    for_each_chip(chip, chips, choose)


def project_first(heads, chips, real, docs, kept, got, gain, bias, weight, *refs):
    bias_mine, scale, starts, normed_own, own = refs[:5]
    width = heads * HEAD_DIM
    chip, core = position()

    def choose(candidate):
        size = max(min(width, real - candidate * width), 0)
        for part in (0, 2):
            if size > 0:
                bias_mine[:, part * width : part * width + size] = bias[
                    part // 2 : part // 2 + 1, candidate * width : candidate * width + size
                ].astype(F32)

    bias_mine[...] = jnp.zeros(bias_mine.shape, F32)
    for_each_chip(chip, chips, choose)
    scale[...] = gain[...].astype(F32).reshape(1, -1)
    places = lax.broadcasted_iota(jnp.int32, starts.shape, 0)
    start, end = jnp.zeros_like(places), jnp.int32(0)
    for at in range(3):
        end = end + docs[core, at]
        start = jnp.where(places >= end, end, start)
    starts[...] = start
    rows = kept.shape[0]
    for at, (piece, half) in enumerate(((kept, core), (got, 1 - core))):
        normed, inverse, qkv = refs[5 + 3 * at : 8 + 3 * at]
        project(piece, scale, weight, bias_mine, normed, inverse, qkv)
        normed_own[at_block(half, rows), :] = normed[...]
        own[at_block(half, rows), :] = piece[...]


def project_more(count, *refs):
    pieces, (weight, bias, scale), outs = refs[:count], refs[count : count + 3], refs[count + 3 :]
    for at, piece in enumerate(pieces):
        project(piece, scale, weight, bias, *outs[3 * at : 3 * at + 3])


def attention_forward(heads, chips, block, places, fresh, *refs):
    count = len(places)
    done, pieces = refs[: count - fresh], refs[count - fresh : count]
    (weight, bias, scale, starts), outs = refs[count : count + 4], refs[count + 4 :]
    qkv, attended, logs = outs[:3]
    sends, parts = outs[3 : 3 + chips], outs[3 + chips :]
    width = heads * HEAD_DIM
    chip, core = position()
    for at, (source, mine) in enumerate(places):
        part = done[at] if at < count - fresh else parts[3 * (at - count + fresh) + 2]
        if at >= count - fresh:
            at_parts = 3 * (at - count + fresh)
            project(pieces[at - count + fresh], scale, weight, bias, *parts[at_parts : at_parts + 3])
        rows = part.shape[0]
        half = core if mine else 1 - core
        start = pl.multiple_of((chip ^ source) * block + half * rows, rows)
        qkv[pl.ds(start, rows), :] = part[...]
    for at_query in range(chips * block // QB):
        rows = pl.ds(at_query * QB, QB)
        keys = (at_query + 1) * QB
        allowed = allowed_block(starts[rows, :], at_query * QB, keys)
        for head in range(heads):
            at = head * HEAD_DIM
            query = qkv[rows, at : at + HEAD_DIM] * BF16(SCALE)
            key = qkv[:keys, width + at : width + at + HEAD_DIM]
            value = qkv[:keys, 2 * width + at : 2 * width + at + HEAD_DIM]
            scores = jnp.where(allowed, dot(query, key, 1, 1), FLOOR)
            top = jnp.max(scores, axis=-1, keepdims=True)
            weights = jnp.exp(scores - top)
            total = jnp.sum(weights, axis=-1, keepdims=True)
            attended[rows, at : at + HEAD_DIM] = dot(weights.astype(BF16), value, 1, 0) / total
            logs[rows, head : head + 1] = top + jnp.log(total)
    for source in range(chips):
        sends[source][...] = attended[at_block(chip ^ source, block), :].astype(BF16)


def attention_backward(heads, chips, block, starts, qkv, attended, logs, *refs):
    grads, sends = refs[:chips], refs[chips : 2 * chips]
    out, grad_row, key_grad, value_grad = refs[2 * chips :]
    width = heads * HEAD_DIM
    chip, core = position()
    for source in range(chips):
        grad_row[at_block(chip ^ source, block), :] = grads[source][...]
    blocks = chips * block // QB
    for head in range(heads):
        at = head * HEAD_DIM
        turned_query = (qkv[:, at : at + HEAD_DIM] * BF16(SCALE)).T
        turned_grad = grad_row[:, at : at + HEAD_DIM].T
        for at_query in reversed(range(blocks)):
            lanes = slice(at_query * QB, (at_query + 1) * QB)
            rows = pl.ds(at_query * QB, QB)
            keys = (at_query + 1) * QB
            allowed = allowed_block(starts[rows, :], at_query * QB, keys)
            query = qkv[rows, at : at + HEAD_DIM] * BF16(SCALE)
            key = qkv[:keys, width + at : width + at + HEAD_DIM]
            value = qkv[:keys, 2 * width + at : 2 * width + at + HEAD_DIM]
            grad = grad_row[rows, at : at + HEAD_DIM]
            delta = jnp.sum(
                grad.astype(F32) * attended[rows, at : at + HEAD_DIM], axis=-1, keepdims=True
            )
            scores = dot(query, key, 1, 1)
            weights = jnp.where(allowed, jnp.exp(scores - logs[rows, head : head + 1]), 0.0)
            grad_weights = dot(grad, value, 1, 1)
            grad_scores = (weights * (grad_weights - delta)).astype(BF16)
            out[rows, at : at + HEAD_DIM] = (dot(grad_scores, key, 1, 0) * SCALE).astype(BF16)
            key_part = dot(turned_query[:, lanes], grad_scores, 1, 0)
            value_part = dot(turned_grad[:, lanes], weights.astype(BF16), 1, 0)
            if at_query == blocks - 1:
                key_grad[...] = key_part
                value_grad[...] = value_part
            else:
                key_grad[:, :keys] += key_part
                value_grad[:, :keys] += value_part
        out[:, width + at : width + at + HEAD_DIM] = key_grad[...].astype(BF16).T
        out[:, 2 * width + at : 2 * width + at + HEAD_DIM] = value_grad[...].astype(BF16).T
    for source in range(chips):
        sends[source][...] = out[at_block(chip ^ source, block), :]


def active_cotangent(kept, got, weight, row, out):
    unused, core = position()
    length = kept.shape[0]
    row[at_block(core, length), :] = kept[...]
    row[at_block(1 - core, length), :] = got[...]
    out[...] = dot(row[...], weight[...], 1, 1)


def up_branch(heads, chips, real, *refs):
    pieces = refs[:chips][::-1]
    tokens, grad_active, out_weight, out_bias, gain, up_weight, up_bias = refs[chips : chips + 7]
    residual, normed, active, grad_up, kept, sent, factors = refs[chips + 7 : chips + 14]
    held = refs[chips + 14 :]
    chip, core = position()
    mine = heads * HEAD_DIM
    ff = up_weight.shape[1]

    values = tokens[...].astype(F32) + out_bias[...].astype(F32).reshape(1, -1)
    for source, piece in enumerate(pieces):
        values = values + dot(piece[...], out_weight[at_block(chip ^ source, mine), :], 1, 0)
    residual[...] = values
    inverse, totals = inverse_rms(values)
    factors[0] = inverse
    factors[1] = totals
    low = (values * gain[...].astype(F32).reshape(1, -1) * inverse).astype(BF16)
    normed[...] = low
    sent[:, ff + real // 2 :] = low

    def share(start, size, at, left, right):
        place = slice(start + at * size, start + (at + 1) * size)
        kept[:, place] = jnp.where(core == 0, left, right)
        sent[:, place] = jnp.where(core == 0, right, left)

    if not held:
        for source, piece in enumerate(pieces):
            share(ff, mine // 2, source, piece[:, : mine // 2], piece[:, mine // 2 :])
    else:

        def place(candidate):
            for source, piece in enumerate(pieces):
                start = (candidate ^ source) * mine
                size = min(mine, real - start)
                if size > 0:
                    held[0][:, start : start + size] = piece[:, :size]

        for_each_chip(chip, chips, place)
        piece = real // (2 * chips)
        for at in range(chips):
            start = 2 * at * piece
            share(ff, piece, at, held[0][:, start : start + piece], held[0][:, start + piece : start + 2 * piece])
    tile = ff // chips
    piece = tile // 2
    for at in range(chips):
        cols = slice(at * tile, (at + 1) * tile)
        upward = dot(normed[...], up_weight[:, cols], 1, 0) + up_bias[cols].astype(F32).reshape(1, -1)
        act, slope = gelu_both(upward)
        low = act.astype(BF16)
        active[:, cols] = low
        share(0, piece, at, low[:, :piece], low[:, piece:])
        back = (grad_active[:, cols] * slope).astype(BF16)
        grad_up[:, cols] = back
        share(ff // 2, piece, at, back[:, :piece], back[:, piece:])


def back_branch(heads, chips, real, residual, factors, cotangent, grad_up, up_weight, out_weight, gain, *refs):
    sends = refs[:chips]
    grad_res, grad_low, gain_grad = refs[chips:]
    chip, unused = position()
    mine = heads * HEAD_DIM
    values = residual[...]
    inverse, totals = factors[0], factors[1]
    incoming = dot(grad_up[...], up_weight[...], 1, 1)
    grad, gain_sum = norm_back(values, gain[...].astype(F32).reshape(1, -1), inverse, totals, incoming)
    cot = cotangent[...].astype(F32)
    grad = grad + cot
    grad_res[...] = grad
    low = grad.astype(BF16)
    grad_low[...] = low
    gain_grad[...] = gain_sum
    for source in range(chips):
        sends[source][...] = dot(low, out_weight[at_block(chip ^ source, mine), :], 1, 1).astype(BF16)


def finish_output(residual, active, weight, bias, kept, sent):
    unused, core = position()
    values = residual[...] + dot(active[...], weight[...], 1, 0) + bias[...].astype(F32).reshape(1, -1)
    low = values.astype(BF16)
    length = kept.shape[0]
    either(core, kept, sent, low[:length], low[length:])


def row_pieces(chips, block, places, pieces, out):
    chip, core = position()
    for (source, mine), piece in zip(places, pieces):
        rows = piece.shape[0]
        half = core if mine else 1 - core
        out[pl.ds(pl.multiple_of((chip ^ source) * block + half * rows, rows), rows), :] = piece[...]


def whole_rows(chips, block, places, *refs):
    count = len(places)
    tokens, normed, inverse = refs[:count], refs[count : 2 * count], refs[2 * count : 3 * count]
    row_normed, row_scaled = refs[3 * count :]
    row_pieces(chips, block, places, normed, row_normed)
    chip, core = position()
    for (source, mine), piece, factor in zip(places, tokens, inverse):
        rows = piece.shape[0]
        half = core if mine else 1 - core
        start = pl.multiple_of((chip ^ source) * block + half * rows, rows)
        row_scaled[pl.ds(start, rows), :] = piece[...].astype(F32) * factor[...]


def row_sums(heads, chips, block, real, units, grad_qkv, weight_mine, gain_grad, low, cotangent, grad_up, *refs):
    (row_normed, row_scaled), outs, partial = refs[:2], refs[2:-1], refs[-1]
    packed = outs[0]
    chip, core = position()
    mine = heads * HEAD_DIM
    if units is not None:
        partial[...] = dot(grad_qkv[...], row_normed[...], 0, 0)
        sent, kept = outs[1:]
        share = kept.shape[1]

        def split(candidate):
            for for_core, for_replica, at, start, size in units[candidate]:

                @pl.when(core == for_core)
                def keep():
                    kept[for_replica, at : at + size] = partial[start : start + size]

                @pl.when(core != for_core)
                def send():
                    place = for_replica * share + at
                    sent[place : place + size, : partial.shape[1]] = partial[start : start + size].astype(BF16)

        for_each_chip(chip, chips, split)
    width = row_scaled.shape[1]
    packed[...] = jnp.zeros(packed.shape, F32)
    gain_sum = jnp.zeros((1, width), F32)
    for at in range(chips):
        rows = pl.ds(at * block, block)
        incoming = dot(grad_qkv[rows, :], weight_mine[...], 1, 1)
        gain_sum += jnp.sum(
            incoming * row_scaled[rows, :], axis=0, keepdims=True
        )
    packed[0:1, :width] = gain_sum
    query_sum = jnp.sum(grad_qkv[:, :mine].astype(F32), axis=0, keepdims=True)
    value_sum = jnp.sum(grad_qkv[:, 2 * mine :].astype(F32), axis=0, keepdims=True)

    def place(candidate):
        size = min(mine, real - candidate * mine)
        if size > 0:
            packed[1:2, candidate * mine : candidate * mine + size] = query_sum[:, :size]
            packed[2:3, candidate * mine : candidate * mine + size] = value_sum[:, :size]

    for_each_chip(chip, chips, place)
    packed[3:4, :width] = jnp.sum(low[...].astype(F32), axis=0, keepdims=True)
    packed[4:5, :width] = gain_grad[...]
    packed[5:6, :width] = jnp.sum(cotangent[...].astype(F32), axis=0, keepdims=True)
    for at in range(grad_up.shape[1] // real):
        part = grad_up[:, at * real : (at + 1) * real].astype(F32)
        packed[6 + at : 7 + at, :real] = jnp.sum(part, axis=0, keepdims=True)
    if units is not None:
        put_small(packed, sent)


def put_small(packed, sent):
    rows, start = packed.shape[0], sent.shape[0] - 2 * packed.shape[0]
    high = packed[...].astype(BF16)
    sent[start : start + rows] = high
    sent[start + rows : start + 2 * rows] = (packed[...] - high.astype(F32)).astype(BF16)


def take_small(got, rows):
    start = got.shape[0] - 2 * rows
    return got[start : start + rows].astype(F32) + got[start + rows : start + 2 * rows].astype(F32)


def finish_tokens(heads, chips, real, *refs):
    placed, far, tokens, gain, grad_res, weight, kept, sent, projected = refs
    chip, core = position()
    mine = heads * HEAD_DIM
    projected[...] = placed[...]
    if far is not None:

        def place(candidate):
            for part in range(3):
                start = part * real + (candidate ^ (chips - 1)) * mine
                projected[:, start : start + mine] = far[:, part * mine : (part + 1) * mine]

        for_each_chip(chip, chips, place)
    values = tokens[...].astype(F32)
    inverse, totals = inverse_rms(values)
    incoming = dot(projected[...], weight[...], 1, 1)
    grad, unused = norm_back(values, gain[...].astype(F32).reshape(1, -1), inverse, totals, incoming)
    low = (grad + grad_res[...]).astype(BF16)
    length = kept.shape[0]
    either(core, kept, sent, low[:length], low[length:])


def finish_near(heads, chips, real, placed, *refs):
    finish_tokens(heads, chips, real, placed, None, *refs)


def shared(chips, bit, at):
    chip, unused = position()
    return ((chip >> bit) & 1) == ((at >> bit) & 1), (at >> (bit + 1) << bit) | (at & ((1 << bit) - 1))


def stream_sums(chips, dp, bit, cut, columns, left, left_other, right, right_other, sent, kept, rest):
    start, rows, right_start = columns
    share = rows // dp
    chip, unused = position()
    mine = (chip >> bit) & 1
    step = math.gcd(start, rows)

    def make(out, place, at, cols, kind):
        total = dot(left[:, cols], right[...], 0, 0) + dot(left_other[:, cols], right_other[:, right_start:], 0, 0)
        for part in range(dp):
            out[place, part] = total[part * share : part * share + cut].astype(kind)
            rest[at, part] = total[part * share + cut : (part + 1) * share]

    for out, stays, kind in ((sent, False, BF16), (kept, True, F32)):
        for place in range(chips // 2):
            side = mine if stays else 1 - mine
            low, high = place & ((1 << bit) - 1), place >> bit << (bit + 1)
            if step % 128 == 0:
                at = high | (side << bit) | low
                make(out, place, at, pl.ds(pl.multiple_of(start + at * rows, step), rows), kind)
                continue
            for value in range(2):
                at = high | (value << bit) | low
                cols = slice(start + at * rows, start + (at + 1) * rows)
                pl.when(side == value)(functools.partial(make, out, place, at, cols, kind))


def third_sums(chips, dp, share, mixed, columns, left, left_other, right, right_other, down_rest, up_rest, sent, kept, held):
    start, rows, unused = columns
    down_more = down_rest.shape[2]
    more = down_more + up_rest.shape[2]
    chip, unused = position()
    mine = lax.axis_index("dp") & 1
    total = dot(left[:, start : start + chips * rows], right[...], 0, 0) + dot(
        left_other[:, start : start + chips * rows], right_other[...], 0, 0
    )
    for source in range(chips):
        at = chip ^ source if mixed else source
        for part in range(dp):
            held[part] = total[source * rows + part * share : source * rows + (part + 1) * share]
        for place in range(dp // 2):
            for ref, part, kind in ((kept, 2 * place + mine, F32), (sent, 2 * place + 1 - mine, BF16)):
                ref[at, place, :down_more] = down_rest[at, part].astype(kind)
                ref[at, place, down_more:more] = up_rest[at, part].astype(kind)
                ref[at, place, more:] = held[part].astype(kind)


def fold(steps, *refs):
    count = len(steps)
    kepts, gots, sents, outs = (refs[at * count : (at + 1) * count] for at in range(4))
    for (axis, shift), kept, got, sent, out in zip(steps, kepts, gots, sents, outs):
        bit = (lax.axis_index(axis) >> shift) & 1
        for chip in range(out.shape[0]):
            for part in range(out.shape[1]):
                if axis == "seq":
                    mine, other = (2 * chip + bit, part), (2 * chip + 1 - bit, part)
                else:
                    mine, other = (chip, 2 * part + bit), (chip, 2 * part + 1 - bit)
                out[chip, part] = kept[mine] + got[mine].astype(F32)
                sent[chip, part] = (kept[other] + got[other].astype(F32)).astype(BF16)


def join_streams(step, *refs):
    kepts, gots, (sent, out) = refs[:3], refs[3:6], refs[6:]
    bit = (lax.axis_index(step[0]) >> step[1]) & 1
    start = 0
    for kept, got in zip(kepts, gots):
        size, width = kept.shape[2], kept.shape[3]
        rows = slice(start, start + size)
        start = rows.stop

        def total(part):
            if len(got.shape) == 4:
                return kept[0, part] + got[0, part].astype(F32)
            return kept[0, part] + got[pl.ds(pl.multiple_of(part * size, 8), size), :width].astype(F32)

        for part in range(out.shape[1]):
            out[0, part, rows] = total(2 * part + bit)
            sent[0, part, rows] = total(2 * part + 1 - bit).astype(BF16)


def fold_inward(step, kept, got, packed, sent, out, packed_out):
    bit = (lax.axis_index(step[0]) >> step[1]) & 1
    rows, share, width = packed.shape[0], kept.shape[1], kept.shape[2]
    packed_out[...] = packed[...] + take_small(got, rows)
    put_small(packed_out, sent)
    for at in range(out.shape[0]):
        left, right = (
            kept[part] + got[part * share : (part + 1) * share, :width].astype(F32)
            for part in (at, out.shape[0] + at)
        )
        start = at * share
        out[at] = jnp.where(bit == 0, left, right)
        sent[start : start + share, :width] = jnp.where(bit == 0, right, left).astype(BF16)


def place_pieces(heads, chips, real, *refs):
    pieces, projected = refs[:-1], refs[-1]
    chip, unused = position()
    mine = heads * HEAD_DIM

    def place(candidate):
        for source, piece in enumerate(pieces):
            start = (candidate ^ source) * mine
            size = min(mine, real - start)
            for part in range(3):
                if size > 0:
                    projected[:, part * real + start : part * real + start + size] = piece[
                        :, part * mine : part * mine + size
                    ]

    for_each_chip(chip, chips, place)


def second_step(steps, *refs):
    kepts, gots, in_sent = refs[:3], refs[3:6], refs[6]
    (message, *sents), outs = refs[7:10], refs[10:]
    fold(steps[1:], *kepts[1:], *gots[1:], *sents, *outs[1:])
    (axis, shift), kept, got, out = steps[0], kepts[0], gots[0], outs[0]
    bit = (lax.axis_index(axis) >> shift) & 1
    rows, start = kept.shape[2], 0
    for part in range(out.shape[1]):
        mine, other = (0, 2 * part + bit), (0, 2 * part + 1 - bit)
        out[0, part] = kept[mine] + got[mine].astype(F32)
        message[start : start + rows, : kept.shape[3]] = (kept[other] + got[other].astype(F32)).astype(BF16)
        start += rows
    message[start:] = in_sent[...]


def last_inward(start, kept, message, packed, share, low, packed_out, far):
    rows, count, width = packed.shape[0], share.shape[0], share.shape[1]
    got = message.at[start:]
    total = kept[0] + got[:count, :width].astype(F32)
    share[...] = total
    low[:count, :width] = total.astype(BF16)
    packed_out[...] = packed[...] + take_small(got, rows)
    put_small(packed_out, low)
    put_small(packed_out, far)


def last_wide(a_cut, b_cut, kept, got, down, up, outward):
    share = down.shape[0]

    def total(start, size):
        rows = slice(start, start + size)
        return kept[0, 0, rows] + got[0, 0, rows].astype(F32)

    down[:a_cut] = total(0, a_cut)
    up[:b_cut] = total(a_cut, b_cut)
    down[a_cut:] = total(a_cut + b_cut, share - a_cut)
    up[b_cut:] = total(b_cut + share, share - b_cut)
    outward[...] = total(2 * share, outward.shape[0])


def place_inward(dp, size, real, table, share, packed, *refs):
    gots, far, out, outs, held = refs[:2], refs[2], refs[3], refs[4:-1], refs[-1]
    count, small = share.shape[0] // size, packed.shape[0]
    width = share.shape[1]
    sums = packed[...] + take_small(far, small)
    for unit in range(count):
        held[0, unit] = share[unit * size : (unit + 1) * size]
        for at, piece in enumerate(gots):
            start = unit * size
            held[at + 1, unit] = piece[start : start + size, :width].astype(F32)
    for piece in gots:
        sums = sums + take_small(piece, small)
    put_sums(real, sums, *outs)
    device = lax.axis_index("seq") * dp + lax.axis_index("dp")
    for unit in range(count):
        place = 2 * (device * count + unit)
        out[unit * size : (unit + 1) * size] = held[table[place], table[place + 1]]


def put_sums(real, sums, gain_first, bias_in, bias_out, gain_second, bias_up, bias_down):
    width = gain_first.shape[0]
    gain_first[...] = sums[0:1, :width].reshape(width)
    bias_in[...] = sums[1:3, :real]
    bias_out[...] = sums[3:4, :width].reshape(width)
    gain_second[...] = sums[4:5, :width].reshape(width)
    bias_down[...] = sums[5:6, :width].reshape(width)
    for at in range(bias_up.shape[0] // real):
        bias_up[at * real : (at + 1) * real] = sums[6 + at : 7 + at, :real].reshape(real)


def last_small(real, packed, *outs):
    put_sums(real, packed[...], *outs)


def inward_units(chips, dp, real, mine):
    share = 3 * real // (2 * chips * dp)
    size = math.gcd(share, mine)
    count = share // size
    if chips != 4 or dp != 4 or chips * mine != real or size % 8:
        return None
    units, table = [], np.zeros((2 * chips * dp, count, 2), np.int32)
    for chip in range(chips):
        filled, own = {}, []
        for part in range(3):
            for at in range(mine // size):
                unit = (part * real + chip * mine) // size + at
                holder, place = unit // count, unit % count
                slot = ((holder // dp) & 1, holder % dp)
                here = filled.get(slot, 0)
                filled[slot] = here + 1
                own.append((*slot, here * size, part * mine + at * size, size))
                table[holder, place] = (holder // dp // 2) ^ chip, here
        if len(filled) != 2 * dp or set(filled.values()) != {count}:
            return None
        units.append(own)
    if table[:, :, 0].max() > 2:
        return None
    return size, units, table.reshape(-1)


def flip(value, mask, axis="seq"):
    return lax.ppermute(value, axis, [(at, at ^ mask) for at in range(lax.axis_size(axis))])


def bits_of(size):
    return [1 << at for at in range(size.bit_length() - 1)]


def local(
    tokens, doc_lengths, first_gain, inward_weight, inward_bias, outward_weight, outward_bias,
    second_gain, up_weight, up_bias, down_weight, down_bias, cotangent,
):
    rows, local_len, width = tokens.shape
    seq, dp = lax.axis_size("seq"), lax.axis_size("dp")
    chips = seq // 2
    block = rows * local_len
    length = seq * local_len
    real = HEADS * HEAD_DIM
    heads = -(-HEADS // chips)
    mine = heads * HEAD_DIM
    slots = chips * mine
    ff = up_weight.shape[1]
    chip_bits, dp_bits = bits_of(chips), bits_of(dp)

    def shape(*dims, kind=BF16):
        return jax.ShapeDtypeStruct(dims, kind)

    def call(kernel, name, outs, args, scratch=(), flops=1, mib=16, specs=None):
        return pl.pallas_call(
            kernel,
            out_shape=outs,
            in_specs=specs or [VMEM] * len(args),
            out_specs=jax.tree.map(lambda unused: VMEM, outs),
            scratch_shapes=scratch,
            compiler_params=pltpu.CompilerParams(vmem_limit_bytes=mib * 1024 * 1024),
            cost_estimate=pl.CostEstimate(flops=flops, bytes_accessed=1, transcendentals=0),
            name=name,
        )(*args)

    def after(value, earlier):
        return hold((value, earlier))[0]

    half_rows = (shape(local_len, width),) * 2

    def to_rows(value, name):
        kept, sent = call(split_rows, name, half_rows, (jnp.transpose(value, (2, 0, 1)),), mib=8)
        return kept, flip(sent, 1)

    def from_rows(kept, sent, name, parts=1):
        size = local_len // parts
        gots = [flip(sent[at * size : (at + 1) * size], 1) for at in range(parts)]
        out = call(join_rows, name, shape(width, rows, local_len), (kept, *gots), mib=8)
        return jnp.transpose(out, (1, 2, 0))

    def exchange(pieces):
        return [pieces[0]] + [flip(pieces[at], 2 * at) for at in range(1, chips)]

    kept, got = to_rows(tokens, "split_tokens")
    weight_mine = call(
        functools.partial(pick_weights, heads, chips, real), "pick_weights", shape(width, 3 * mine),
        (after(inward_weight, kept),),
    )
    places, pieces = [(0, 1), (0, 0)], [kept, got]
    if chips == 4:
        kept_one, kept_two = flip(kept, 2), flip(kept, 4)
        got_late = after(got, weight_mine)
        got_one, got_two = flip(got_late, 2), flip(got_late, 4)
        places += [(1, 1), (2, 1), (1, 0), (2, 0), (3, 1), (3, 0)]
        pieces += [kept_one, kept_two, got_one, got_two]
    else:
        for which, value in ((1, kept), (0, got)):
            held = value[None]
            for bit in chip_bits:
                held = jnp.concatenate([held, flip(held, 2 * bit)], axis=0)
            places += [(at, which) for at in range(1, chips)]
            pieces += [held[at] for at in range(1, chips)]
    projected = [shape(local_len, width), shape(local_len, 1, kind=F32), shape(local_len, 3 * mine)]
    bias_mine, scale, starts, normed_one, row_tokens, *parts = call(
        functools.partial(project_first, heads, chips, real), "project_first",
        [shape(1, 3 * mine, kind=F32), shape(1, width, kind=F32), shape(length, 1, kind=jnp.int32)]
        + [shape(block, width)] * 2 + projected * 2,
        (doc_lengths, kept, got, first_gain, inward_bias, weight_mine),
        flops=2 * block * width * 3 * mine, specs=[SMEM] + [VMEM] * 5,
    )
    if chips == 4:
        pieces.append(flip(after(kept_one, (kept_two, row_tokens)), 4))
        pieces.append(flip(after(got_two, row_tokens), 2))
    cot_kept, cot_got = to_rows(after(cotangent, pieces[3]), "split_cotangent")
    fresh = 2
    middle = pieces[2:-fresh]
    parts += call(
        functools.partial(project_more, len(middle)), "project_more", projected * len(middle),
        (*middle, weight_mine, bias_mine, scale), flops=block * len(middle) * width * 3 * mine,
    )
    row_cot, grad_active = call(
        active_cotangent, "active_cotangent", (shape(block, width), shape(block, ff, kind=F32)),
        (cot_kept, cot_got, down_weight), mib=16,
    )

    outward_pad = outward_weight
    if slots != real:
        outward_pad = jnp.pad(outward_weight, ((0, slots - real), (0, 0)))

    forward = call(
        functools.partial(attention_forward, heads, chips, block, places, fresh), "attention_forward",
        [shape(length, 3 * mine), shape(length, mine, kind=F32), shape(length, 8, kind=F32)]
        + [shape(block, mine)] * chips + projected * fresh,
        (*parts[2::3], *pieces[-fresh:], weight_mine, bias_mine, scale, starts),
        flops=8 * length * length * mine, mib=8 + length // 128,
    )
    qkv, attended, logs = forward[:3]
    parts += forward[3 + chips :]
    attended_in = exchange(forward[3 : 3 + chips])
    row_cot, grad_active = call(
        active_cotangent, "active_cotangent", (shape(block, width), shape(block, ff, kind=F32)),
        (after(cot_kept, forward[3]), cot_got, down_weight), flops=2 * block * width * ff,
    )

    whole = call(
        functools.partial(whole_rows, chips, block, places), "whole_rows",
        [shape(length, width), shape(length, width, kind=F32)],
        (after(pieces[0], grad_active), *pieces[1:], *parts[0::3], *parts[1::3]), mib=8 + length // 128 + 2,
    )

    cot_other = flip(row_cot, 1)
    residual, normed_two, active, grad_up, kept, sent, factors = call(
        functools.partial(up_branch, heads, chips, real), "up_branch",
        (
            shape(block, width, kind=F32), shape(block, width), shape(block, ff), shape(block, ff),
            shape(block, ff + real // 2), shape(block, ff + real // 2 + width),
            shape(2, block, 1, kind=F32),
        ),
        (
            *attended_in[::-1], after(row_tokens, whole[0]), grad_active, outward_pad, outward_bias, second_gain,
            up_weight, up_bias,
        ),
        scratch=[] if slots == real else [pltpu.VMEM((block, real), BF16)],
        flops=2 * block * width * ff, mib=23,
    )
    other = flip(sent, 1)
    back = call(
        functools.partial(back_branch, heads, chips, real), "back_branch",
        (shape(block, mine),) * chips
        + (shape(block, width, kind=F32), shape(block, width), shape(1, width, kind=F32)),
        (residual, factors, row_cot, grad_up, up_weight, outward_pad, second_gain),
        flops=2 * block * width * ff, mib=16,
    )
    grad_res, grad_low, gain_grad = back[chips:]
    low_other = flip(grad_low, 1)
    grad_in = exchange(back[:chips])

    share, out_share, in_share = ff // (seq * dp), real // (seq * dp), 3 * real // (seq * dp)
    a_cut, b_cut = share - share // 4, share - share // 4
    third = 2 * share - a_cut - b_cut + out_share
    x_bit, y_bit = 0, len(chip_bits) - 1

    def stream(name, bit, cut, columns, args):
        dims = (chips // 2, dp, cut, width)
        return call(
            functools.partial(stream_sums, chips, dp, bit, cut, columns), name,
            [shape(*dims), shape(*dims, kind=F32), shape(chips, dp, share - cut, width, kind=F32)], args,
            mib=18,
        )

    a_sent, a_kept, down_rest = stream(
        "down_sums", x_bit, a_cut, (0, ff // seq, 0), (kept, other, row_cot, cot_other)
    )
    b_sent, b_kept, up_rest = stream(
        "up_sums", y_bit, b_cut, (ff // 2, ff // seq, ff + real // 2), (after(kept, a_sent), other, normed_two, other)
    )
    c_dims = (chips, dp // 2, third, width)
    c_sent, c_kept = call(
        functools.partial(third_sums, chips, dp, out_share, slots == real, (ff, real // seq, 0)), "out_sums",
        [shape(*c_dims), shape(*c_dims, kind=F32)],
        (after(kept, (b_sent, *grad_in[1:-1])), other, grad_low, low_other, down_rest, up_rest),
        scratch=[pltpu.VMEM((dp, out_share, width), F32)], mib=18,
    )
    a_got, b_got, c_got = flip(a_sent, 2 << x_bit), flip(b_sent, 2 << y_bit), flip(c_sent, 1, "dp")

    grad_in[0] = after(grad_in[0], c_sent)
    *grad_qkv, grad_all = call(
        functools.partial(attention_backward, heads, chips, block), "attention_backward",
        [shape(block, 3 * mine)] * chips + [shape(length, 3 * mine)],
        (starts, qkv, attended, logs, *grad_in),
        scratch=[
            pltpu.VMEM((length, mine), BF16), pltpu.VMEM((HEAD_DIM, length), F32),
            pltpu.VMEM((HEAD_DIM, length), F32),
        ],
        flops=200 * length * length * mine, mib=8 + length // 128,
    )
    plan = inward_units(chips, dp, real, mine)
    small_rows = 6 + ff // real
    packed_shape = shape(small_rows, real, kind=F32)
    row_outs = [packed_shape]
    if plan is not None:
        row_outs += [shape(2 * small_rows + dp * in_share, real), shape(dp, in_share, width, kind=F32)]
    packed, *inward = call(
        functools.partial(row_sums, heads, chips, block, real, plan and plan[1]), "row_sums", row_outs,
        (grad_all, weight_mine, gain_grad, grad_low, row_cot, grad_up, *whole),
        scratch=[
            pltpu.VMEM((3 * mine, width), F32),
        ],
        flops=12 * length * mine * width, mib=8 + length // 128 + 2,
    )

    def hop(value, step):
        return flip(value, 1 << step[1], step[0])

    chip_steps = [("seq", 1 + at) for at in range(len(chip_bits))]
    dp_steps = [("dp", at) for at in range(len(dp_bits))]
    rounds = list(zip(
        [step for step in chip_steps if step[1] != 1 + x_bit] + dp_steps[:1],
        dp_steps[:1] + [step for step in chip_steps if step[1] != 1 + y_bit],
        chip_steps,
    ))
    kepts, gots = [a_kept, b_kept, c_kept], [a_got, b_got, c_got]
    earlier = packed
    if plan is not None:
        in_sent, in_kept = inward
        in_got, small = flip(in_sent, 1), packed

    def half_dims(at):
        dims = [list(kept.shape) for kept in kepts]
        for dim, step in zip(dims, rounds[at]):
            dim[step[0] == "dp"] //= 2
        return dims

    sums_shapes = [shape(width, kind=F32), shape(2, real, kind=F32), shape(width, kind=F32)]
    sums_shapes += [shape(width, kind=F32), shape(ff, kind=F32), shape(width, kind=F32)]
    def finish_outputs(earlier):
        out_kept, out_sent = call(
            finish_output, "finish_output", half_rows, (residual, after(active, earlier), down_weight, down_bias),
        )
        return from_rows(out_kept, out_sent, "join_output")

    if plan is not None:
        half = (in_kept.shape[0] // 2,) + in_kept.shape[1:]
        in_sent, in_kept, small = call(
            functools.partial(fold_inward, dp_steps[1]), "fold_inward",
            [shape(2 * small_rows + half[0] * in_share, real), shape(*half, kind=F32), packed_shape],
            (in_kept, in_got, small),
        )
        in_got = hop(in_sent, dp_steps[1])
        near = [grad_qkv[0], flip(grad_qkv[1], 2), flip(grad_qkv[2], 4)]
        dims = half_dims(0)
        outs = call(
            functools.partial(fold, rounds[0]), "round_0",
            [shape(*dim) for dim in dims] + [shape(*dim, kind=F32) for dim in dims],
            (after(kepts[0], in_sent), *kepts[1:], *gots),
        )
        gots = [hop(sent, step) for sent, step in zip(outs[:3], rounds[0])]
        kepts = outs[3:]
        placed = call(
            functools.partial(place_pieces, heads, chips, real), "place_pieces", shape(block, 3 * real),
            (after(near[0], outs[0]), *near[1:]), flops=20 * 10**9,
        )
        output_tokens = finish_outputs(placed)
        half = (half[0] // 2,) + half[1:]
        in_sent, in_kept, small = call(
            functools.partial(fold_inward, dp_steps[0]), "fold_inward",
            [shape(2 * small_rows + half[0] * in_share, real), shape(*half, kind=F32), packed_shape],
            (after(in_kept, output_tokens), in_got, small),
        )
        dims = half_dims(1)
        counts = [math.prod(dim[:3]) for dim in dims]
        outs = call(
            functools.partial(second_step, rounds[1]), "round_1",
            [shape(counts[0] + in_sent.shape[0], real)] + [shape(*dim) for dim in dims[1:]]
            + [shape(*dim, kind=F32) for dim in dims],
            (*kepts, *gots, in_sent),
        )
        gots = [hop(sent, step) for sent, step in zip(outs[:3], rounds[1])]
        kepts = outs[3:]
        earlier = outs[0]
        across = flip(after(grad_qkv[3], (gots[1], gots[2])), 6)
    else:
        for at in range(len(rounds)):
            dims = half_dims(at)
            outs = call(
                functools.partial(fold, rounds[at]), f"round_{at}",
                [shape(*dim) for dim in dims] + [shape(*dim, kind=F32) for dim in dims], (*kepts, *gots),
            )
            kepts, gots = outs[3:], [hop(sent, step) for sent, step in zip(outs[:3], rounds[at])]
        placed = call(
            functools.partial(place_pieces, heads, chips, real), "place_pieces", shape(block, 3 * real),
            tuple(exchange(grad_qkv)),
        )
        output_tokens = finish_outputs(placed)
    if plan is not None:
        share_sum, low, small, far = call(
            functools.partial(last_inward, counts[0]), "last_inward",
            [
                shape(in_share, width, kind=F32), shape(2 * small_rows + in_share, real), packed_shape,
                shape(2 * small_rows, real),
            ],
            (after(in_kept, earlier), gots[0], small),
        )
        earlier = low
    dims = (1, kepts[0].shape[1] // 2, a_cut + b_cut + third, width)
    sent, kept = call(
        functools.partial(join_streams, dp_steps[1]), "join_streams", [shape(*dims), shape(*dims, kind=F32)],
        (after(kepts[0], earlier), *kepts[1:], *gots),
    )
    got = hop(sent, dp_steps[1])
    earlier = sent
    for step in dp_steps[2:]:
        dims = (1, kept.shape[1] // 2) + kept.shape[2:]
        sent, kept = call(
            functools.partial(fold, (step,)), "fold_joined", [shape(*dims), shape(*dims, kind=F32)], (kept, got)
        )
        got = hop(sent, step)
    if plan is not None:
        low = after(low, sent)
        far = flip(after(far, sent), 6)
        in_pieces = [share_sum, small, flip(low, 2), flip(low, 4), far]

    rows_kept, rows_sent = call(
        functools.partial(finish_tokens if plan is not None else finish_near, heads, chips, real), "finish_tokens",
        list(half_rows),
        (placed, *([across] if plan is not None else []), after(row_tokens, earlier), first_gain, grad_res, inward_weight),
        scratch=[pltpu.VMEM((block, 3 * real), BF16)],
        mib=16,
    )
    if plan is not None:
        size, unused, table = plan
        in_out, *sums_out = call(
            functools.partial(place_inward, dp, size, real), "place_inward",
            [shape(in_share, width, kind=F32)] + sums_shapes, (jnp.asarray(table), in_pieces[0], *in_pieces[1:]),
            scratch=[pltpu.VMEM((3, in_share // size, size, width), F32)],
            specs=[SMEM] + [VMEM] * (chips + 1),
        )
    else:
        in_out = lax.psum_scatter(dot(placed, normed_one, 0, 0), ("seq", "dp"), scatter_dimension=0, tiled=True)
        for step in [("seq", 0)] + chip_steps + dp_steps:
            packed = packed + hop(packed, step)
        sums_out = call(functools.partial(last_small, real), "last_small", sums_shapes, (packed,))
    grad_tokens = from_rows(after(rows_kept, in_out), rows_sent, "join_tokens", 2)
    down_share, up_share, out_out = call(
        functools.partial(last_wide, a_cut, b_cut), "last_wide",
        [shape(share, width, kind=F32), shape(share, width, kind=F32), shape(out_share, width, kind=F32)],
        (after(kept, grad_tokens), got),
    )

    gain_first, bias_in, bias_out, gain_second, bias_up, bias_down = sums_out
    return (
        output_tokens, grad_tokens, gain_first, in_out.T, bias_in, out_out, bias_out, gain_second,
        up_share.T, bias_up, down_share, bias_down,
    )


def solution(mesh):
    return jax.shard_map(
        local,
        mesh=mesh,
        in_specs=(P("dp", "seq", None), P("dp", None)) + (P(),) * 10 + (P("dp", "seq", None),),
        out_specs=(
            P("dp", "seq", None),
            P("dp", "seq", None),
            P(),
            P(None, ("seq", "dp")),
            P(),
            P(("seq", "dp"), None),
            P(),
            P(),
            P(None, ("seq", "dp")),
            P(),
            P(("seq", "dp"), None),
            P(),
        ),
        check_vma=False,
    )
```
